128 devices in a mesh: outer: 16 (over y, z_lo, core), inner: 8 (over z_hi, x).
Axes of the slice: x: 4, y: 4, z: 4 (z_hi: 2, z_lo: 2; z = z_hi * 2 + z_lo), core: 2. Of those that a mesh axis runs over, the one named last changes fastest.
Arguments:
- queries: bfloat16 [16384, 768], P(('outer', 'inner')), may hold values from -5.5 to 5.5
- keys: bfloat16 [16384, 128], P(('outer', 'inner')), may hold values from -5.5 to 5.5
- values: bfloat16 [16384, 128], P(('outer', 'inner')), may hold values from -6 to 6
- grad_out: bfloat16 [16384, 768], P(('outer', 'inner')), may hold values from -96 to 96
- span_slot: int32 [256], replicated, may hold values from 0 to 255, as said below
Outputs:
- grad_queries: bfloat16 [16384, 768], P(('outer', 'inner'))
- grad_keys: bfloat16 [16384, 128], P(('outer', 'inner'))
- grad_values: bfloat16 [16384, 128], P(('outer', 'inner'))
The draws below stay inside these ranges and needn't reach their ends.
Inputs may be any that keep to these rules, and one draw needn't show every extreme that they name: `span_slot`: slots 2 d and 2 d + 1 hold spans c and 255 - c for some c below 128; every span is held once.
All inputs are finite; a program needn't handle non-finite values.
Results may differ from the reference program's by a relative error of at most 0.0074.
Values may be sent and summed in bfloat16 or wider, within the bound.
No kernel may reach another device: no remote copies, remote signals or barrier semaphores. Data moves between devices by JAX's collectives and lax.ppermute only.
A program may use at most 128 MiB of HBM per device.

```python
import math
import jax
import jax.numpy as jnp
from jax import lax

HD = 128
GROUP = 6
TOKENS = 16384
SPANS = 256


def draw_queries(key, part):
    key = jax.random.fold_in(key, 3)
    base = jnp.clip(jax.random.normal(key, (TOKENS, GROUP * HD), jnp.float32), -4.5, 4.5)
    return base.astype(jnp.bfloat16)


def draw_keys(key, part):
    key = jax.random.fold_in(key, 5)
    base = jnp.clip(jax.random.normal(key, (TOKENS, HD), jnp.float32), -4.5, 4.5)
    return base.astype(jnp.bfloat16)


def draw_span_slot(key, part):
    key = jax.random.fold_in(key, 7)
    half = SPANS // 2
    order = jax.random.permutation(key, half).astype(jnp.int32)
    paired = jnp.stack([order, SPANS - 1 - order], axis=1)
    return paired.reshape(-1).astype(jnp.int32)


def levels(rng, shape, pieces, smallest, largest):
    level, own = 1.0, jax.random.fold_in(rng, 6)
    for dim, shards_of in pieces:
        heights = jnp.exp(jax.random.uniform(jax.random.fold_in(own, dim), (shards_of,), jnp.float32, smallest / len(pieces), largest / len(pieces)))
        level = level * jnp.repeat(heights, shape[dim] // shards_of).reshape([-1 if axis == dim else 1 for axis in range(len(shape))])
    return level


def normal_values(stream_key, dims, spread, bound, pieces=(), kind=jnp.bfloat16):
    entries = jax.random.normal(stream_key, dims, jnp.float32) * spread
    if len(pieces) > 0:
        entries = levels(stream_key, dims, pieces, -0.22, 0.18) * entries
    return jnp.clip(entries, min=-bound, max=bound).astype(kind)


def setup_inputs(seed: int = 0) -> dict:
    arg_keys = jax.random.split(jax.random.key(seed), 6)
    queries = draw_queries(jax.random.fold_in(arg_keys[5], 71), 0)
    keys = draw_keys(jax.random.fold_in(arg_keys[5], 71), 0)
    values = normal_values(arg_keys[2], (TOKENS, HD), 1.0, 6.0, ((0, 128),))
    grad_out = normal_values(arg_keys[3], (TOKENS, GROUP * HD), 16.0, 96.0, ((0, 128),))
    span_slot = draw_span_slot(jax.random.fold_in(arg_keys[5], 71), 0)
    return dict(queries=queries, keys=keys, values=values, grad_out=grad_out, span_slot=span_slot)


NEG_FILL = -1e+30

def reference(queries, keys, values, grad_out, span_slot):
    tokens = keys.shape[0]
    span_len = tokens // span_slot.shape[0]
    offsets = jnp.arange(span_len, dtype=jnp.int32)
    position = (span_slot[:, None].astype(jnp.int32) * span_len + offsets[None, :]).reshape(-1)
    scale = 1.0 / math.sqrt(HD)
    q_block = math.gcd(tokens, 128)
    blocks = tokens // q_block
    q_all = queries.reshape(blocks, q_block * GROUP, HD)
    do_all = grad_out.reshape(blocks, q_block * GROUP, HD)
    pos_all = jnp.repeat(position, GROUP).reshape(blocks, q_block * GROUP)

    def step(carry, item):
        dkey, dval = carry
        q_rows, do_rows, q_pos = item
        live = q_pos[:, None] >= position[None, :]
        scores = jnp.where(live, jnp.dot(q_rows, keys.T, preferred_element_type=jnp.float32) * scale, NEG_FILL)
        top = lax.optimization_barrier(jnp.max(scores, axis=1))
        lse = top + jnp.log(lax.optimization_barrier(jnp.sum(jnp.where(live, jnp.exp(scores - top[:, None]), 0.0), axis=1)))
        probs = jnp.where(live, jnp.exp(scores - lse[:, None]), 0.0)
        dprobs = jnp.dot(do_rows, values.T, preferred_element_type=jnp.float32)
        delta = lax.optimization_barrier(jnp.sum(probs * dprobs, axis=1))
        dscores = (probs * (dprobs - delta[:, None]) * scale).astype(jnp.bfloat16)
        dq_rows = jnp.dot(dscores, keys, preferred_element_type=jnp.float32).astype(jnp.bfloat16)
        dkey = dkey + jnp.dot(dscores.T, q_rows, preferred_element_type=jnp.float32)
        dval = dval + jnp.dot(probs.astype(jnp.bfloat16).T, do_rows, preferred_element_type=jnp.float32)
        return ((dkey, dval), dq_rows)
    start = (jnp.zeros((tokens, HD), jnp.float32), jnp.zeros((tokens, HD), jnp.float32))
    (dkey, dval), dq_all = lax.scan(step, start, (q_all, do_all, pos_all))
    grad_queries = dq_all.reshape(tokens, GROUP * HD)
    return (grad_queries, dkey.astype(jnp.bfloat16), dval.astype(jnp.bfloat16))
```

```python
import math

import jax
import jax.numpy as jnp
from jax import lax
from jax.experimental import pallas as pl
from jax.experimental.pallas import tpu as pltpu
from jax.sharding import Mesh, PartitionSpec as P

AXES = ("y", "zl", "core", "zh", "x")
NEG = -1e30
HD = 128
SCALE = 1.0 / math.sqrt(HD)
C2 = math.log2(math.e) * SCALE
SPAN = 64
HEADS = 6
ROWS = SPAN * HEADS
KB = 256
UNITS = 8
KEYS = 4096

NT = (((1,), (1,)), ((), ()))
NN = (((1,), (0,)), ((), ()))
TN = (((0,), (0,)), ((), ()))


def dot(a, b, dims):
    return lax.dot_general(a, b, dims, preferred_element_type=jnp.float32)


def load_sorted(meta, kvs, kv_s):
    for g, ref in enumerate(kvs):
        for s in range(32):
            r = pl.multiple_of(meta[g * 32 + s] * SPAN, SPAN)
            kv_s[pl.ds(r, SPAN), :] = ref[s // 2, (s % 2) * SPAN : (s % 2 + 1) * SPAN, :]


def load_rows(qds, q_s, do_s):
    for d, ref in enumerate(qds):
        for half in range(2):
            t = slice(half * SPAN, (half + 1) * SPAN)
            for h in range(HEADS):
                r = slice(h * SPAN, (h + 1) * SPAN)
                q_s[d * 2 + half, r, :] = ref[t, h * HD : (h + 1) * HD]
                do_s[d * 2 + half, r, :] = ref[t, (HEADS + h) * HD : (HEADS + h + 1) * HD]


def stats_kernel(meta, lim, qd0, qd1, qd2, qd3, kv0, kv1, out, q_s, do_s, kv_s):
    load_sorted(meta, (kv0, kv1), kv_s)
    load_rows((qd0, qd1, qd2, qd3), q_s, do_s)
    iota = lax.broadcasted_iota(jnp.int32, (KB, ROWS), 0)
    for u in range(UNITS):
        q = q_s[u]
        do = do_s[u]
        limit = lim[u : u + 1, :]

        def body(j, carry):
            m, l, d = carry
            k0 = pl.multiple_of(j * KB, KB)
            kv = kv_s[pl.ds(k0, KB), :]
            s = dot(kv[:, :HD], q, NT) * C2
            dp = dot(kv[:, HD:], do, NT)
            s = jnp.where(iota < limit - k0, s, NEG).reshape(KB // 8, 8, ROWS)
            mn = jnp.maximum(m, jnp.max(s, axis=0))
            a = jnp.exp2(m - mn)
            e = jnp.exp2(s - mn[None])
            l = l * a + jnp.sum(e, axis=0)
            d = d * a + jnp.sum(e * dp.reshape(KB // 8, 8, ROWS), axis=0)
            return mn, l, d

        zero = jnp.zeros((8, ROWS), jnp.float32)
        m, l, d = lax.fori_loop(0, meta[64 + u], body, (zero + NEG, zero, zero))
        live = jnp.where(m > 0.5 * NEG, 1.0, 0.0)
        top = jnp.max(m, axis=0, keepdims=True)
        a = jnp.exp2(m - top) * live
        ll = jnp.sum(l * a, axis=0, keepdims=True)
        dd = jnp.sum(d * a, axis=0, keepdims=True)
        safe = jnp.where(ll > 0, ll, 1.0)
        out[0, u : u + 1, :] = jnp.where(ll > 0, top + jnp.log2(safe), NEG)
        out[1, u : u + 1, :] = dd / safe


def grads_kernel(
    meta, lim, st0, st1, st2, st3, qd0, qd1, qd2, qd3, kv0, kv1, dq, dkv, q_s, do_s, kv_s, acc, dq_s
):
    load_sorted(meta, (kv0, kv1), kv_s)
    load_rows((qd0, qd1, qd2, qd3), q_s, do_s)
    acc[...] = jnp.zeros_like(acc)
    sts = (st0, st1, st2, st3)
    top = jnp.maximum(jnp.maximum(st0[0], st1[0]), jnp.maximum(st2[0], st3[0]))
    ws = [jnp.exp2(t[0] - top) for t in sts]
    total = ws[0] + ws[1] + ws[2] + ws[3]
    lse = top + jnp.log2(total)
    delta = (ws[0] * st0[1] + ws[1] * st1[1] + ws[2] * st2[1] + ws[3] * st3[1]) / total
    iota = lax.broadcasted_iota(jnp.int32, (KB, ROWS), 0)
    for u in range(UNITS):
        q = q_s[u]
        do = do_s[u]
        limit = lim[u : u + 1, :]
        lse_u = lse[u : u + 1]
        delta_u = delta[u : u + 1]
        dq_s[...] = jnp.zeros_like(dq_s)

        def body(j, carry):
            k0 = pl.multiple_of(j * KB, KB)
            kv = kv_s[pl.ds(k0, KB), :]
            k = kv[:, :HD]
            s = dot(k, q, NT)
            dp = dot(kv[:, HD:], do, NT)
            p = jnp.where(iota < limit - k0, jnp.exp2(s * C2 - lse_u), 0.0)
            ds = (p * (dp - delta_u)).astype(jnp.bfloat16)
            acc[pl.ds(k0, KB), :HD] += dot(ds, q, NN)
            acc[pl.ds(k0, KB), HD:] += dot(p.astype(jnp.bfloat16), do, NN)
            dq_s[...] += dot(ds, k, TN)
            return carry

        lax.fori_loop(0, meta[64 + u], body, 0)
        t = slice((u % 2) * SPAN, (u % 2 + 1) * SPAN)
        for h in range(HEADS):
            dq[u // 2, t, h * HD : (h + 1) * HD] = (
                dq_s[h * SPAN : (h + 1) * SPAN, :] * SCALE
            ).astype(jnp.bfloat16)
    for g in range(2):
        for s in range(32):
            r = pl.multiple_of(meta[g * 32 + s] * SPAN, SPAN)
            t = slice((s % 2) * SPAN, (s % 2 + 1) * SPAN)
            dkv[g, s // 2, t, :HD] = (acc[pl.ds(r, SPAN), :HD] * SCALE).astype(jnp.bfloat16)
            dkv[g, s // 2, t, HD:] = acc[pl.ds(r, SPAN), HD:].astype(jnp.bfloat16)


VM = pl.BlockSpec(memory_space=pltpu.VMEM)
SM = pl.BlockSpec(memory_space=pltpu.SMEM)
PARAMS = pltpu.CompilerParams(vmem_limit_bytes=48 * 2**20)
COPIES = [
    pltpu.VMEM((UNITS, ROWS, HD), jnp.bfloat16),
    pltpu.VMEM((UNITS, ROWS, HD), jnp.bfloat16),
    pltpu.VMEM((KEYS, 2 * HD), jnp.bfloat16),
]


def stats(meta, lim, qds, kvs):
    return pl.pallas_call(
        stats_kernel,
        out_shape=jax.ShapeDtypeStruct((2, UNITS, ROWS), jnp.float32),
        in_specs=[SM] + [VM] * 7,
        out_specs=VM,
        scratch_shapes=COPIES,
        compiler_params=PARAMS,
        name="stats",
    )(meta, lim, *qds, *kvs)


def grads(meta, lim, sts, qds, kvs):
    return pl.pallas_call(
        grads_kernel,
        out_shape=(
            jax.ShapeDtypeStruct((4, 2 * SPAN, HEADS * HD), jnp.bfloat16),
            jax.ShapeDtypeStruct((2, 16, 2 * SPAN, 2 * HD), jnp.bfloat16),
        ),
        in_specs=[SM] + [VM] * 11,
        out_specs=(VM, VM),
        scratch_shapes=COPIES
        + [pltpu.VMEM((KEYS, 2 * HD), jnp.float32), pltpu.VMEM((ROWS, HD), jnp.float32)],
        compiler_params=PARAMS,
        name="grads",
    )(meta, lim, *sts, *qds, *kvs)


def x_shift(a, step):
    return lax.ppermute(a, "x", [(i, (i + step) % 4) for i in range(4)])


def core_swap(a):
    return lax.ppermute(a, "core", [(0, 1), (1, 0)])


def local(queries, keys, values, grad_out, span_slot):
    y, zl, core, zh, x = (lax.axis_index(a) for a in AXES)
    qd = jnp.concatenate([queries, grad_out], axis=1)
    qds = [qd] + [x_shift(qd, r) for r in (1, 2, 3)]
    kv = jnp.concatenate([keys, values], axis=1)
    mine = lax.all_to_all(
        jnp.broadcast_to(kv[None], (16,) + kv.shape), ("y", "zl", "zh"), 0, 0, tiled=True
    )
    kvs = [mine, core_swap(mine)]

    grid = span_slot.reshape(4, 2, 2, 2, 4, 2)
    at_x = lax.dynamic_index_in_dim(grid, x, 4, keepdims=False)
    key_spans = jnp.concatenate(
        [
            lax.dynamic_index_in_dim(at_x, c, 2, keepdims=False).reshape(32)
            for c in (core, 1 - core)
        ]
    )
    ring = grid[y, zl, core, zh]
    query_spans = jnp.concatenate([ring[(x - r) % 4] for r in range(4)])
    rank = jnp.sum((key_spans[None, :] < key_spans[:, None]).astype(jnp.int32), axis=1)
    below = jnp.sum((key_spans[None, :] < query_spans[:, None]).astype(jnp.int32), axis=1)
    own = jnp.any(key_spans[None, :] == query_spans[:, None], axis=1)
    token = jnp.tile(jnp.arange(SPAN, dtype=jnp.int32), HEADS)
    lim = below[:, None] * SPAN + jnp.where(own[:, None], token[None, :] + 1, 0)
    tiles = (below * SPAN + jnp.where(own, SPAN, 0) + KB - 1) // KB
    meta = jnp.concatenate([rank, tiles]).astype(jnp.int32)

    part = stats(meta, lim, qds, kvs)
    def turned(r):
        got = x_shift(part, r)
        return jnp.roll(got, 2 * r, axis=1)

    sts = [part] + [turned(r) for r in (1, 2, 3)]
    dq, dkv = grads(meta, lim, sts, qds, kvs)

    pair = (dkv[0].astype(jnp.float32) + core_swap(dkv[1]).astype(jnp.float32)).astype(jnp.bfloat16)
    parts = lax.all_to_all(pair, ("y", "zl", "zh"), 0, 0, tiled=True)
    summed = jnp.sum(parts.astype(jnp.float32), axis=0)
    total = dq[0].astype(jnp.float32)
    for r in (1, 2, 3):
        total = total + x_shift(dq[r], 4 - r).astype(jnp.float32)
    return (
        total.astype(jnp.bfloat16),
        summed[:, :HD].astype(jnp.bfloat16),
        summed[:, HD:].astype(jnp.bfloat16),
    )


def solution(mesh):
    fine = Mesh(mesh.devices.reshape(4, 2, 2, 2, 4), AXES)
    rows = P(AXES, None)
    return jax.shard_map(
        local,
        mesh=fine,
        in_specs=(rows, rows, rows, rows, P()),
        out_specs=(rows, rows, rows),
        check_vma=False,
    )
```

```python
import math

import jax
import jax.numpy as jnp
from jax import lax
from jax.experimental import pallas as pl
from jax.experimental.pallas import tpu as pltpu
from jax.sharding import Mesh, PartitionSpec as P

AXES = ("y", "zl", "core", "zh", "x")
NEG = -1e30
HD = 128
SCALE = 1.0 / math.sqrt(HD)
C2 = math.log2(math.e) * SCALE
SPAN = 64
HEADS = 6
WIDE = HEADS * HD
KEYS = 4096
KB = 256
R = 256
GROUPS = 12
UNROLL = 8
LIST = 136
IN, OUT, UNIT, COUNT = 0, 64, 128, 136
GROUP, BLOCK = 137, 137 + LIST

NT = (((1,), (1,)), ((), ()))
NN = (((1,), (0,)), ((), ()))
TN = (((0,), (0,)), ((), ()))


def dot(a, b, dims):
    return lax.dot_general(a, b, dims, preferred_element_type=jnp.float32)


def aligned(i, n):
    return pl.multiple_of(i * n, n)


def tree(op, xs):
    acc = list(xs[:4])
    for i, x in enumerate(xs[4:]):
        acc[i % 4] = op(acc[i % 4], x)
    return op(op(acc[0], acc[1]), op(acc[2], acc[3]))


def load_sorted(meta, kvs, kv_s):
    s = 0
    for ref in kvs:
        for e in range(ref.shape[0]):
            for half in range(2):
                r = aligned(meta[IN + s], SPAN)
                kv_s[pl.ds(r, SPAN), :] = ref[e, half * SPAN : (half + 1) * SPAN, :]
                s += 1


def row_of(place, h):
    odd = place % 2
    inner = odd * 512 + h * SPAN if h < 4 else R + odd * 128 + (h - 4) * SPAN
    return pl.multiple_of((place // 2) * 768 + inner, SPAN)


def load_rows(meta, qs, dos, q_s, do_s):
    for d in range(4):
        for half in range(2):
            place = meta[UNIT + 2 * d + half]
            t = slice(half * SPAN, (half + 1) * SPAN)
            for h in range(HEADS):
                r = row_of(place, h)
                for (ref, first), dst in ((qs[d], q_s), (dos[d], do_s)):
                    dst[pl.ds(r, SPAN), :] = ref[t, first + h * HD : first + (h + 1) * HD]
    q_s[GROUPS * R :, :] = jnp.zeros((R, HD), q_s.dtype)
    do_s[GROUPS * R :, :] = jnp.zeros((R, HD), do_s.dtype)


def products(meta, t, q_s, do_s, kv_s, s_b, dp_b):
    r, k = aligned(meta[GROUP + t], R), aligned(meta[BLOCK + t], KB)
    s_b[...] = dot(kv_s[pl.ds(k, KB), :HD], q_s[pl.ds(r, R), :], NT)
    dp_b[...] = dot(kv_s[pl.ds(k, KB), HD:], do_s[pl.ds(r, R), :], NT)


def operands(refs):
    qd0, qd1, q2, do2, qd3 = refs[:5]
    qs = ((qd0, 0), (qd1, 0), (q2, 0), (qd3, 0))
    dos = ((qd0, WIDE), (qd1, WIDE), (do2, 0), (qd3, WIDE))
    return qs, dos, refs[5:13]


def stats_kernel(meta, lim, *refs):
    qs, dos, kvs = operands(refs)
    out, q_s, do_s, kv_s, s0, s1, dp0, dp1, m_s, l_s, d_s = refs[13:]
    load_sorted(meta, kvs, kv_s)
    load_rows(meta, qs, dos, q_s, do_s)
    m_s[...] = jnp.full_like(m_s, NEG)
    l_s[...] = jnp.zeros_like(l_s)
    d_s[...] = jnp.zeros_like(d_s)
    iota = lax.broadcasted_iota(jnp.int32, (KB, R), 0)

    def online(t, s_b, dp_b):
        g = meta[GROUP + t]
        limit = lim[pl.ds(g, 1), :] - meta[BLOCK + t] * KB
        rows = [slice(8 * i, 8 * i + 8) for i in range(KB // 8)]
        s = [jnp.where(iota[r] < limit, s_b[r, :] * C2, NEG) for r in rows]
        m = m_s[g]
        top = jnp.maximum(m, tree(jnp.maximum, s))
        a = jnp.exp2(m - top)
        e = [jnp.exp2(x - top) for x in s]
        m_s[g] = top
        l_s[g] = l_s[g] * a + tree(jnp.add, e)
        d_s[g] = d_s[g] * a + tree(jnp.add, [x * dp_b[r, :] for r, x in zip(rows, e)])

    ss, dps = (s0, s1), (dp0, dp1)
    products(meta, 0, q_s, do_s, kv_s, s0, dp0)

    def body(i, carry):
        for v in range(UNROLL):
            t = i * UNROLL + v
            products(meta, t + 1, q_s, do_s, kv_s, ss[(v + 1) % 2], dps[(v + 1) % 2])
            online(t, ss[v % 2], dps[v % 2])
        return carry

    lax.fori_loop(0, (meta[COUNT] + UNROLL - 1) // UNROLL, body, 0)
    for g in range(GROUPS):
        m = m_s[g]
        live = jnp.where(m > 0.5 * NEG, 1.0, 0.0)
        top = jnp.max(m, axis=0, keepdims=True)
        a = jnp.exp2(m - top) * live
        ll = jnp.sum(l_s[g] * a, axis=0, keepdims=True)
        dd = jnp.sum(d_s[g] * a, axis=0, keepdims=True)
        safe = jnp.where(ll > 0, ll, 1.0)
        out[0, g : g + 1, :] = jnp.where(ll > 0, top + jnp.log2(safe), NEG)
        out[1, g : g + 1, :] = dd / safe
    out[:, GROUPS:, :] = jnp.zeros((2, 16 - GROUPS, R), jnp.float32)


def grads_kernel(meta, lim, st0, st1, st2, st3, *refs):
    qs, dos, kvs = operands(refs)
    dqs, dkvs = refs[13:17], refs[17:19]
    q_s, do_s, kv_s, s0, s1, dp0, dp1, acc, dq_s, p0, p1, ds0, ds1, lse, delta = refs[19:]
    load_sorted(meta, kvs, kv_s)
    load_rows(meta, qs, dos, q_s, do_s)
    acc[...] = jnp.zeros_like(acc)
    dq_s[...] = jnp.zeros_like(dq_s)
    sts = (st0, st1, st2, st3)
    top = jnp.maximum(jnp.maximum(st0[0], st1[0]), jnp.maximum(st2[0], st3[0]))
    ws = [jnp.exp2(t[0] - top) for t in sts]
    total = ws[0] + ws[1] + ws[2] + ws[3]
    lse[...] = top + jnp.log2(total)
    delta[...] = sum(w * t[1] for w, t in zip(ws, sts)) / total
    iota = lax.broadcasted_iota(jnp.int32, (KB, R), 0)

    def weights(t, s_b, dp_b, p_b, ds_b):
        g = meta[GROUP + t]
        limit = lim[pl.ds(g, 1), :] - meta[BLOCK + t] * KB
        p = jnp.where(iota < limit, jnp.exp2(s_b[...] * C2 - lse[pl.ds(g, 1), :]), 0.0)
        p_b[...] = p.astype(jnp.bfloat16)
        ds_b[...] = (p * (dp_b[...] - delta[pl.ds(g, 1), :])).astype(jnp.bfloat16)

    def sums(t, p_b, ds_b):
        r, k = aligned(meta[GROUP + t], R), aligned(meta[BLOCK + t], KB)
        dk = dot(ds_b[...], q_s[pl.ds(r, R), :], NN)
        dv = dot(p_b[...], do_s[pl.ds(r, R), :], NN)
        dq = dot(ds_b[...], kv_s[pl.ds(k, KB), :HD], TN)
        acc[pl.ds(k, KB), :HD] += dk
        acc[pl.ds(k, KB), HD:] += dv
        dq_s[pl.ds(r, R), :] += dq

    ss, dps, ps, dss = (s0, s1), (dp0, dp1), (p0, p1), (ds0, ds1)
    products(meta, 0, q_s, do_s, kv_s, s0, dp0)
    products(meta, 1, q_s, do_s, kv_s, s1, dp1)
    weights(0, s0, dp0, p0, ds0)

    def body(i, carry):
        for v in range(UNROLL):
            t, a, b = i * UNROLL + v, v % 2, 1 - v % 2
            products(meta, t + 2, q_s, do_s, kv_s, ss[a], dps[a])
            weights(t + 1, ss[b], dps[b], ps[b], dss[b])
            sums(t, ps[a], dss[a])
        return carry

    lax.fori_loop(0, (meta[COUNT] + UNROLL - 1) // UNROLL, body, 0)
    for d in range(4):
        for half in range(2):
            place = meta[UNIT + 2 * d + half]
            t = slice(half * SPAN, (half + 1) * SPAN)
            for h in range(HEADS):
                got = dq_s[pl.ds(row_of(place, h), SPAN), :] * SCALE
                dqs[d][t, h * HD : (h + 1) * HD] = got.astype(dqs[d].dtype)
    for c in range(2):
        for s in range(32):
            r = aligned(meta[OUT + c * 32 + s], SPAN)
            t = slice((s % 2) * SPAN, (s % 2 + 1) * SPAN)
            dkvs[c][s // 2, t, :HD] = (acc[pl.ds(r, SPAN), :HD] * SCALE).astype(jnp.bfloat16)
            dkvs[c][s // 2, t, HD:] = acc[pl.ds(r, SPAN), HD:].astype(jnp.bfloat16)


VM = pl.BlockSpec(memory_space=pltpu.VMEM)
SM = pl.BlockSpec(memory_space=pltpu.SMEM)
PARAMS = pltpu.CompilerParams(vmem_limit_bytes=48 * 2**20)
COPIES = [
    pltpu.VMEM(((GROUPS + 1) * R, HD), jnp.bfloat16),
    pltpu.VMEM(((GROUPS + 1) * R, HD), jnp.bfloat16),
    pltpu.VMEM((KEYS, 2 * HD), jnp.bfloat16),
] + [pltpu.VMEM((KB, R), jnp.float32)] * 4


def stats(meta, lim, arrays):
    return pl.pallas_call(
        stats_kernel,
        out_shape=jax.ShapeDtypeStruct((2, 16, R), jnp.float32),
        in_specs=[SM] + [VM] * 14,
        out_specs=VM,
        scratch_shapes=COPIES + [pltpu.VMEM((GROUPS + 1, 8, R), jnp.float32)] * 3,
        compiler_params=PARAMS,
        name="stats",
    )(meta, lim, *arrays)


def grads(meta, lim, sts, arrays):
    dq = [jax.ShapeDtypeStruct((2 * SPAN, WIDE), t) for t in (jnp.float32,) + (jnp.bfloat16,) * 3]
    dkv = [jax.ShapeDtypeStruct((16, 2 * SPAN, 2 * HD), jnp.bfloat16)] * 2
    return pl.pallas_call(
        grads_kernel,
        out_shape=dq + dkv,
        in_specs=[SM] + [VM] * 18,
        out_specs=[VM] * 6,
        scratch_shapes=COPIES
        + [
            pltpu.VMEM((KEYS, 2 * HD), jnp.float32),
            pltpu.VMEM(((GROUPS + 1) * R, HD), jnp.float32),
        ]
        + [pltpu.VMEM((KB, R), jnp.bfloat16)] * 4
        + [pltpu.VMEM((16, R), jnp.float32)] * 2,
        compiler_params=PARAMS,
        name="grads",
    )(meta, lim, *sts, *arrays)


def shift(a, axis, step):
    if axis == "z":
        at = lambda z: (z % 2) * 2 + z // 2
        return lax.ppermute(a, ("zl", "zh"), [(at(i), at((i + step) % 4)) for i in range(4)])
    return lax.ppermute(a, axis, [(i, (i + step) % 4) for i in range(4)])


def core_swap(a):
    return lax.ppermute(a, "core", [(0, 1), (1, 0)])


def plan(span_slot):
    i32 = jnp.int32
    y, zl, core, zh, x = (lax.axis_index(a) for a in AXES)
    z = 2 * zh + zl
    grid = span_slot.reshape(4, 2, 2, 2, 4, 2)
    own_x = jnp.transpose(lax.dynamic_index_in_dim(grid, x, 4, keepdims=False), (2, 0, 3, 1, 4))
    own_x = own_x.reshape(2, 4, 4, 2)
    own_x = jnp.where(core == 0, own_x, own_x[::-1])
    by_z = jnp.stack([lax.dynamic_index_in_dim(own_x, (z - r) % 4, 2, keepdims=False) for r in range(4)], 1)
    by_yz = jnp.stack([lax.dynamic_index_in_dim(by_z, (y - r) % 4, 2, keepdims=False) for r in range(4)], 2)
    arrived = by_yz.reshape(64)
    owners = jnp.transpose(own_x.reshape(2, 4, 2, 2, 2), (0, 1, 3, 2, 4)).reshape(64)
    ring = grid[y, zl, core, zh]
    queries = jnp.concatenate([ring[(x - r) % 4] for r in range(4)])

    def rank(a, among):
        return jnp.sum((among[None, :] < a[:, None]).astype(i32), axis=1)

    place = rank(queries, queries)
    hit = (place[None, :] == jnp.arange(8)[:, None]).astype(i32)
    spans = jnp.sum(hit * queries[None, :], axis=1)
    below = rank(spans, owners)
    own = jnp.any(owners[None, :] == spans[:, None], axis=1).astype(i32)
    token = jnp.tile(jnp.arange(SPAN, dtype=i32), 2)
    seen = below[:, None] * SPAN + own[:, None] * (token[None, :] + 1)
    a, b = seen[0::2], seen[1::2]
    lim = jnp.stack([a, a, a, b, b, b], axis=1).reshape(GROUPS, R)
    lim = jnp.concatenate([lim, jnp.zeros((4, R), i32)])
    tiles = ((below + own) * SPAN + KB - 1) // KB
    each = jnp.stack([tiles[0::2], tiles[1::2], tiles[1::2]], axis=1).reshape(GROUPS)
    end = jnp.sum(jnp.tril(jnp.ones((GROUPS, GROUPS), i32)) * each[None, :], axis=1)
    t = jnp.arange(LIST, dtype=i32)
    past = (t[:, None] >= end[None, :]).astype(i32)
    group = jnp.sum(past, axis=1)
    block = jnp.where(group < GROUPS, t - jnp.sum(past * each[None, :], axis=1), 0)
    meta = [rank(arrived, owners), rank(owners, owners), place, end[-1:], group, block]
    return jnp.concatenate(meta).astype(i32), lim


def local(queries, keys, values, grad_out, span_slot):
    meta, lim = plan(span_slot)
    qd0 = jnp.concatenate([queries, grad_out], axis=1)
    qd1, qd3 = shift(qd0, "x", 1), shift(qd0, "x", 3)
    q2, do2 = shift(qd3[:, :WIDE], "x", 3), shift(qd1[:, WIDE:], "x", 1)
    kv = jnp.concatenate([keys, values], axis=1)[None]
    kv = jnp.concatenate([kv] + [shift(kv, "y", r) for r in (1, 2, 3)], axis=0)
    kvs = [kv] + [shift(kv, "z", r) for r in (1, 2, 3)]
    arrays = [qd0, qd1, q2, do2, qd3] + kvs + [core_swap(a) for a in kvs]

    part = stats(meta, lim, arrays)
    sts = [part] + [shift(part, "x", r) for r in (1, 2, 3)]
    dq0, dq1, dq2, dq3, dkv, dkv_other = grads(meta, lim, sts, arrays)

    pair = (dkv.astype(jnp.float32) + core_swap(dkv_other).astype(jnp.float32)).astype(jnp.bfloat16)
    parts = lax.all_to_all(pair, ("y", "zl", "zh"), 0, 0, tiled=True)
    summed = jnp.sum(parts.astype(jnp.float32), axis=0)
    for r, part in ((1, dq1), (2, dq2), (3, dq3)):
        dq0 = dq0 + shift(part, "x", 4 - r).astype(jnp.float32)
    return (
        dq0.astype(jnp.bfloat16),
        summed[:, :HD].astype(jnp.bfloat16),
        summed[:, HD:].astype(jnp.bfloat16),
    )


def solution(mesh):
    fine = Mesh(mesh.devices.reshape(4, 2, 2, 2, 4), AXES)
    rows = P(AXES, None)
    return jax.shard_map(
        local,
        mesh=fine,
        in_specs=(rows, rows, rows, rows, P()),
        out_specs=(rows, rows, rows),
        check_vma=False,
    )
```

```python
import math

import jax
import jax.numpy as jnp
import numpy as np
from jax import lax
from jax.experimental import pallas as pl
from jax.experimental.pallas import tpu as pltpu
from jax.sharding import Mesh, PartitionSpec as P

AXES = ("y", "zl", "core", "zh", "x")
SIZES = (4, 2, 2, 2, 4)
STEPS = (0, 1, 3, 2)
NEG = -1e30
HD = 128
SCALE = 1.0 / math.sqrt(HD)
C2 = math.log2(math.e) * SCALE
SPAN = 64
HEADS = 6
WIDE = HEADS * HD
KEYS = 4096
KB = 256
R = 256
GROUPS = 12
UNROLL = 8
LIST = 136
IN, UNIT, COUNT = 0, 64, 72
GROUP, BLOCK = 73, 73 + LIST

NT = (((1,), (1,)), ((), ()))
NN = (((1,), (0,)), ((), ()))
TN = (((0,), (0,)), ((), ()))


def dot(a, b, dims):
    return lax.dot_general(a, b, dims, preferred_element_type=jnp.float32)


def aligned(i, n):
    return pl.multiple_of(i * n, n)


def tree(op, xs):
    acc = list(xs[:4])
    for i, x in enumerate(xs[4:]):
        acc[i % 4] = op(acc[i % 4], x)
    return op(op(acc[0], acc[1]), op(acc[2], acc[3]))


def load_sorted(meta, kvs, kv_s):
    s = 0
    for ref in kvs:
        for e in range(ref.shape[0]):
            for half in range(2):
                r = aligned(meta[IN + s], SPAN)
                kv_s[pl.ds(r, SPAN), :] = ref[e, half * SPAN : (half + 1) * SPAN, :]
                s += 1


def row_of(place, h):
    odd = place % 2
    inner = odd * 512 + h * SPAN if h < 4 else R + odd * 128 + (h - 4) * SPAN
    return pl.multiple_of((place // 2) * 768 + inner, SPAN)


def load_rows(meta, qds, q_s, do_s):
    for d, ref in enumerate(qds):
        for half in range(2):
            place = meta[UNIT + 2 * d + half]
            t = slice(half * SPAN, (half + 1) * SPAN)
            for h in range(HEADS):
                r = row_of(place, h)
                q_s[pl.ds(r, SPAN), :] = ref[t, h * HD : (h + 1) * HD]
                do_s[pl.ds(r, SPAN), :] = ref[t, WIDE + h * HD : WIDE + (h + 1) * HD]
    q_s[GROUPS * R :, :] = jnp.zeros((R, HD), q_s.dtype)
    do_s[GROUPS * R :, :] = jnp.zeros((R, HD), do_s.dtype)


def products(meta, t, q_s, do_s, kv_s, s_b, dp_b):
    r, k = aligned(meta[GROUP + t], R), aligned(meta[BLOCK + t], KB)
    s_b[...] = dot(kv_s[pl.ds(k, KB), :HD], q_s[pl.ds(r, R), :], NT)
    dp_b[...] = dot(kv_s[pl.ds(k, KB), HD:], do_s[pl.ds(r, R), :], NT)


def stats_kernel(meta, lim, *refs):
    qds, kvs = refs[:4], refs[4:12]
    out, q_s, do_s, kv_s, s0, s1, dp0, dp1, m_s, l_s, d_s = refs[12:]
    load_sorted(meta, kvs, kv_s)
    load_rows(meta, qds, q_s, do_s)
    m_s[...] = jnp.full_like(m_s, NEG)
    l_s[...] = jnp.zeros_like(l_s)
    d_s[...] = jnp.zeros_like(d_s)
    iota = lax.broadcasted_iota(jnp.int32, (KB, R), 0)

    def online(t, s_b, dp_b):
        g = meta[GROUP + t]
        limit = lim[pl.ds(g, 1), :] - meta[BLOCK + t] * KB
        rows = [slice(8 * i, 8 * i + 8) for i in range(KB // 8)]
        s = [jnp.where(iota[r] < limit, s_b[r, :] * C2, NEG) for r in rows]
        m = m_s[g]
        top = jnp.maximum(m, tree(jnp.maximum, s))
        a = jnp.exp2(m - top)
        e = [jnp.exp2(x - top) for x in s]
        m_s[g] = top
        l_s[g] = l_s[g] * a + tree(jnp.add, e)
        d_s[g] = d_s[g] * a + tree(jnp.add, [x * dp_b[r, :] for r, x in zip(rows, e)])

    ss, dps = (s0, s1), (dp0, dp1)
    products(meta, 0, q_s, do_s, kv_s, s0, dp0)

    def body(i, carry):
        for v in range(UNROLL):
            t = i * UNROLL + v
            products(meta, t + 1, q_s, do_s, kv_s, ss[(v + 1) % 2], dps[(v + 1) % 2])
            online(t, ss[v % 2], dps[v % 2])
        return carry

    lax.fori_loop(0, (meta[COUNT] + UNROLL - 1) // UNROLL, body, 0)
    for g in range(GROUPS):
        m = m_s[g]
        live = jnp.where(m > 0.5 * NEG, 1.0, 0.0)
        top = jnp.max(m, axis=0, keepdims=True)
        a = jnp.exp2(m - top) * live
        ll = jnp.sum(l_s[g] * a, axis=0, keepdims=True)
        dd = jnp.sum(d_s[g] * a, axis=0, keepdims=True)
        safe = jnp.where(ll > 0, ll, 1.0)
        out[0, g : g + 1, :] = jnp.where(ll > 0, top + jnp.log2(safe), NEG)
        out[1, g : g + 1, :] = dd / safe
    out[:, GROUPS:, :] = jnp.zeros((2, 16 - GROUPS, R), jnp.float32)


def grads_kernel(meta, lim, st0, st1, st2, st3, *refs):
    qds, kvs = refs[:4], refs[4:12]
    dqs, dkvs, dkv_other = refs[12:16], refs[16:20], refs[20]
    q_s, do_s, kv_s, s0, s1, dp0, dp1, acc, dq_s, p0, p1, ds0, ds1, lse, delta = refs[21:]
    load_sorted(meta, kvs, kv_s)
    load_rows(meta, qds, q_s, do_s)
    acc[...] = jnp.zeros_like(acc)
    dq_s[...] = jnp.zeros_like(dq_s)
    sts = (st0, st1, st2, st3)
    top = jnp.maximum(jnp.maximum(st0[0], st1[0]), jnp.maximum(st2[0], st3[0]))
    ws = [jnp.exp2(t[0] - top) for t in sts]
    total = ws[0] + ws[1] + ws[2] + ws[3]
    lse[...] = top + jnp.log2(total)
    delta[...] = sum(w * t[1] for w, t in zip(ws, sts)) / total
    iota = lax.broadcasted_iota(jnp.int32, (KB, R), 0)

    def weights(t, s_b, dp_b, p_b, ds_b):
        g = meta[GROUP + t]
        limit = lim[pl.ds(g, 1), :] - meta[BLOCK + t] * KB
        p = jnp.where(iota < limit, jnp.exp2(s_b[...] * C2 - lse[pl.ds(g, 1), :]), 0.0)
        p_b[...] = p.astype(jnp.bfloat16)
        ds_b[...] = (p * (dp_b[...] - delta[pl.ds(g, 1), :])).astype(jnp.bfloat16)

    def sums(t, p_b, ds_b):
        r, k = aligned(meta[GROUP + t], R), aligned(meta[BLOCK + t], KB)
        dk = dot(ds_b[...], q_s[pl.ds(r, R), :], NN)
        dv = dot(p_b[...], do_s[pl.ds(r, R), :], NN)
        dq = dot(ds_b[...], kv_s[pl.ds(k, KB), :HD], TN)
        acc[pl.ds(k, KB), :HD] += dk
        acc[pl.ds(k, KB), HD:] += dv
        dq_s[pl.ds(r, R), :] += dq

    ss, dps, ps, dss = (s0, s1), (dp0, dp1), (p0, p1), (ds0, ds1)
    products(meta, 0, q_s, do_s, kv_s, s0, dp0)
    products(meta, 1, q_s, do_s, kv_s, s1, dp1)
    weights(0, s0, dp0, p0, ds0)

    def body(i, carry):
        for v in range(UNROLL):
            t, a, b = i * UNROLL + v, v % 2, 1 - v % 2
            products(meta, t + 2, q_s, do_s, kv_s, ss[a], dps[a])
            weights(t + 1, ss[b], dps[b], ps[b], dss[b])
            sums(t, ps[a], dss[a])
        return carry

    lax.fori_loop(0, (meta[COUNT] + UNROLL - 1) // UNROLL, body, 0)
    for d in range(4):
        for half in range(2):
            place = meta[UNIT + 2 * d + half]
            t = slice(half * SPAN, (half + 1) * SPAN)
            for h in range(HEADS):
                got = dq_s[pl.ds(row_of(place, h), SPAN), :] * SCALE
                dqs[d][t, h * HD : (h + 1) * HD] = got.astype(dqs[d].dtype)
    for s in range(64):
        r = aligned(meta[IN + s], SPAN)
        t = slice((s % 2) * SPAN, (s % 2 + 1) * SPAN)
        e = (s // 2) % 4
        ref = dkvs[s // 8] if s < 32 else dkv_other.at[s // 8 - 4]
        ref[e, t, :HD] = (acc[pl.ds(r, SPAN), :HD] * SCALE).astype(jnp.bfloat16)
        ref[e, t, HD:] = acc[pl.ds(r, SPAN), HD:].astype(jnp.bfloat16)


VM = pl.BlockSpec(memory_space=pltpu.VMEM)
SM = pl.BlockSpec(memory_space=pltpu.SMEM)
PARAMS = pltpu.CompilerParams(vmem_limit_bytes=48 * 2**20)
COPIES = [
    pltpu.VMEM(((GROUPS + 1) * R, HD), jnp.bfloat16),
    pltpu.VMEM(((GROUPS + 1) * R, HD), jnp.bfloat16),
    pltpu.VMEM((KEYS, 2 * HD), jnp.bfloat16),
] + [pltpu.VMEM((KB, R), jnp.float32)] * 4


def stats(meta, lim, arrays):
    return pl.pallas_call(
        stats_kernel,
        out_shape=jax.ShapeDtypeStruct((2, 16, R), jnp.float32),
        in_specs=[SM] + [VM] * 13,
        out_specs=VM,
        scratch_shapes=COPIES + [pltpu.VMEM((GROUPS + 1, 8, R), jnp.float32)] * 3,
        compiler_params=PARAMS,
        name="stats",
    )(meta, lim, *arrays)


def grads(meta, lim, sts, arrays):
    dq = [jax.ShapeDtypeStruct((2 * SPAN, WIDE), t) for t in (jnp.float32,) + (jnp.bfloat16,) * 3]
    dkv = [jax.ShapeDtypeStruct((4, 2 * SPAN, 2 * HD), jnp.bfloat16)] * 4
    dkv += [jax.ShapeDtypeStruct((4, 4, 2 * SPAN, 2 * HD), jnp.bfloat16)]
    return pl.pallas_call(
        grads_kernel,
        out_shape=dq + dkv,
        in_specs=[SM] + [VM] * 17,
        out_specs=[VM] * 9,
        scratch_shapes=COPIES
        + [
            pltpu.VMEM((KEYS, 2 * HD), jnp.float32),
            pltpu.VMEM(((GROUPS + 1) * R, HD), jnp.float32),
        ]
        + [pltpu.VMEM((KB, R), jnp.bfloat16)] * 4
        + [pltpu.VMEM((16, R), jnp.float32)] * 2,
        compiler_params=PARAMS,
        name="grads",
    )(meta, lim, *sts, *arrays)


def permute(a, move):
    pairs = []
    for i in range(128):
        y, zl, core, zh, x = (int(c) for c in np.unravel_index(i, SIZES))
        y, z, core, x = (c % n for c, n in zip(move(y, 2 * zh + zl, core, x), (4, 4, 2, 4)))
        pairs.append((i, int(np.ravel_multi_index((y, z % 2, core, z // 2, x), SIZES))))
    return lax.ppermute(a, AXES, pairs)


def x_shift(a, step):
    return permute(a, lambda y, z, core, x: (y, z, core, x + step))


def first_shift(a, step):
    return permute(a, lambda y, z, core, x: (y, z + step, core, x) if core else (y + step, z, core, x))


def second_shift(a, step):
    return permute(a, lambda y, z, core, x: (y + step, z, core, x) if core else (y, z + step, core, x))


def core_swap(a):
    return permute(a, lambda y, z, core, x: (y, z, 1 - core, x))


def plan(span_slot):
    i32 = jnp.int32
    y, zl, core, zh, x = (lax.axis_index(a) for a in AXES)
    z = 2 * zh + zl
    grid = span_slot.reshape(*SIZES, 2)
    own_x = jnp.transpose(lax.dynamic_index_in_dim(grid, x, 4, keepdims=False), (2, 0, 3, 1, 4))
    own_x = own_x.reshape(2, 4, 4, 2)
    by_y = jnp.stack([lax.dynamic_index_in_dim(own_x, (y - r) % 4, 1, keepdims=False) for r in STEPS], 1)
    by_yz = jnp.stack([lax.dynamic_index_in_dim(by_y, (z - r) % 4, 2, keepdims=False) for r in STEPS], 2)
    of_core = jnp.stack([jnp.transpose(by_yz[0], (1, 0, 2)), by_yz[1]])
    arrived = jnp.where(core == 0, of_core, of_core[::-1]).reshape(64)
    ring = grid[y, zl, core, zh]
    queries = jnp.concatenate([ring[(x - r) % 4] for r in STEPS])

    def rank(a, among):
        return jnp.sum((among[None, :] < a[:, None]).astype(i32), axis=1)

    place = rank(queries, queries)
    hit = (place[None, :] == jnp.arange(8)[:, None]).astype(i32)
    spans = jnp.sum(hit * queries[None, :], axis=1)
    below = rank(spans, arrived)
    own = jnp.any(arrived[None, :] == spans[:, None], axis=1).astype(i32)
    token = jnp.tile(jnp.arange(SPAN, dtype=i32), 2)
    seen = below[:, None] * SPAN + own[:, None] * (token[None, :] + 1)
    a, b = seen[0::2], seen[1::2]
    lim = jnp.stack([a, a, a, b, b, b], axis=1).reshape(GROUPS, R)
    lim = jnp.concatenate([lim, jnp.zeros((4, R), i32)])
    tiles = ((below + own) * SPAN + KB - 1) // KB
    each = jnp.stack([tiles[0::2], tiles[1::2], tiles[1::2]], axis=1).reshape(GROUPS)
    end = jnp.sum(jnp.tril(jnp.ones((GROUPS, GROUPS), i32)) * each[None, :], axis=1)
    t = jnp.arange(LIST, dtype=i32)
    past = (t[:, None] >= end[None, :]).astype(i32)
    group = jnp.sum(past, axis=1)
    block = jnp.where(group < GROUPS, t - jnp.sum(past * each[None, :], axis=1), 0)
    meta = [rank(arrived, arrived), place, end[-1:], group, block]
    return jnp.concatenate(meta).astype(i32), lim


def local(queries, keys, values, grad_out, span_slot):
    meta, lim = plan(span_slot)
    kv = jnp.concatenate([keys, values], axis=1)[None]
    kv = jnp.concatenate([kv] + [first_shift(kv, r) for r in STEPS[1:]], axis=0)
    kvs = [kv] + [second_shift(kv, r) for r in STEPS[1:]]
    qd = jnp.concatenate([queries, grad_out], axis=1)
    qds = [qd] + [x_shift(qd, r) for r in STEPS[1:]]
    kvs[1], meta, lim = lax.optimization_barrier((kvs[1], meta, lim))
    arrays = qds + kvs + [core_swap(a) for a in kvs]

    part = stats(meta, lim, arrays)
    sts = [part] + [x_shift(part, r) for r in (1, 2, 3)]
    dqs_dkv = grads(meta, lim, sts, arrays)
    dqs, dkv, dkv_other = dqs_dkv[:4], dqs_dkv[4:8], dqs_dkv[8]

    def total(*parts):
        out = parts[0].astype(jnp.float32)
        for part in parts[1:]:
            out = out + part.astype(jnp.float32)
        return out

    dq = total(dqs[0], *[x_shift(a, -r) for r, a in zip(STEPS[1:], dqs[1:])])
    other = core_swap(dkv_other)
    pairs = [total(a, other[i]).astype(jnp.bfloat16) for i, a in enumerate(dkv)]
    some = total(pairs[0], *[second_shift(a, -r) for r, a in zip(STEPS[1:], pairs[1:])])
    sent = [first_shift(some[i].astype(jnp.bfloat16), -r) for i, r in ((1, 1), (2, 3), (3, 2))]
    summed = total(some[0], *sent)
    return (
        dq.astype(jnp.bfloat16),
        summed[:, :HD].astype(jnp.bfloat16),
        summed[:, HD:].astype(jnp.bfloat16),
    )


def solution(mesh):
    fine = Mesh(mesh.devices.reshape(4, 2, 2, 2, 4), AXES)
    rows = P(AXES, None)
    return jax.shard_map(
        local,
        mesh=fine,
        in_specs=(rows, rows, rows, rows, P()),
        out_specs=(rows, rows, rows),
        check_vma=False,
    )
```

```python
import math

import jax
import jax.numpy as jnp
import numpy as np
from jax import lax
from jax.experimental import pallas as pl
from jax.experimental.pallas import tpu as pltpu
from jax.sharding import Mesh, PartitionSpec as P

AXES = ("y", "zl", "core", "zh", "x")
SIZES = (4, 2, 2, 2, 4)
STEPS = (0, 1, 3, 2)
NEG = -1e30
HD = 128
SCALE = 1.0 / math.sqrt(HD)
C2 = math.log2(math.e) * SCALE
SPAN = 64
HEADS = 6
WIDE = HEADS * HD
KEYS = 4096
KB = 256
R = 256
GROUPS = 12
UNROLL = 8
LIST = 136
IN, UNIT, COUNT = 0, 64, 72
GROUP, BLOCK = 73, 73 + LIST

NT = (((1,), (1,)), ((), ()))
NN = (((1,), (0,)), ((), ()))
TN = (((0,), (0,)), ((), ()))


def dot(a, b, dims):
    return lax.dot_general(a, b, dims, preferred_element_type=jnp.float32)


def aligned(i, n):
    return pl.multiple_of(i * n, n)


def tree(op, xs):
    acc = list(xs[:4])
    for i, x in enumerate(xs[4:]):
        acc[i % 4] = op(acc[i % 4], x)
    return op(op(acc[0], acc[1]), op(acc[2], acc[3]))


def merged(lse, delta, lse_b, delta_b):
    top = jnp.maximum(lse, lse_b)
    w, w_b = jnp.exp2(lse - top), jnp.exp2(lse_b - top)
    total = w + w_b
    return top + jnp.log2(total), (w * delta + w_b * delta_b) / total


def tiles_loop(count, step):
    def many(i, carry):
        for v in range(UNROLL):
            step(i * UNROLL + v, v)
        return carry

    def few(i, carry):
        for v in range(2):
            step(i * 2 + v, v)
        return carry

    bodies = count // UNROLL
    lax.fori_loop(0, bodies, many, 0)
    lax.fori_loop(bodies * (UNROLL // 2), (count + 1) // 2, few, 0)


def load_sorted(meta, kvs, kv_s):
    for s in range(64):
        r = aligned(meta[IN + s], SPAN)
        t = slice((s % 2) * SPAN, (s % 2 + 1) * SPAN)
        kv_s[pl.ds(r, SPAN), :] = kvs[s // 16][(s // 4) % 4, (s // 2) % 2, t, :]


def row_of(place, h):
    odd = place % 2
    inner = odd * 512 + h * SPAN if h < 4 else R + odd * 128 + (h - 4) * SPAN
    return pl.multiple_of((place // 2) * 768 + inner, SPAN)


def load_rows(meta, qds, q_s, do_s):
    for d, ref in enumerate(qds):
        for half in range(2):
            place = meta[UNIT + 2 * d + half]
            t = slice(half * SPAN, (half + 1) * SPAN)
            for h in range(HEADS):
                r = row_of(place, h)
                q_s[pl.ds(r, SPAN), :] = ref[t, h * HD : (h + 1) * HD]
                do_s[pl.ds(r, SPAN), :] = ref[t, WIDE + h * HD : WIDE + (h + 1) * HD]
    q_s[GROUPS * R :, :] = jnp.zeros((R, HD), q_s.dtype)
    do_s[GROUPS * R :, :] = jnp.zeros((R, HD), do_s.dtype)


def products(meta, t, q_s, do_s, kv_s, s_b, dp_b):
    r, k = aligned(meta[GROUP + t], R), aligned(meta[BLOCK + t], KB)
    s_b[...] = dot(kv_s[pl.ds(k, KB), :HD], q_s[pl.ds(r, R), :], NT)
    dp_b[...] = dot(kv_s[pl.ds(k, KB), HD:], do_s[pl.ds(r, R), :], NT)


def stats_kernel(meta, lim, *refs):
    qds, kvs = refs[:4], refs[4:8]
    out, q_s, do_s, kv_s, s0, s1, dp0, dp1, m_s, l_s, d_s = refs[8:]
    load_sorted(meta, kvs, kv_s)
    load_rows(meta, qds, q_s, do_s)
    m_s[...] = jnp.full_like(m_s, NEG)
    l_s[...] = jnp.zeros_like(l_s)
    d_s[...] = jnp.zeros_like(d_s)
    iota = lax.broadcasted_iota(jnp.int32, (KB, R), 0)

    def online(t, s_b, dp_b):
        g = meta[GROUP + t]
        limit = lim[pl.ds(g, 1), :] - meta[BLOCK + t] * KB
        rows = [slice(8 * i, 8 * i + 8) for i in range(KB // 8)]
        s = [jnp.where(iota[r] < limit, s_b[r, :] * C2, NEG) for r in rows]
        m = m_s[g]
        top = jnp.maximum(m, tree(jnp.maximum, s))
        a = jnp.exp2(m - top)
        e = [jnp.exp2(x - top) for x in s]
        m_s[g] = top
        l_s[g] = l_s[g] * a + tree(jnp.add, e)
        d_s[g] = d_s[g] * a + tree(jnp.add, [x * dp_b[r, :] for r, x in zip(rows, e)])

    ss, dps = (s0, s1), (dp0, dp1)
    products(meta, 0, q_s, do_s, kv_s, s0, dp0)

    def step(t, v):
        products(meta, t + 1, q_s, do_s, kv_s, ss[(v + 1) % 2], dps[(v + 1) % 2])
        online(t, ss[v % 2], dps[v % 2])

    tiles_loop(meta[COUNT], step)
    for g in range(GROUPS):
        m = m_s[g]
        live = jnp.where(m > 0.5 * NEG, 1.0, 0.0)
        top = jnp.max(m, axis=0, keepdims=True)
        a = jnp.exp2(m - top) * live
        ll = jnp.sum(l_s[g] * a, axis=0, keepdims=True)
        dd = jnp.sum(d_s[g] * a, axis=0, keepdims=True)
        safe = jnp.where(ll > 0, ll, 1.0)
        out[0, g : g + 1, :] = jnp.where(ll > 0, top + jnp.log2(safe), NEG)
        out[1, g : g + 1, :] = dd / safe
    out[:, GROUPS:, :] = jnp.zeros((2, 16 - GROUPS, R), jnp.float32)


def grads_kernel(meta, lim, st0, st1, *refs):
    qds, kvs = refs[:4], refs[4:8]
    dqs, dkvs, dkv_other = refs[8:12], refs[12:16], refs[16]
    q_s, do_s, kv_s, s0, s1, dp0, dp1, acc, dq_s, p0, p1, ds0, ds1, lse, delta = refs[17:]
    load_sorted(meta, kvs, kv_s)
    load_rows(meta, qds, q_s, do_s)
    acc[...] = jnp.zeros_like(acc)
    dq_s[...] = jnp.zeros_like(dq_s)
    lse[...], delta[...] = merged(st0[0], st0[1], st1[0], st1[1])
    iota = lax.broadcasted_iota(jnp.int32, (KB, R), 0)

    def weights(t, s_b, dp_b, p_b, ds_b):
        g = meta[GROUP + t]
        limit = lim[pl.ds(g, 1), :] - meta[BLOCK + t] * KB
        p = jnp.where(iota < limit, jnp.exp2(s_b[...] * C2 - lse[pl.ds(g, 1), :]), 0.0)
        p_b[...] = p.astype(jnp.bfloat16)
        ds_b[...] = (p * (dp_b[...] - delta[pl.ds(g, 1), :])).astype(jnp.bfloat16)

    def sums(t, p_b, ds_b):
        r, k = aligned(meta[GROUP + t], R), aligned(meta[BLOCK + t], KB)
        dk = dot(ds_b[...], q_s[pl.ds(r, R), :], NN)
        dv = dot(p_b[...], do_s[pl.ds(r, R), :], NN)
        dq = dot(ds_b[...], kv_s[pl.ds(k, KB), :HD], TN)
        acc[pl.ds(k, KB), :HD] += dk
        acc[pl.ds(k, KB), HD:] += dv
        dq_s[pl.ds(r, R), :] += dq

    ss, dps, ps, dss = (s0, s1), (dp0, dp1), (p0, p1), (ds0, ds1)
    products(meta, 0, q_s, do_s, kv_s, s0, dp0)
    products(meta, 1, q_s, do_s, kv_s, s1, dp1)
    weights(0, s0, dp0, p0, ds0)

    def step(t, v):
        a, b = v % 2, 1 - v % 2
        products(meta, t + 2, q_s, do_s, kv_s, ss[a], dps[a])
        weights(t + 1, ss[b], dps[b], ps[b], dss[b])
        sums(t, ps[a], dss[a])

    tiles_loop(meta[COUNT], step)
    for d in range(4):
        for half in range(2):
            place = meta[UNIT + 2 * d + half]
            t = slice(half * SPAN, (half + 1) * SPAN)
            for h in range(HEADS):
                got = dq_s[pl.ds(row_of(place, h), SPAN), :] * SCALE
                dqs[d][t, h * HD : (h + 1) * HD] = got.astype(dqs[d].dtype)
    for s in range(64):
        r = aligned(meta[IN + s], SPAN)
        t = slice((s % 2) * SPAN, (s % 2 + 1) * SPAN)
        second, first = s // 16, (s // 4) % 4
        ref, e = (dkv_other.at[first], second) if (s // 2) % 2 else (dkvs[second], first)
        ref[e, t, :HD] = (acc[pl.ds(r, SPAN), :HD] * SCALE).astype(jnp.bfloat16)
        ref[e, t, HD:] = acc[pl.ds(r, SPAN), HD:].astype(jnp.bfloat16)


VM = pl.BlockSpec(memory_space=pltpu.VMEM)
SM = pl.BlockSpec(memory_space=pltpu.SMEM)
PARAMS = pltpu.CompilerParams(vmem_limit_bytes=48 * 2**20)
COPIES = [
    pltpu.VMEM(((GROUPS + 1) * R, HD), jnp.bfloat16),
    pltpu.VMEM(((GROUPS + 1) * R, HD), jnp.bfloat16),
    pltpu.VMEM((KEYS, 2 * HD), jnp.bfloat16),
] + [pltpu.VMEM((KB, R), jnp.float32)] * 4


def pack_kernel(q, do, k, v, qd, kv, sem):
    copies = [
        pltpu.make_async_copy(a, b, sem.at[i])
        for i, (a, b) in enumerate(
            (
                (q, qd.at[:, :WIDE]),
                (do, qd.at[:, WIDE:]),
                (k, kv.at[:, :HD]),
                (v, kv.at[:, HD:]),
            )
        )
    ]
    for c in copies:
        c.start()
    for c in copies:
        c.wait()


def pack(queries, grad_out, keys, values):
    return pl.pallas_call(
        pack_kernel,
        out_shape=(
            jax.ShapeDtypeStruct((2 * SPAN, 2 * WIDE), jnp.bfloat16),
            jax.ShapeDtypeStruct((2 * SPAN, 2 * HD), jnp.bfloat16),
        ),
        in_specs=[pl.BlockSpec(memory_space=pltpu.HBM)] * 4,
        out_specs=(VM, VM),
        scratch_shapes=[pltpu.SemaphoreType.DMA((4,))],
        compiler_params=pltpu.CompilerParams(vmem_limit_bytes=60 * 2**20),
        name="pack",
    )(queries, grad_out, keys, values)


def stats(meta, lim, arrays):
    return pl.pallas_call(
        stats_kernel,
        out_shape=jax.ShapeDtypeStruct((2, 16, R), jnp.float32),
        in_specs=[SM] + [VM] * 9,
        out_specs=VM,
        scratch_shapes=COPIES + [pltpu.VMEM((GROUPS + 1, 8, R), jnp.float32)] * 3,
        compiler_params=PARAMS,
        name="stats",
    )(meta, lim, *arrays)


def grads(meta, lim, sts, arrays):
    dq = [jax.ShapeDtypeStruct((2 * SPAN, WIDE), t) for t in (jnp.float32,) + (jnp.bfloat16,) * 3]
    dkv = [jax.ShapeDtypeStruct((4, 2 * SPAN, 2 * HD), jnp.bfloat16)] * 4
    dkv += [jax.ShapeDtypeStruct((4, 4, 2 * SPAN, 2 * HD), jnp.bfloat16)]
    return pl.pallas_call(
        grads_kernel,
        out_shape=dq + dkv,
        in_specs=[SM] + [VM] * 11,
        out_specs=[VM] * 9,
        scratch_shapes=COPIES
        + [
            pltpu.VMEM((KEYS, 2 * HD), jnp.float32),
            pltpu.VMEM(((GROUPS + 1) * R, HD), jnp.float32),
        ]
        + [pltpu.VMEM((KB, R), jnp.bfloat16)] * 4
        + [pltpu.VMEM((16, R), jnp.float32)] * 2,
        compiler_params=PARAMS,
        name="grads",
    )(meta, lim, *sts, *arrays)


def permute(a, move):
    pairs = []
    for i in range(128):
        y, zl, core, zh, x = (int(c) for c in np.unravel_index(i, SIZES))
        y, z, core, x = (c % n for c, n in zip(move(y, 2 * zh + zl, core, x), (4, 4, 2, 4)))
        pairs.append((i, int(np.ravel_multi_index((y, z % 2, core, z // 2, x), SIZES))))
    return lax.ppermute(a, AXES, pairs)


def x_shift(a, step):
    return permute(a, lambda y, z, core, x: (y, z, core, x + step))


def first_shift(a, step):
    return permute(a, lambda y, z, core, x: (y, z + step, core, x) if core else (y + step, z, core, x))


def second_shift(a, step):
    return permute(a, lambda y, z, core, x: (y + step, z, core, x) if core else (y, z + step, core, x))


def core_swap(a):
    return permute(a, lambda y, z, core, x: (y, z, 1 - core, x))


def plan(span_slot):
    i32 = jnp.int32
    y, zl, core, zh, x = (lax.axis_index(a) for a in AXES)
    z = 2 * zh + zl
    grid = span_slot.reshape(*SIZES, 2)
    own_x = jnp.transpose(lax.dynamic_index_in_dim(grid, x, 4, keepdims=False), (2, 0, 3, 1, 4))
    own_x = own_x.reshape(2, 4, 4, 2)
    by_y = jnp.stack([lax.dynamic_index_in_dim(own_x, (y - r) % 4, 1, keepdims=False) for r in STEPS], 1)
    by_yz = jnp.stack([lax.dynamic_index_in_dim(by_y, (z - r) % 4, 2, keepdims=False) for r in STEPS], 2)
    mine = jnp.where(core == 0, jnp.transpose(by_yz, (2, 1, 0, 3)), jnp.transpose(by_yz[::-1], (1, 2, 0, 3)))
    arrived = mine.reshape(64)
    ring = grid[y, zl, core, zh]
    queries = jnp.concatenate([ring[(x - r) % 4] for r in STEPS])

    def rank(a, among):
        return jnp.sum((among[None, :] < a[:, None]).astype(i32), axis=1)

    place = rank(queries, queries)
    hit = (place[None, :] == jnp.arange(8)[:, None]).astype(i32)
    spans = jnp.sum(hit * queries[None, :], axis=1)
    below = rank(spans, arrived)
    own = jnp.any(arrived[None, :] == spans[:, None], axis=1).astype(i32)
    token = jnp.tile(jnp.arange(SPAN, dtype=i32), 2)
    seen = below[:, None] * SPAN + own[:, None] * (token[None, :] + 1)
    a, b = seen[0::2], seen[1::2]
    lim = jnp.stack([a, a, a, b, b, b], axis=1).reshape(GROUPS, R)
    lim = jnp.concatenate([lim, jnp.zeros((4, R), i32)])
    tiles = ((below + own) * SPAN + KB - 1) // KB
    each = jnp.stack([tiles[0::2], tiles[1::2], tiles[1::2]], axis=1).reshape(GROUPS)
    end = jnp.sum(jnp.tril(jnp.ones((GROUPS, GROUPS), i32)) * each[None, :], axis=1)
    t = jnp.arange(LIST, dtype=i32)
    past = (t[:, None] >= end[None, :]).astype(i32)
    group = jnp.sum(past, axis=1)
    block = jnp.where(group < GROUPS, t - jnp.sum(past * each[None, :], axis=1), 0)
    meta = [rank(arrived, arrived), place, end[-1:], group, block]
    return jnp.concatenate(meta).astype(i32), lim


def local(queries, keys, values, grad_out, span_slot):
    meta, lim = plan(span_slot)
    qd, kv = pack(queries, grad_out, keys, values)
    qds = [qd] + [x_shift(qd, r) for r in STEPS[1:]]
    kv = jnp.stack([kv, core_swap(kv)])[None]
    kv = jnp.concatenate([kv] + [first_shift(kv, r) for r in STEPS[1:]], axis=0)
    kvs = [kv] + [second_shift(kv, r) for r in STEPS[1:]]
    arrays = qds + kvs

    part = stats(meta, lim, arrays)
    got = permute(part, lambda y, z, core, x: (y, z, core, x ^ 1))
    part = jnp.stack(merged(part[0], part[1], got[0], got[1]))
    got = permute(part, lambda y, z, core, x: (y, z, core, x ^ 2))
    results = grads(meta, lim, (part, got), arrays)
    dqs, dkv, dkv_other = results[:4], results[4:8], results[8]

    def total(*parts):
        out = parts[0].astype(jnp.float32)
        for part in parts[1:]:
            out = out + part.astype(jnp.float32)
        return out

    dq = total(dqs[0], *[x_shift(a, -r) for r, a in zip(STEPS[1:], dqs[1:])])
    other = core_swap(dkv_other)
    pairs = [total(a, other[i]).astype(jnp.bfloat16) for i, a in enumerate(dkv)]
    some = total(pairs[0], *[second_shift(a, -r) for r, a in zip(STEPS[1:], pairs[1:])])
    sent = [first_shift(some[i].astype(jnp.bfloat16), -r) for i, r in ((1, 1), (2, 3), (3, 2))]
    summed = total(some[0], *sent)
    return (
        dq.astype(jnp.bfloat16),
        summed[:, :HD].astype(jnp.bfloat16),
        summed[:, HD:].astype(jnp.bfloat16),
    )


def solution(mesh):
    fine = Mesh(mesh.devices.reshape(4, 2, 2, 2, 4), AXES)
    rows = P(AXES, None)
    return jax.shard_map(
        local,
        mesh=fine,
        in_specs=(rows, rows, rows, rows, P()),
        out_specs=(rows, rows, rows),
        check_vma=False,
    )
```

```python
import functools
import math

import jax
import jax.numpy as jnp
import numpy as np
from jax import lax
from jax.experimental import pallas as pl
from jax.experimental.pallas import tpu as pltpu
from jax.sharding import Mesh, PartitionSpec as P

AXES = ("y", "zl", "core", "zh", "x")
SIZES = (4, 2, 2, 2, 4)
STEPS = (0, 1, 3, 2)
NEG = -1e30
HD = 128
SCALE = 1.0 / math.sqrt(HD)
C2 = math.log2(math.e) * SCALE
SPAN = 64
HEADS = 6
WIDE = HEADS * HD
KEYS = 4096
KB = 256
R = 256
GROUPS = 12
UNROLL = 8
LIST = 136
IN = 0
ALL, NEAR, FAR = range(3)
UNIT, CANON, COUNT, GROUP = 0, 8, 16, 17
BLOCK = GROUP + LIST
SIZE = BLOCK + LIST


def of(which):
    return 64 + which * SIZE


NT = (((1,), (1,)), ((), ()))
NN = (((1,), (0,)), ((), ()))
TN = (((0,), (0,)), ((), ()))


def dot(a, b, dims):
    return lax.dot_general(a, b, dims, preferred_element_type=jnp.float32)


def aligned(i, n):
    return pl.multiple_of(i * n, n)


def tree(op, xs):
    acc = list(xs[:4])
    for i, x in enumerate(xs[4:]):
        acc[i % 4] = op(acc[i % 4], x)
    return op(op(acc[0], acc[1]), op(acc[2], acc[3]))


def merged(lse, delta, lse_b, delta_b):
    top = jnp.maximum(lse, lse_b)
    w, w_b = jnp.exp2(lse - top), jnp.exp2(lse_b - top)
    total = w + w_b
    return top + jnp.log2(total), (w * delta + w_b * delta_b) / total


def tiles_loop(count, step):
    def many(i, carry):
        for v in range(UNROLL):
            step(i * UNROLL + v, v)
        return carry

    def few(i, carry):
        for v in range(2):
            step(i * 2 + v, v)
        return carry

    bodies = count // UNROLL
    lax.fori_loop(0, bodies, many, 0)
    lax.fori_loop(bodies * (UNROLL // 2), (count + 1) // 2, few, 0)


def load_sorted(meta, kvs, kv_s):
    for s in range(64):
        r = aligned(meta[IN + s], SPAN)
        t = slice((s % 2) * SPAN, (s % 2 + 1) * SPAN)
        kv_s[pl.ds(r, SPAN), :] = kvs[s // 8][(s // 2) % 4, t, :]


def row_of(place, h):
    odd = place % 2
    inner = odd * 512 + h * SPAN if h < 4 else R + odd * 128 + (h - 4) * SPAN
    return pl.multiple_of((place // 2) * 768 + inner, SPAN)


def load_rows(meta, base, qds, q_s, do_s, first=0):
    for d, ref in enumerate(qds):
        for half in range(2):
            place = meta[base + UNIT + 2 * (first + d) + half]
            t = slice(half * SPAN, (half + 1) * SPAN)
            for h in range(HEADS):
                r = row_of(place, h)
                q_s[pl.ds(r, SPAN), :] = ref[t, h * HD : (h + 1) * HD]
                do_s[pl.ds(r, SPAN), :] = ref[t, WIDE + h * HD : WIDE + (h + 1) * HD]
    rows = 3 * R * len(qds)
    q_s[rows : rows + R, :] = jnp.zeros((R, HD), q_s.dtype)
    do_s[rows : rows + R, :] = jnp.zeros((R, HD), do_s.dtype)


def products(meta, base, t, q_s, do_s, kv_s, s_b, dp_b):
    r, k = aligned(meta[base + GROUP + t], R), aligned(meta[base + BLOCK + t], KB)
    s_b[...] = dot(kv_s[pl.ds(k, KB), :HD], q_s[pl.ds(r, R), :], NT)
    dp_b[...] = dot(kv_s[pl.ds(k, KB), HD:], do_s[pl.ds(r, R), :], NT)


HALVES = ((0, 1), (2, 5), (3, 4))


def stats_kernel(which, devices, meta, lim, *refs):
    qds, kvs = refs[:devices], refs[devices : devices + 8]
    rest = refs[devices + 8 :]
    if which == FAR:
        before, rest = rest[0], rest[1:]
    out, q_s, do_s, kv_s, s0, s1, dp0, dp1, m_s, l_s, d_s = rest
    base, groups = of(which), 3 * devices
    load_sorted(meta, kvs, kv_s)
    load_rows(meta, base, qds, q_s, do_s, first=3 if which == FAR else 0)
    m_s[...] = jnp.full_like(m_s, NEG)
    l_s[...] = jnp.zeros_like(l_s)
    d_s[...] = jnp.zeros_like(d_s)
    iota = lax.broadcasted_iota(jnp.int32, (KB, R), 0)

    def online(t, s_b, dp_b):
        g = meta[base + GROUP + t]
        limit = lim[which, pl.ds(g, 1), :] - meta[base + BLOCK + t] * KB
        rows = [slice(8 * i, 8 * i + 8) for i in range(KB // 8)]
        s = [jnp.where(iota[r] < limit, s_b[r, :] * C2, NEG) for r in rows]
        m = m_s[g]
        top = jnp.maximum(m, tree(jnp.maximum, s))
        a = jnp.exp2(m - top)
        e = [jnp.exp2(x - top) for x in s]
        m_s[g] = top
        l_s[g] = l_s[g] * a + tree(jnp.add, e)
        d_s[g] = d_s[g] * a + tree(jnp.add, [x * dp_b[r, :] for r, x in zip(rows, e)])

    ss, dps = (s0, s1), (dp0, dp1)
    products(meta, base, 0, q_s, do_s, kv_s, s0, dp0)

    def step(t, v):
        products(meta, base, t + 1, q_s, do_s, kv_s, ss[(v + 1) % 2], dps[(v + 1) % 2])
        online(t, ss[v % 2], dps[v % 2])

    tiles_loop(meta[base + COUNT], step)
    out[...] = before[...] if which == FAR else jnp.zeros_like(out)
    for g in range(groups):
        m = m_s[g]
        live = jnp.where(m > 0.5 * NEG, 1.0, 0.0)
        top = jnp.max(m, axis=0, keepdims=True)
        a = jnp.exp2(m - top) * live
        ll = jnp.sum(l_s[g] * a, axis=0, keepdims=True)
        dd = jnp.sum(d_s[g] * a, axis=0, keepdims=True)
        safe = jnp.where(ll > 0, ll, 1.0)
        lse = jnp.where(ll > 0, top + jnp.log2(safe), NEG)
        for half in range(2):
            place, pair = divmod(HALVES[g % 3][half], 3)
            row = meta[base + CANON + g // 3 * 2 + place] * 3 + pair
            at = slice(half * 128, half * 128 + 128)
            out[0, pl.ds(row, 1), :] = lse[:, at]
            out[1, pl.ds(row, 1), :] = (dd / safe)[:, at]


def grads_kernel(meta, lim, st0, st1, *refs):
    qds, kvs = refs[:4], refs[4:12]
    dqs, dkvs, dkv_other = refs[12:16], refs[16:20], refs[20]
    q_s, do_s, kv_s, s0, s1, dp0, dp1, acc, dq_s, p0, p1, ds0, ds1, lse, delta = refs[21:]
    load_sorted(meta, kvs, kv_s)
    base = of(ALL)
    load_rows(meta, base, qds, q_s, do_s)
    acc[...] = jnp.zeros_like(acc)
    dq_s[...] = jnp.zeros_like(dq_s)
    all_lse, all_delta = merged(st0[0], st0[1], st1[0], st1[1])
    lse[...] = jnp.zeros_like(lse)
    delta[...] = jnp.zeros_like(delta)
    for g in range(GROUPS):
        for half in range(2):
            row = g // 3 * 6 + HALVES[g % 3][half]
            at = slice(half * 128, half * 128 + 128)
            lse[g : g + 1, at] = all_lse[row : row + 1]
            delta[g : g + 1, at] = all_delta[row : row + 1]
    iota = lax.broadcasted_iota(jnp.int32, (KB, R), 0)

    def weights(t, s_b, dp_b, p_b, ds_b):
        g = meta[base + GROUP + t]
        limit = lim[ALL, pl.ds(g, 1), :] - meta[base + BLOCK + t] * KB
        p = jnp.where(iota < limit, jnp.exp2(s_b[...] * C2 - lse[pl.ds(g, 1), :]), 0.0)
        p_b[...] = p.astype(jnp.bfloat16)
        ds_b[...] = (p * (dp_b[...] - delta[pl.ds(g, 1), :])).astype(jnp.bfloat16)

    def sums(t, p_b, ds_b):
        r, k = aligned(meta[base + GROUP + t], R), aligned(meta[base + BLOCK + t], KB)
        dk = dot(ds_b[...], q_s[pl.ds(r, R), :], NN)
        dv = dot(p_b[...], do_s[pl.ds(r, R), :], NN)
        dq = dot(ds_b[...], kv_s[pl.ds(k, KB), :HD], TN)
        acc[pl.ds(k, KB), :HD] += dk
        acc[pl.ds(k, KB), HD:] += dv
        dq_s[pl.ds(r, R), :] += dq

    ss, dps, ps, dss = (s0, s1), (dp0, dp1), (p0, p1), (ds0, ds1)
    products(meta, base, 0, q_s, do_s, kv_s, s0, dp0)
    products(meta, base, 1, q_s, do_s, kv_s, s1, dp1)
    weights(0, s0, dp0, p0, ds0)

    def step(t, v):
        a, b = v % 2, 1 - v % 2
        products(meta, base, t + 2, q_s, do_s, kv_s, ss[a], dps[a])
        weights(t + 1, ss[b], dps[b], ps[b], dss[b])
        sums(t, ps[a], dss[a])

    tiles_loop(meta[base + COUNT], step)
    for d in range(4):
        for half in range(2):
            place = meta[base + UNIT + 2 * d + half]
            t = slice(half * SPAN, (half + 1) * SPAN)
            for h in range(HEADS):
                got = dq_s[pl.ds(row_of(place, h), SPAN), :] * SCALE
                dqs[d][t, h * HD : (h + 1) * HD] = got.astype(dqs[d].dtype)
    for s in range(64):
        r = aligned(meta[IN + s], SPAN)
        t = slice((s % 2) * SPAN, (s % 2 + 1) * SPAN)
        e = (s // 2) % 4
        ref = dkvs[s // 8] if s < 32 else dkv_other.at[s // 8 - 4]
        ref[e, t, :HD] = (acc[pl.ds(r, SPAN), :HD] * SCALE).astype(jnp.bfloat16)
        ref[e, t, HD:] = acc[pl.ds(r, SPAN), HD:].astype(jnp.bfloat16)


VM = pl.BlockSpec(memory_space=pltpu.VMEM)
SM = pl.BlockSpec(memory_space=pltpu.SMEM)
PARAMS = pltpu.CompilerParams(vmem_limit_bytes=48 * 2**20)
COPIES = [
    pltpu.VMEM(((GROUPS + 1) * R, HD), jnp.bfloat16),
    pltpu.VMEM(((GROUPS + 1) * R, HD), jnp.bfloat16),
    pltpu.VMEM((KEYS, 2 * HD), jnp.bfloat16),
] + [pltpu.VMEM((KB, R), jnp.float32)] * 4


def stats(which, meta, lim, qds, kvs, *before):
    n = len(qds)
    return pl.pallas_call(
        functools.partial(stats_kernel, which, n),
        out_shape=jax.ShapeDtypeStruct((2, 24, 128), jnp.float32),
        in_specs=[SM] + [VM] * (1 + n + 8 + len(before)),
        out_specs=VM,
        scratch_shapes=COPIES + [pltpu.VMEM((3 * n + 1, 8, R), jnp.float32)] * 3,
        compiler_params=PARAMS,
        cost_estimate=pl.CostEstimate(flops=n * 1_600_000_000, bytes_accessed=4_000_000, transcendentals=0),
        name="stats_near" if which == NEAR else "stats_far",
    )(meta, lim, *qds, *kvs, *before)


def grads(meta, lim, sts, arrays):
    dq = [jax.ShapeDtypeStruct((2 * SPAN, WIDE), t) for t in (jnp.float32,) + (jnp.bfloat16,) * 3]
    dkv = [jax.ShapeDtypeStruct((4, 2 * SPAN, 2 * HD), jnp.bfloat16)] * 4
    dkv += [jax.ShapeDtypeStruct((4, 4, 2 * SPAN, 2 * HD), jnp.bfloat16)]
    return pl.pallas_call(
        grads_kernel,
        out_shape=dq + dkv,
        in_specs=[SM] + [VM] * 15,
        out_specs=[VM] * 9,
        scratch_shapes=COPIES
        + [
            pltpu.VMEM((KEYS, 2 * HD), jnp.float32),
            pltpu.VMEM(((GROUPS + 1) * R, HD), jnp.float32),
        ]
        + [pltpu.VMEM((KB, R), jnp.bfloat16)] * 4
        + [pltpu.VMEM((16, R), jnp.float32)] * 2,
        compiler_params=PARAMS,
        name="grads",
    )(meta, lim, *sts, *arrays)


def permute(a, move):
    pairs = []
    for i in range(128):
        y, zl, core, zh, x = (int(c) for c in np.unravel_index(i, SIZES))
        y, z, core, x = (c % n for c, n in zip(move(y, 2 * zh + zl, core, x), (4, 4, 2, 4)))
        pairs.append((i, int(np.ravel_multi_index((y, z % 2, core, z // 2, x), SIZES))))
    return lax.ppermute(a, AXES, pairs)


def x_shift(a, step):
    return permute(a, lambda y, z, core, x: (y, z, core, x + step))


def first_shift(a, step):
    return permute(a, lambda y, z, core, x: (y, z + step, core, x) if core else (y + step, z, core, x))


def second_shift(a, step):
    return permute(a, lambda y, z, core, x: (y + step, z, core, x) if core else (y, z + step, core, x))


def core_swap(a):
    return permute(a, lambda y, z, core, x: (y, z, 1 - core, x))


def plan(span_slot):
    i32 = jnp.int32
    y, zl, core, zh, x = (lax.axis_index(a) for a in AXES)
    z = 2 * zh + zl
    grid = span_slot.reshape(*SIZES, 2)
    own_x = jnp.transpose(lax.dynamic_index_in_dim(grid, x, 4, keepdims=False), (2, 0, 3, 1, 4))
    own_x = own_x.reshape(2, 4, 4, 2)
    by_y = jnp.stack([lax.dynamic_index_in_dim(own_x, (y - r) % 4, 1, keepdims=False) for r in STEPS], 1)
    by_yz = jnp.stack([lax.dynamic_index_in_dim(by_y, (z - r) % 4, 2, keepdims=False) for r in STEPS], 2)
    of_core = jnp.stack([jnp.transpose(by_yz[0], (1, 0, 2)), by_yz[1]])
    arrived = jnp.where(core == 0, of_core, of_core[::-1]).reshape(64)
    ring = grid[y, zl, core, zh]
    queries = jnp.concatenate([ring[(x - r) % 4] for r in STEPS])

    def rank(a, among):
        return jnp.sum((among[None, :] < a[:, None]).astype(i32), axis=1)

    place = rank(queries, queries)
    eight = jnp.arange(8, dtype=i32)
    hit = (place[None, :] == eight[:, None]).astype(i32)
    spans = jnp.sum(hit * queries[None, :], axis=1)
    below = rank(spans, arrived)
    own = jnp.any(arrived[None, :] == spans[:, None], axis=1).astype(i32)
    far = jnp.sum(hit[:, 6:], axis=1)
    before = jnp.sum(jnp.tril(jnp.ones((8, 8), i32), -1) * far[None, :], axis=1)
    order = jnp.stack([eight, jnp.where(far == 0, eight - before, 9), jnp.where(far == 1, before, 9)])
    taken = (order[:, None, :] == eight[None, :, None]).astype(i32)
    canon = jnp.sum(taken * eight, axis=2)
    units = jnp.sum(order[:, None, :] * hit.T[None], axis=2)
    token = jnp.tile(jnp.arange(SPAN, dtype=i32), 2)
    seen = below[:, None] * SPAN + own[:, None] * (token[None, :] + 1)
    seen = jnp.sum(taken[:, :, :, None] * seen[None, None], axis=2)
    a, b = seen[:, 0::2], seen[:, 1::2]
    lim = jnp.stack([a, a, a, b, b, b], axis=2).reshape(3, GROUPS, R)
    lim = jnp.concatenate([lim, jnp.zeros((3, 4, R), i32)], axis=1)
    tiles = ((below + own) * SPAN + KB - 1) // KB
    tiles = jnp.sum(taken * tiles, axis=2)
    each = jnp.stack([tiles[:, 0::2], tiles[:, 1::2], tiles[:, 1::2]], axis=2).reshape(3, GROUPS)
    end = jnp.sum(jnp.tril(jnp.ones((GROUPS, GROUPS), i32)) * each[:, None, :], axis=2)
    t = jnp.arange(LIST, dtype=i32)
    past = (t[None, :, None] >= end[:, None, :]).astype(i32)
    group = jnp.minimum(jnp.sum(past, axis=2), jnp.array([[12], [9], [3]], i32))
    block = jnp.where(t[None] < end[:, -1:], t[None] - jnp.sum(past * each[:, None, :], axis=2), 0)
    lists = jnp.concatenate([units, canon, end[:, -1:], group, block], axis=1)
    return jnp.concatenate([rank(arrived, arrived), lists.reshape(-1)]).astype(i32), lim


def local(queries, keys, values, grad_out, span_slot):
    kv = jnp.concatenate([keys, values], axis=1)[None]
    kv = jnp.concatenate([kv] + [first_shift(kv, r) for r in STEPS[1:]], axis=0)
    kvs = [kv] + [second_shift(kv, r) for r in STEPS[1:]]
    qd = jnp.concatenate([queries, grad_out], axis=1)
    near = [qd, x_shift(qd, 1), x_shift(qd, 3)]
    near[1], near[2], later = lax.optimization_barrier((near[1], near[2], qd))
    far = x_shift(later, 2)
    kvs[0], kvs[1], span_slot = lax.optimization_barrier((kvs[0], kvs[1], span_slot))
    meta, lim = plan(span_slot)
    kvs = kvs + [core_swap(a) for a in kvs]
    arrays = near + [far] + kvs

    part = stats(NEAR, meta, lim, near, kvs)
    part = stats(FAR, meta, lim, [far], kvs, part)
    got = permute(part, lambda y, z, core, x: (y, z, core, x ^ 1))
    part = jnp.stack(merged(part[0], part[1], got[0], got[1]))
    got = permute(part, lambda y, z, core, x: (y, z, core, x ^ 2))
    results = grads(meta, lim, (part, got), arrays)
    dqs, dkv, dkv_other = results[:4], results[4:8], results[8]

    def total(*parts):
        out = parts[0].astype(jnp.float32)
        for part in parts[1:]:
            out = out + part.astype(jnp.float32)
        return out

    dq = total(dqs[0], *[x_shift(a, -r) for r, a in zip(STEPS[1:], dqs[1:])])
    other = core_swap(dkv_other)
    pairs = [total(a, other[i]).astype(jnp.bfloat16) for i, a in enumerate(dkv)]
    some = total(pairs[0], *[second_shift(a, -r) for r, a in zip(STEPS[1:], pairs[1:])])
    sent = [first_shift(some[i].astype(jnp.bfloat16), -r) for i, r in ((1, 1), (2, 3), (3, 2))]
    summed = total(some[0], *sent)
    return (
        dq.astype(jnp.bfloat16),
        summed[:, :HD].astype(jnp.bfloat16),
        summed[:, HD:].astype(jnp.bfloat16),
    )


def solution(mesh):
    fine = Mesh(mesh.devices.reshape(4, 2, 2, 2, 4), AXES)
    rows = P(AXES, None)
    return jax.shard_map(
        local,
        mesh=fine,
        in_specs=(rows, rows, rows, rows, P()),
        out_specs=(rows, rows, rows),
        check_vma=False,
    )
```

```python
import functools
import math

import jax
import jax.numpy as jnp
import numpy as np
from jax import lax
from jax.experimental import pallas as pl
from jax.experimental.pallas import tpu as pltpu
from jax.sharding import Mesh, PartitionSpec as P

AXES = ("y", "zl", "core", "zh", "x")
SIZES = (4, 2, 2, 2, 4)
STEPS = (0, 1, 3, 2)
NEG = -1e30
HD = 128
SCALE = 1.0 / math.sqrt(HD)
C2 = math.log2(math.e) * SCALE
SPAN = 64
HEADS = 6
WIDE = HEADS * HD
KEYS = 2048
KB = 256
R = 256
UNITS = 16
GROUPS = 24
UNROLL = 8
LIST = 136
IN = 0
ALL, NEAR, OTHER, FAR = range(4)
IDS = (tuple(range(8)), (0, 1, 2), (4, 5, 6), (3, 7))
NAMES = ("", "stats_near", "stats_other", "stats_far")
UNIT, CANON, COUNT, GROUP = 0, UNITS, 2 * UNITS, 2 * UNITS + 1
BLOCK = GROUP + LIST
SIZE = BLOCK + LIST


def of(which):
    return 32 + which * SIZE


NT = (((1,), (1,)), ((), ()))
NN = (((1,), (0,)), ((), ()))
TN = (((0,), (0,)), ((), ()))


def dot(a, b, dims):
    return lax.dot_general(a, b, dims, preferred_element_type=jnp.float32)


def aligned(i, n):
    return pl.multiple_of(i * n, n)


def tree(op, xs):
    acc = list(xs[:4])
    for i, x in enumerate(xs[4:]):
        acc[i % 4] = op(acc[i % 4], x)
    return op(op(acc[0], acc[1]), op(acc[2], acc[3]))


def merged(lse, delta, lse_b, delta_b):
    top = jnp.maximum(lse, lse_b)
    w, w_b = jnp.exp2(lse - top), jnp.exp2(lse_b - top)
    total = w + w_b
    return top + jnp.log2(total), (w * delta + w_b * delta_b) / total


def tiles_loop(count, step):
    def many(i, carry):
        for v in range(UNROLL):
            step(i * UNROLL + v, v)
        return carry

    def few(i, carry):
        for v in range(2):
            step(i * 2 + v, v)
        return carry

    bodies = count // UNROLL
    lax.fori_loop(0, bodies, many, 0)
    lax.fori_loop(bodies * (UNROLL // 2), (count + 1) // 2, few, 0)


def load_sorted(meta, kvs, kv_s):
    for s in range(32):
        r = aligned(meta[IN + s], SPAN)
        t = slice((s % 2) * SPAN, (s % 2 + 1) * SPAN)
        kv_s[pl.ds(r, SPAN), :] = kvs[s // 8][(s // 2) % 4, t, :]


def row_of(place, h):
    odd = place % 2
    inner = odd * 512 + h * SPAN if h < 4 else R + odd * 128 + (h - 4) * SPAN
    return pl.multiple_of((place // 2) * 768 + inner, SPAN)


def load_rows(meta, base, ids, qds, q_s, do_s):
    for d, ref in zip(ids, qds):
        for half in range(2):
            place = meta[base + UNIT + 2 * d + half]
            t = slice(half * SPAN, (half + 1) * SPAN)
            for h in range(HEADS):
                r = row_of(place, h)
                q_s[pl.ds(r, SPAN), :] = ref[t, h * HD : (h + 1) * HD]
                do_s[pl.ds(r, SPAN), :] = ref[t, WIDE + h * HD : WIDE + (h + 1) * HD]
    rows = 3 * R * len(qds)
    q_s[rows : rows + R, :] = jnp.zeros((R, HD), q_s.dtype)
    do_s[rows : rows + R, :] = jnp.zeros((R, HD), do_s.dtype)


def products(meta, base, t, q_s, do_s, kv_s, s_b, dp_b):
    r, k = aligned(meta[base + GROUP + t], R), aligned(meta[base + BLOCK + t], KB)
    s_b[...] = dot(kv_s[pl.ds(k, KB), :HD], q_s[pl.ds(r, R), :], NT)
    dp_b[...] = dot(kv_s[pl.ds(k, KB), HD:], do_s[pl.ds(r, R), :], NT)


HALVES = ((0, 1), (2, 5), (3, 4))


def stats_kernel(which, meta, lim, *refs):
    ids = IDS[which]
    devices = len(ids)
    qds, kvs = refs[:devices], refs[devices : devices + 4]
    rest = refs[devices + 4 :]
    if which != NEAR:
        before, rest = rest[0], rest[1:]
    out, q_s, do_s, kv_s, s0, s1, dp0, dp1, m_s, l_s, d_s = rest
    base, groups = of(which), 3 * devices
    load_sorted(meta, kvs, kv_s)
    load_rows(meta, base, ids, qds, q_s, do_s)
    m_s[...] = jnp.full_like(m_s, NEG)
    l_s[...] = jnp.zeros_like(l_s)
    d_s[...] = jnp.zeros_like(d_s)
    iota = lax.broadcasted_iota(jnp.int32, (KB, R), 0)

    def online(t, s_b, dp_b):
        g = meta[base + GROUP + t]
        limit = lim[which, pl.ds(g, 1), :] - meta[base + BLOCK + t] * KB
        rows = [slice(8 * i, 8 * i + 8) for i in range(KB // 8)]
        s = [jnp.where(iota[r] < limit, s_b[r, :] * C2, NEG) for r in rows]
        m = m_s[g]
        top = jnp.maximum(m, tree(jnp.maximum, s))
        a = jnp.exp2(m - top)
        e = [jnp.exp2(x - top) for x in s]
        m_s[g] = top
        l_s[g] = l_s[g] * a + tree(jnp.add, e)
        d_s[g] = d_s[g] * a + tree(jnp.add, [x * dp_b[r, :] for r, x in zip(rows, e)])

    ss, dps = (s0, s1), (dp0, dp1)
    products(meta, base, 0, q_s, do_s, kv_s, s0, dp0)

    def step(t, v):
        products(meta, base, t + 1, q_s, do_s, kv_s, ss[(v + 1) % 2], dps[(v + 1) % 2])
        online(t, ss[v % 2], dps[v % 2])

    tiles_loop(meta[base + COUNT], step)
    out[...] = before[...] if which != NEAR else jnp.zeros_like(out)
    for g in range(groups):
        m = m_s[g]
        live = jnp.where(m > 0.5 * NEG, 1.0, 0.0)
        top = jnp.max(m, axis=0, keepdims=True)
        a = jnp.exp2(m - top) * live
        ll = jnp.sum(l_s[g] * a, axis=0, keepdims=True)
        dd = jnp.sum(d_s[g] * a, axis=0, keepdims=True)
        safe = jnp.where(ll > 0, ll, 1.0)
        lse = jnp.where(ll > 0, top + jnp.log2(safe), NEG)
        for half in range(2):
            place, pair = divmod(HALVES[g % 3][half], 3)
            row = meta[base + CANON + g // 3 * 2 + place] * 3 + pair
            at = slice(half * 128, half * 128 + 128)
            out[0, pl.ds(row, 1), :] = lse[:, at]
            out[1, pl.ds(row, 1), :] = (dd / safe)[:, at]


def grads_kernel(meta, lim, st0, st1, *refs):
    qds, kvs = refs[:8], refs[8:12]
    dqs, dq_other, dkvs = refs[12:16], refs[16], refs[17:21]
    q_s, do_s, kv_s, s0, s1, dp0, dp1, acc, dq_s, p0, p1, ds0, ds1, lse, delta = refs[21:]
    load_sorted(meta, kvs, kv_s)
    base = of(ALL)
    load_rows(meta, base, IDS[ALL], qds, q_s, do_s)
    acc[...] = jnp.zeros_like(acc)
    dq_s[...] = jnp.zeros_like(dq_s)
    all_lse, all_delta = merged(st0[0], st0[1], st1[0], st1[1])
    lse[...] = jnp.zeros_like(lse)
    delta[...] = jnp.zeros_like(delta)
    for g in range(GROUPS):
        for half in range(2):
            row = g // 3 * 6 + HALVES[g % 3][half]
            at = slice(half * 128, half * 128 + 128)
            lse[g : g + 1, at] = all_lse[row : row + 1]
            delta[g : g + 1, at] = all_delta[row : row + 1]
    iota = lax.broadcasted_iota(jnp.int32, (KB, R), 0)

    def weights(t, s_b, dp_b, p_b, ds_b):
        g = meta[base + GROUP + t]
        limit = lim[ALL, pl.ds(g, 1), :] - meta[base + BLOCK + t] * KB
        p = jnp.where(iota < limit, jnp.exp2(s_b[...] * C2 - lse[pl.ds(g, 1), :]), 0.0)
        p_b[...] = p.astype(jnp.bfloat16)
        ds_b[...] = (p * (dp_b[...] - delta[pl.ds(g, 1), :])).astype(jnp.bfloat16)

    def sums(t, p_b, ds_b):
        r, k = aligned(meta[base + GROUP + t], R), aligned(meta[base + BLOCK + t], KB)
        dk = dot(ds_b[...], q_s[pl.ds(r, R), :], NN)
        dv = dot(p_b[...], do_s[pl.ds(r, R), :], NN)
        dq = dot(ds_b[...], kv_s[pl.ds(k, KB), :HD], TN)
        acc[pl.ds(k, KB), :HD] += dk
        acc[pl.ds(k, KB), HD:] += dv
        dq_s[pl.ds(r, R), :] += dq

    ss, dps, ps, dss = (s0, s1), (dp0, dp1), (p0, p1), (ds0, ds1)
    products(meta, base, 0, q_s, do_s, kv_s, s0, dp0)
    products(meta, base, 1, q_s, do_s, kv_s, s1, dp1)
    weights(0, s0, dp0, p0, ds0)

    def step(t, v):
        a, b = v % 2, 1 - v % 2
        products(meta, base, t + 2, q_s, do_s, kv_s, ss[a], dps[a])
        weights(t + 1, ss[b], dps[b], ps[b], dss[b])
        sums(t, ps[a], dss[a])

    tiles_loop(meta[base + COUNT], step)
    for d in range(8):
        ref = dqs[d] if d < 4 else dq_other.at[d - 4]
        for half in range(2):
            place = meta[base + UNIT + 2 * d + half]
            t = slice(half * SPAN, (half + 1) * SPAN)
            for h in range(HEADS):
                got = dq_s[pl.ds(row_of(place, h), SPAN), :] * SCALE
                ref[t, h * HD : (h + 1) * HD] = got.astype(ref.dtype)
    for s in range(32):
        r = aligned(meta[IN + s], SPAN)
        t = slice((s % 2) * SPAN, (s % 2 + 1) * SPAN)
        ref, e = dkvs[s // 8], (s // 2) % 4
        ref[e, t, :HD] = (acc[pl.ds(r, SPAN), :HD] * SCALE).astype(jnp.bfloat16)
        ref[e, t, HD:] = acc[pl.ds(r, SPAN), HD:].astype(jnp.bfloat16)


VM = pl.BlockSpec(memory_space=pltpu.VMEM)
SM = pl.BlockSpec(memory_space=pltpu.SMEM)
PARAMS = pltpu.CompilerParams(vmem_limit_bytes=48 * 2**20)
COPIES = [
    pltpu.VMEM(((GROUPS + 1) * R, HD), jnp.bfloat16),
    pltpu.VMEM(((GROUPS + 1) * R, HD), jnp.bfloat16),
    pltpu.VMEM((KEYS, 2 * HD), jnp.bfloat16),
] + [pltpu.VMEM((KB, R), jnp.float32)] * 4


def stats(which, meta, lim, qds, kvs, *before):
    n = len(IDS[which])
    return pl.pallas_call(
        functools.partial(stats_kernel, which),
        out_shape=jax.ShapeDtypeStruct((2, 3 * UNITS, 128), jnp.float32),
        in_specs=[SM] + [VM] * (1 + n + 4 + len(before)),
        out_specs=VM,
        scratch_shapes=COPIES + [pltpu.VMEM((3 * n + 1, 8, R), jnp.float32)] * 3,
        compiler_params=PARAMS,
        cost_estimate=pl.CostEstimate(flops=n * 800_000_000, bytes_accessed=4_000_000, transcendentals=0),
        name=NAMES[which],
    )(meta, lim, *qds, *kvs, *before)


def grads(meta, lim, sts, qds, kvs):
    dq = [jax.ShapeDtypeStruct((2 * SPAN, WIDE), jnp.float32)] * 4
    dq += [jax.ShapeDtypeStruct((4, 2 * SPAN, WIDE), jnp.bfloat16)]
    dkv = [jax.ShapeDtypeStruct((4, 2 * SPAN, 2 * HD), jnp.bfloat16)] * 4
    return pl.pallas_call(
        grads_kernel,
        out_shape=dq + dkv,
        in_specs=[SM] + [VM] * 15,
        out_specs=[VM] * 9,
        scratch_shapes=COPIES
        + [
            pltpu.VMEM((KEYS, 2 * HD), jnp.float32),
            pltpu.VMEM(((GROUPS + 1) * R, HD), jnp.float32),
        ]
        + [pltpu.VMEM((KB, R), jnp.bfloat16)] * 4
        + [pltpu.VMEM((32, R), jnp.float32)] * 2,
        compiler_params=PARAMS,
        name="grads",
    )(meta, lim, *sts, *qds, *kvs)


def permute(a, move):
    pairs = []
    for i in range(128):
        y, zl, core, zh, x = (int(c) for c in np.unravel_index(i, SIZES))
        y, z, core, x = (c % n for c, n in zip(move(y, 2 * zh + zl, core, x), (4, 4, 2, 4)))
        pairs.append((i, int(np.ravel_multi_index((y, z % 2, core, z // 2, x), SIZES))))
    return lax.ppermute(a, AXES, pairs)


def x_shift(a, step):
    return permute(a, lambda y, z, core, x: (y, z, core, x + step))


def first_shift(a, step):
    return permute(a, lambda y, z, core, x: (y, z + step, core, x) if core else (y + step, z, core, x))


def second_shift(a, step):
    return permute(a, lambda y, z, core, x: (y + step, z, core, x) if core else (y, z + step, core, x))


def core_swap(a):
    return permute(a, lambda y, z, core, x: (y, z, 1 - core, x))


def plan(span_slot):
    i32 = jnp.int32
    y, zl, core, zh, x = (lax.axis_index(a) for a in AXES)
    z = 2 * zh + zl
    i = jnp.arange(48, dtype=i32)
    is_key = i < 32
    low, high = (i // 2) % 4, (i // 8) % 4
    low, high = low ^ (low >> 1), high ^ (high >> 1)
    at_y = jnp.where(is_key, (y - jnp.where(core == 0, low, high)) % 4, y)
    at_z = jnp.where(is_key, (z - jnp.where(core == 0, high, low)) % 4, z)
    at_x = jnp.where(is_key, x, (x - low) % 4)
    at_core = jnp.where(is_key | (i < 40), core, 1 - core)
    slot = ((((at_y * 2 + at_z % 2) * 2 + at_core) * 2 + at_z // 2) * 4 + at_x) * 2 + i % 2
    spans = jnp.sum(jnp.where(slot[:, None] == jnp.arange(256)[None, :], span_slot[None, :], 0), axis=1)
    arrived, queries = spans[:32], spans[32:]

    def rank(a, among):
        return jnp.sum((among[None, :] < a[:, None]).astype(i32), axis=1)

    place = rank(queries, queries)
    every = jnp.arange(UNITS, dtype=i32)
    hit = (place[None, :] == every[:, None]).astype(i32)
    spans = jnp.sum(hit * queries[None, :], axis=1)
    below = rank(spans, arrived)
    own = jnp.any(arrived[None, :] == spans[:, None], axis=1).astype(i32)
    group = jnp.where((every // 2) % 4 == 3, FAR, jnp.where(every < 8, NEAR, OTHER))
    group = jnp.sum(hit * group, axis=1)
    members = (group[None, :] == jnp.arange(4)[:, None]) | (jnp.arange(4)[:, None] == ALL)
    lower = jnp.tril(jnp.ones((UNITS, UNITS), i32), -1)
    before = jnp.sum(lower[None] * members.astype(i32)[:, None, :], axis=2)
    order = jnp.where(members, before, 99)
    taken = (order[:, None, :] == every[None, :, None]).astype(i32)
    canon = jnp.sum(taken * every, axis=2)
    units = jnp.sum(order[:, None, :] * hit.T[None], axis=2)
    token = jnp.tile(jnp.arange(SPAN, dtype=i32), 2)
    count, diagonal = jnp.sum(taken * below, axis=2), jnp.sum(taken * own, axis=2)
    seen = count[:, :, None] * SPAN + diagonal[:, :, None] * (token + 1)
    a, b = seen[:, 0::2], seen[:, 1::2]
    lim = jnp.stack([a, a, a, b, b, b], axis=2).reshape(4, GROUPS, R)
    lim = jnp.concatenate([lim, jnp.zeros((4, 8, R), i32)], axis=1)
    tiles = ((count + diagonal) * SPAN + KB - 1) // KB
    each = jnp.stack([tiles[:, 0::2], tiles[:, 1::2], tiles[:, 1::2]], axis=2).reshape(4, GROUPS)
    end = jnp.sum(jnp.tril(jnp.ones((GROUPS, GROUPS), i32)) * each[:, None, :], axis=2)
    t = jnp.arange(LIST, dtype=i32)
    past = (t[None, :, None] >= end[:, None, :]).astype(i32)
    last = jnp.array([[3 * len(ids)] for ids in IDS], i32)
    group = jnp.minimum(jnp.sum(past, axis=2), last)
    block = jnp.where(t[None] < end[:, -1:], t[None] - jnp.sum(past * each[:, None, :], axis=2), 0)
    lists = jnp.concatenate([units, canon, end[:, -1:], group, block], axis=1)
    return jnp.concatenate([rank(arrived, arrived), lists.reshape(-1)]).astype(i32), lim


def local(queries, keys, values, grad_out, span_slot):
    kv = jnp.concatenate([keys, values], axis=1)[None]
    kv = jnp.concatenate([kv] + [first_shift(kv, r) for r in STEPS[1:]], axis=0)
    kvs = [kv] + [second_shift(kv, r) for r in STEPS[1:]]
    qd = jnp.concatenate([queries, grad_out], axis=1)
    near = [qd, x_shift(qd, 1), x_shift(qd, 3)]
    near[1], near[2], later = lax.optimization_barrier((near[1], near[2], qd))
    far = x_shift(later, 2)
    other = [core_swap(a) for a in near]
    kvs[1], span_slot = lax.optimization_barrier((kvs[1], span_slot))
    meta, lim = plan(span_slot)

    part = stats(NEAR, meta, lim, near, kvs)
    part, far = lax.optimization_barrier((part, far))
    far_other = core_swap(far)
    part = stats(OTHER, meta, lim, other, kvs, part)
    part = stats(FAR, meta, lim, [far, far_other], kvs, part)
    got = core_swap(part)
    part = jnp.stack(merged(part[0], part[1], got[0], got[1]))
    got = permute(part, lambda y, z, core, x: (y, z, core, x ^ 1))
    part = jnp.stack(merged(part[0], part[1], got[0], got[1]))
    got = permute(part, lambda y, z, core, x: (y, z, core, x ^ 2))
    results = grads(meta, lim, (part, got), near + [far] + other + [far_other], kvs)
    dqs, dq_other, dkv = results[:4], results[4], results[5:]

    def total(*parts):
        out = parts[0].astype(jnp.float32)
        for part in parts[1:]:
            out = out + part.astype(jnp.float32)
        return out

    swapped = core_swap(dq_other)
    first = [second_shift(a, -r) for r, a in zip(STEPS[1:3], dkv[1:3])]
    last, swapped = lax.optimization_barrier((dkv[3], swapped))
    some = total(dkv[0], *first, second_shift(last, -2))
    pairs = [total(a, swapped[i]) for i, a in enumerate(dqs)]
    back = [x_shift(a.astype(jnp.bfloat16), -r) for r, a in zip(STEPS[1:], pairs[1:])]
    some, back[0], back[1] = lax.optimization_barrier((some, back[0], back[1]))
    sent = [first_shift(some[i].astype(jnp.bfloat16), -r) for i, r in ((1, 1), (2, 3), (3, 2))]
    summed = total(some[0], *sent)
    dq = total(pairs[0], *back)
    return (
        dq.astype(jnp.bfloat16),
        summed[:, :HD].astype(jnp.bfloat16),
        summed[:, HD:].astype(jnp.bfloat16),
    )


def solution(mesh):
    fine = Mesh(mesh.devices.reshape(4, 2, 2, 2, 4), AXES)
    rows = P(AXES, None)
    return jax.shard_map(
        local,
        mesh=fine,
        in_specs=(rows, rows, rows, rows, P()),
        out_specs=(rows, rows, rows),
        check_vma=False,
    )
```

```python
import functools
import math

import jax
import jax.numpy as jnp
import numpy as np
from jax import lax
from jax.experimental import pallas as pl
from jax.experimental.pallas import tpu as pltpu
from jax.sharding import Mesh, PartitionSpec as P

AXES = ("y", "zl", "core", "zh", "x")
SIZES = (4, 2, 2, 2, 4)
STEPS = (0, 1, 3, 2)
NEG = -1e30
HD = 128
SCALE = 1.0 / math.sqrt(HD)
C2 = math.log2(math.e) * SCALE
SPAN = 64
HEADS = 6
WIDE = HEADS * HD
KEYS = 4096
KB = 256
R = 256
GROUPS = 12
MANY, FEW = 16, 8
LIST = 144
IN = 0
ALL, NEAR, FAR = range(3)
UNIT, CANON, FULL, COUNT, GROUP = 0, 8, 16, 17, 18
BLOCK = GROUP + LIST
SIZE = BLOCK + LIST


def of(which):
    return 64 + which * SIZE


NT = (((1,), (1,)), ((), ()))
NN = (((1,), (0,)), ((), ()))
TN = (((0,), (0,)), ((), ()))


def dot(a, b, dims):
    return lax.dot_general(a, b, dims, preferred_element_type=jnp.float32)


def aligned(i, n):
    return pl.multiple_of(i * n, n)


def tree(op, xs):
    acc = list(xs[:4])
    for i, x in enumerate(xs[4:]):
        acc[i % 4] = op(acc[i % 4], x)
    return op(op(acc[0], acc[1]), op(acc[2], acc[3]))


def merged(lse, delta, lse_b, delta_b):
    top = jnp.maximum(lse, lse_b)
    w, w_b = jnp.exp2(lse - top), jnp.exp2(lse_b - top)
    total = w + w_b
    return top + jnp.log2(total), (w * delta + w_b * delta_b) / total


def tiles_loop(full, count, step):
    def body(size, masked):
        def run(i, carry):
            for v in range(size):
                step(i * size + v, v, masked)
            return carry

        return run

    bodies = full // MANY
    lax.fori_loop(0, bodies, body(MANY, False), 0)
    lax.fori_loop(bodies * (MANY // FEW), (count + FEW - 1) // FEW, body(FEW, True), 0)


def load_sorted(meta, kvs, kv_s):
    for s in range(64):
        r = aligned(meta[IN + s], SPAN)
        t = slice((s % 2) * SPAN, (s % 2 + 1) * SPAN)
        kv_s[pl.ds(r, SPAN), :] = kvs[s // 8][(s // 2) % 4, t, :]


def row_of(place, h):
    odd = place % 2
    inner = odd * 512 + h * SPAN if h < 4 else R + odd * 128 + (h - 4) * SPAN
    return pl.multiple_of((place // 2) * 768 + inner, SPAN)


def load_rows(meta, base, qds, q_s, do_s, first=0):
    for d, ref in enumerate(qds):
        for half in range(2):
            place = meta[base + UNIT + 2 * (first + d) + half]
            t = slice(half * SPAN, (half + 1) * SPAN)
            for h in range(HEADS):
                r = row_of(place, h)
                q_s[pl.ds(r, SPAN), :] = ref[t, h * HD : (h + 1) * HD]
                do_s[pl.ds(r, SPAN), :] = ref[t, WIDE + h * HD : WIDE + (h + 1) * HD]
    rows = 3 * R * len(qds)
    q_s[rows : rows + R, :] = jnp.zeros((R, HD), q_s.dtype)
    do_s[rows : rows + R, :] = jnp.zeros((R, HD), do_s.dtype)


def products(meta, base, t, q_s, do_s, kv_s, s_b, dp_b):
    r, k = aligned(meta[base + GROUP + t], R), aligned(meta[base + BLOCK + t], KB)
    s_b[...] = dot(kv_s[pl.ds(k, KB), :HD], q_s[pl.ds(r, R), :], NT)
    dp_b[...] = dot(kv_s[pl.ds(k, KB), HD:], do_s[pl.ds(r, R), :], NT)


HALVES = ((0, 1), (2, 5), (3, 4))


def stats_kernel(which, devices, meta, lim, *refs):
    qds, kvs = refs[:devices], refs[devices : devices + 8]
    rest = refs[devices + 8 :]
    if which == FAR:
        before, rest = rest[0], rest[1:]
    out, q_s, do_s, kv_s, s0, s1, dp0, dp1, m_s, l_s, d_s = rest
    base, groups = of(which), 3 * devices
    load_sorted(meta, kvs, kv_s)
    load_rows(meta, base, qds, q_s, do_s, first=3 if which == FAR else 0)
    m_s[...] = jnp.full_like(m_s, NEG)
    l_s[...] = jnp.zeros_like(l_s)
    d_s[...] = jnp.zeros_like(d_s)
    iota = lax.broadcasted_iota(jnp.int32, (KB, R), 0)

    def online(t, s_b, dp_b, masked):
        g = meta[base + GROUP + t]
        rows = [slice(8 * i, 8 * i + 8) for i in range(KB // 8)]
        s = [s_b[r, :] * C2 for r in rows]
        if masked:
            limit = lim[which, pl.ds(g, 1), :] - meta[base + BLOCK + t] * KB
            s = [jnp.where(iota[r] < limit, x, NEG) for r, x in zip(rows, s)]
        m = m_s[g]
        top = jnp.maximum(m, tree(jnp.maximum, s))
        a = jnp.exp2(m - top)
        e = [jnp.exp2(x - top) for x in s]
        m_s[g] = top
        l_s[g] = l_s[g] * a + tree(jnp.add, e)
        d_s[g] = d_s[g] * a + tree(jnp.add, [x * dp_b[r, :] for r, x in zip(rows, e)])

    ss, dps = (s0, s1), (dp0, dp1)
    products(meta, base, 0, q_s, do_s, kv_s, s0, dp0)

    def step(t, v, masked):
        products(meta, base, t + 1, q_s, do_s, kv_s, ss[(v + 1) % 2], dps[(v + 1) % 2])
        online(t, ss[v % 2], dps[v % 2], masked)

    tiles_loop(meta[base + FULL], meta[base + COUNT], step)
    out[...] = before[...] if which == FAR else jnp.zeros_like(out)
    for g in range(groups):
        m = m_s[g]
        live = jnp.where(m > 0.5 * NEG, 1.0, 0.0)
        top = jnp.max(m, axis=0, keepdims=True)
        a = jnp.exp2(m - top) * live
        ll = jnp.sum(l_s[g] * a, axis=0, keepdims=True)
        dd = jnp.sum(d_s[g] * a, axis=0, keepdims=True)
        safe = jnp.where(ll > 0, ll, 1.0)
        lse = jnp.where(ll > 0, top + jnp.log2(safe), NEG)
        for half in range(2):
            place, pair = divmod(HALVES[g % 3][half], 3)
            row = meta[base + CANON + g // 3 * 2 + place] * 3 + pair
            at = slice(half * 128, half * 128 + 128)
            out[0, pl.ds(row, 1), :] = lse[:, at]
            out[1, pl.ds(row, 1), :] = (dd / safe)[:, at]


def grads_kernel(meta, lim, st0, st1, *refs):
    qds, kvs = refs[:4], refs[4:12]
    dqs, dkvs, dkv_other = refs[12:16], refs[16:20], refs[20]
    q_s, do_s, kv_s, s0, s1, dp0, dp1, acc, dq_s, p0, p1, ds0, ds1, lse, delta = refs[21:]
    load_sorted(meta, kvs, kv_s)
    base = of(ALL)
    load_rows(meta, base, qds, q_s, do_s)
    acc[...] = jnp.zeros_like(acc)
    dq_s[...] = jnp.zeros_like(dq_s)
    all_lse, all_delta = merged(st0[0], st0[1], st1[0], st1[1])
    lse[...] = jnp.zeros_like(lse)
    delta[...] = jnp.zeros_like(delta)
    for g in range(GROUPS):
        for half in range(2):
            row = g // 3 * 6 + HALVES[g % 3][half]
            at = slice(half * 128, half * 128 + 128)
            lse[g : g + 1, at] = all_lse[row : row + 1]
            delta[g : g + 1, at] = all_delta[row : row + 1]
    iota = lax.broadcasted_iota(jnp.int32, (KB, R), 0)

    def weights(t, s_b, dp_b, p_b, ds_b, masked):
        g = meta[base + GROUP + t]
        p = jnp.exp2(s_b[...] * C2 - lse[pl.ds(g, 1), :])
        if masked:
            limit = lim[ALL, pl.ds(g, 1), :] - meta[base + BLOCK + t] * KB
            p = jnp.where(iota < limit, p, 0.0)
        p_b[...] = p.astype(jnp.bfloat16)
        ds_b[...] = (p * (dp_b[...] - delta[pl.ds(g, 1), :])).astype(jnp.bfloat16)

    def sums(t, p_b, ds_b):
        r, k = aligned(meta[base + GROUP + t], R), aligned(meta[base + BLOCK + t], KB)
        dk = dot(ds_b[...], q_s[pl.ds(r, R), :], NN)
        dv = dot(p_b[...], do_s[pl.ds(r, R), :], NN)
        dq = dot(ds_b[...], kv_s[pl.ds(k, KB), :HD], TN)
        acc[pl.ds(k, KB), :HD] += dk
        acc[pl.ds(k, KB), HD:] += dv
        dq_s[pl.ds(r, R), :] += dq

    ss, dps, ps, dss = (s0, s1), (dp0, dp1), (p0, p1), (ds0, ds1)
    products(meta, base, 0, q_s, do_s, kv_s, s0, dp0)
    products(meta, base, 1, q_s, do_s, kv_s, s1, dp1)
    weights(0, s0, dp0, p0, ds0, True)

    def step(t, v, masked):
        a, b = v % 2, 1 - v % 2
        products(meta, base, t + 2, q_s, do_s, kv_s, ss[a], dps[a])
        weights(t + 1, ss[b], dps[b], ps[b], dss[b], masked or v == MANY - 1)
        sums(t, ps[a], dss[a])

    tiles_loop(meta[base + FULL], meta[base + COUNT], step)
    for d in range(4):
        for half in range(2):
            place = meta[base + UNIT + 2 * d + half]
            t = slice(half * SPAN, (half + 1) * SPAN)
            for h in range(HEADS):
                got = dq_s[pl.ds(row_of(place, h), SPAN), :] * SCALE
                dqs[d][t, h * HD : (h + 1) * HD] = got.astype(dqs[d].dtype)
    for s in range(64):
        r = aligned(meta[IN + s], SPAN)
        t = slice((s % 2) * SPAN, (s % 2 + 1) * SPAN)
        e = (s // 2) % 4
        ref = dkvs[s // 8] if s < 32 else dkv_other.at[s // 8 - 4]
        ref[e, t, :HD] = (acc[pl.ds(r, SPAN), :HD] * SCALE).astype(jnp.bfloat16)
        ref[e, t, HD:] = acc[pl.ds(r, SPAN), HD:].astype(jnp.bfloat16)


VM = pl.BlockSpec(memory_space=pltpu.VMEM)
SM = pl.BlockSpec(memory_space=pltpu.SMEM)
PARAMS = pltpu.CompilerParams(vmem_limit_bytes=48 * 2**20)
COPIES = [
    pltpu.VMEM(((GROUPS + 1) * R, HD), jnp.bfloat16),
    pltpu.VMEM(((GROUPS + 1) * R, HD), jnp.bfloat16),
    pltpu.VMEM((KEYS, 2 * HD), jnp.bfloat16),
] + [pltpu.VMEM((KB, R), jnp.float32)] * 4


def stats(which, meta, lim, qds, kvs, *before):
    n = len(qds)
    return pl.pallas_call(
        functools.partial(stats_kernel, which, n),
        out_shape=jax.ShapeDtypeStruct((2, 24, 128), jnp.float32),
        in_specs=[SM] + [VM] * (1 + n + 8 + len(before)),
        out_specs=VM,
        scratch_shapes=COPIES + [pltpu.VMEM((3 * n + 1, 8, R), jnp.float32)] * 3,
        compiler_params=PARAMS,
        cost_estimate=pl.CostEstimate(flops=n * 1_600_000_000, bytes_accessed=4_000_000, transcendentals=0),
        name="stats_near" if which == NEAR else "stats_far",
    )(meta, lim, *qds, *kvs, *before)


def grads(meta, lim, sts, arrays):
    dq = [jax.ShapeDtypeStruct((2 * SPAN, WIDE), t) for t in (jnp.float32,) + (jnp.bfloat16,) * 3]
    dkv = [jax.ShapeDtypeStruct((4, 2 * SPAN, 2 * HD), jnp.bfloat16)] * 4
    dkv += [jax.ShapeDtypeStruct((4, 4, 2 * SPAN, 2 * HD), jnp.bfloat16)]
    return pl.pallas_call(
        grads_kernel,
        out_shape=dq + dkv,
        in_specs=[SM] + [VM] * 15,
        out_specs=[VM] * 9,
        scratch_shapes=COPIES
        + [
            pltpu.VMEM((KEYS, 2 * HD), jnp.float32),
            pltpu.VMEM(((GROUPS + 1) * R, HD), jnp.float32),
        ]
        + [pltpu.VMEM((KB, R), jnp.bfloat16)] * 4
        + [pltpu.VMEM((16, R), jnp.float32)] * 2,
        compiler_params=PARAMS,
        name="grads",
    )(meta, lim, *sts, *arrays)


def permute(a, move):
    pairs = []
    for i in range(128):
        y, zl, core, zh, x = (int(c) for c in np.unravel_index(i, SIZES))
        y, z, core, x = (c % n for c, n in zip(move(y, 2 * zh + zl, core, x), (4, 4, 2, 4)))
        pairs.append((i, int(np.ravel_multi_index((y, z % 2, core, z // 2, x), SIZES))))
    return lax.ppermute(a, AXES, pairs)


def x_shift(a, step):
    return permute(a, lambda y, z, core, x: (y, z, core, x + step))


def first_shift(a, step):
    return permute(a, lambda y, z, core, x: (y, z + step, core, x) if core else (y + step, z, core, x))


def second_shift(a, step):
    return permute(a, lambda y, z, core, x: (y + step, z, core, x) if core else (y, z + step, core, x))


def core_swap(a):
    return permute(a, lambda y, z, core, x: (y, z, 1 - core, x))


def plan(span_slot):
    i32 = jnp.int32
    y, zl, core, zh, x = (lax.axis_index(a) for a in AXES)
    z = 2 * zh + zl
    grid = span_slot.reshape(*SIZES, 2)
    own_x = jnp.transpose(lax.dynamic_index_in_dim(grid, x, 4, keepdims=False), (2, 0, 3, 1, 4))
    own_x = own_x.reshape(2, 4, 4, 2)
    by_y = jnp.stack([lax.dynamic_index_in_dim(own_x, (y - r) % 4, 1, keepdims=False) for r in STEPS], 1)
    by_yz = jnp.stack([lax.dynamic_index_in_dim(by_y, (z - r) % 4, 2, keepdims=False) for r in STEPS], 2)
    of_core = jnp.stack([jnp.transpose(by_yz[0], (1, 0, 2)), by_yz[1]])
    arrived = jnp.where(core == 0, of_core, of_core[::-1]).reshape(64)
    ring = grid[y, zl, core, zh]
    queries = jnp.concatenate([ring[(x - r) % 4] for r in STEPS])

    def rank(a, among):
        return jnp.sum((among[None, :] < a[:, None]).astype(i32), axis=1)

    place = rank(queries, queries)
    eight = jnp.arange(8, dtype=i32)
    hit = (place[None, :] == eight[:, None]).astype(i32)
    spans = jnp.sum(hit * queries[None, :], axis=1)
    below = rank(spans, arrived)
    own = jnp.any(arrived[None, :] == spans[:, None], axis=1).astype(i32)
    far = jnp.sum(hit[:, 6:], axis=1)
    before = jnp.sum(jnp.tril(jnp.ones((8, 8), i32), -1) * far[None, :], axis=1)
    order = jnp.stack([eight, jnp.where(far == 0, eight - before, 9), jnp.where(far == 1, before, 9)])
    taken = (order[:, None, :] == eight[None, :, None]).astype(i32)
    canon = jnp.sum(taken * eight, axis=2)
    units = jnp.sum(order[:, None, :] * hit.T[None], axis=2)
    token = jnp.tile(jnp.arange(SPAN, dtype=i32), 2)
    seen = below[:, None] * SPAN + own[:, None] * (token[None, :] + 1)
    seen = jnp.sum(taken[:, :, :, None] * seen[None, None], axis=2)
    a, b = seen[:, 0::2], seen[:, 1::2]
    lim = jnp.stack([a, a, a, b, b, b], axis=2).reshape(3, GROUPS, R)
    lim = jnp.concatenate([lim, jnp.zeros((3, 4, R), i32)], axis=1)
    most = (jnp.sum(taken * (below + own), axis=2) * SPAN + KB - 1) // KB
    least = jnp.sum(taken * below, axis=2) * SPAN // KB
    most = jnp.stack([most[:, 0::2], most[:, 1::2], most[:, 1::2]], axis=2).reshape(3, GROUPS)
    least = jnp.stack([least[:, 0::2], least[:, 0::2], least[:, 1::2]], axis=2).reshape(3, GROUPS)
    each = jnp.concatenate([least, most - least], axis=1)
    first = jnp.concatenate([jnp.zeros_like(least), least], axis=1)
    end = jnp.sum(jnp.tril(jnp.ones((2 * GROUPS, 2 * GROUPS), i32)) * each[:, None, :], axis=2)
    t = jnp.arange(LIST, dtype=i32)
    begin = end - each
    inside = ((t[None, :, None] >= begin[:, None, :]) & (t[None, :, None] < end[:, None, :])).astype(i32)
    number = jnp.tile(jnp.arange(GROUPS, dtype=i32), 2)
    group = jnp.sum(inside * number, axis=2)
    block = jnp.sum(inside * (t[None, :, None] - (begin - first)[:, None, :]), axis=2)
    group = jnp.where(t[None] < end[:, -1:], group, jnp.array([[12], [9], [3]], i32))
    lists = jnp.concatenate([units, canon, end[:, GROUPS - 1 : GROUPS], end[:, -1:], group, block], axis=1)
    return jnp.concatenate([rank(arrived, arrived), lists.reshape(-1)]).astype(i32), lim


def local(queries, keys, values, grad_out, span_slot):
    kv = jnp.concatenate([keys, values], axis=1)[None]
    kv = jnp.concatenate([kv] + [first_shift(kv, r) for r in STEPS[1:]], axis=0)
    kvs = [kv] + [second_shift(kv, r) for r in STEPS[1:]]
    qd = jnp.concatenate([queries, grad_out], axis=1)
    near = [qd, x_shift(qd, 1), x_shift(qd, 3)]
    near[1], near[2], later = lax.optimization_barrier((near[1], near[2], qd))
    far = x_shift(later, 2)
    kvs[1], span_slot = lax.optimization_barrier((kvs[1], span_slot))
    meta, lim = plan(span_slot)
    kvs = kvs + [core_swap(a) for a in kvs]
    arrays = near + [far] + kvs

    part = stats(NEAR, meta, lim, near, kvs)
    part = stats(FAR, meta, lim, [far], kvs, part)
    got = permute(part, lambda y, z, core, x: (y, z, core, x ^ 1))
    part = jnp.stack(merged(part[0], part[1], got[0], got[1]))
    got = permute(part, lambda y, z, core, x: (y, z, core, x ^ 2))
    results = grads(meta, lim, (part, got), arrays)
    dqs, dkv, dkv_other = results[:4], results[4:8], results[8]

    def total(*parts):
        out = parts[0].astype(jnp.float32)
        for part in parts[1:]:
            out = out + part.astype(jnp.float32)
        return out

    dq = total(dqs[0], *[x_shift(a, -r) for r, a in zip(STEPS[1:], dqs[1:])])
    other = core_swap(dkv_other)
    pairs = [total(a, other[i]).astype(jnp.bfloat16) for i, a in enumerate(dkv)]
    some = total(pairs[0], *[second_shift(a, -r) for r, a in zip(STEPS[1:], pairs[1:])])
    sent = [first_shift(some[i].astype(jnp.bfloat16), -r) for i, r in ((1, 1), (2, 3), (3, 2))]
    summed = total(some[0], *sent)
    return (
        dq.astype(jnp.bfloat16),
        summed[:, :HD].astype(jnp.bfloat16),
        summed[:, HD:].astype(jnp.bfloat16),
    )


def solution(mesh):
    fine = Mesh(mesh.devices.reshape(4, 2, 2, 2, 4), AXES)
    rows = P(AXES, None)
    return jax.shard_map(
        local,
        mesh=fine,
        in_specs=(rows, rows, rows, rows, P()),
        out_specs=(rows, rows, rows),
        check_vma=False,
    )
```

```python
import functools
import math

import jax
import jax.numpy as jnp
import numpy as np
from jax import lax
from jax.experimental import pallas as pl
from jax.experimental.pallas import tpu as pltpu
from jax.sharding import Mesh, PartitionSpec as P

AXES = ("y", "zl", "core", "zh", "x")
SIZES = (4, 2, 2, 2, 4)
STEPS = (0, 1, 3, 2)
NEG = -1e30
HD = 128
SCALE = 1.0 / math.sqrt(HD)
C2 = math.log2(math.e) * SCALE
SPAN = 64
HEADS = 6
WIDE = HEADS * HD
KEYS = 4096
KB = 256
R = 256
GROUPS = 12
MANY, FEW = 16, 8
LIST = 144
IN = 0
ALL, NEAR, FAR = range(3)
UNIT, CANON, FULL, COUNT, GROUP = 0, 8, 16, 17, 18
BLOCK = GROUP + LIST
SIZE = BLOCK + LIST


def of(which):
    return 64 + which * SIZE


NT = (((1,), (1,)), ((), ()))
NN = (((1,), (0,)), ((), ()))
TN = (((0,), (0,)), ((), ()))


def dot(a, b, dims):
    return lax.dot_general(a, b, dims, preferred_element_type=jnp.float32)


def aligned(i, n):
    return pl.multiple_of(i * n, n)


def tree(op, xs):
    acc = list(xs[:4])
    for i, x in enumerate(xs[4:]):
        acc[i % 4] = op(acc[i % 4], x)
    return op(op(acc[0], acc[1]), op(acc[2], acc[3]))


def merged(lse, delta, lse_b, delta_b):
    top = jnp.maximum(lse, lse_b)
    w, w_b = jnp.exp2(lse - top), jnp.exp2(lse_b - top)
    total = w + w_b
    return top + jnp.log2(total), (w * delta + w_b * delta_b) / total


def tiles_loop(full, count, step):
    def body(size, masked):
        def run(i, carry):
            for v in range(size):
                step(i * size + v, v, masked)
            return carry

        return run

    bodies = full // MANY
    lax.fori_loop(0, bodies, body(MANY, False), 0)
    lax.fori_loop(bodies * (MANY // FEW), (count + FEW - 1) // FEW, body(FEW, True), 0)


def load_sorted(meta, kvs, kv_s):
    for s in range(64):
        r = aligned(meta[IN + s], SPAN)
        t = slice((s % 2) * SPAN, (s % 2 + 1) * SPAN)
        kv_s[pl.ds(r, SPAN), :] = kvs[s // 8][(s // 2) % 4, t, :]


def row_of(place, h):
    odd = place % 2
    inner = odd * 512 + h * SPAN if h < 4 else R + odd * 128 + (h - 4) * SPAN
    return pl.multiple_of((place // 2) * 768 + inner, SPAN)


def load_rows(meta, base, qds, q_s, do_s, first=0):
    for d, ref in enumerate(qds):
        for half in range(2):
            place = meta[base + UNIT + 2 * (first + d) + half]
            t = slice(half * SPAN, (half + 1) * SPAN)
            for h in range(HEADS):
                r = row_of(place, h)
                q_s[pl.ds(r, SPAN), :] = ref[t, h * HD : (h + 1) * HD]
                do_s[pl.ds(r, SPAN), :] = ref[t, WIDE + h * HD : WIDE + (h + 1) * HD]
    rows = 3 * R * len(qds)
    q_s[rows : rows + R, :] = jnp.zeros((R, HD), q_s.dtype)
    do_s[rows : rows + R, :] = jnp.zeros((R, HD), do_s.dtype)


def products(meta, base, t, q_s, do_s, kv_s, s_b, dp_b):
    r, k = aligned(meta[base + GROUP + t], R), aligned(meta[base + BLOCK + t], KB)
    s_b[...] = dot(kv_s[pl.ds(k, KB), :HD], q_s[pl.ds(r, R), :], NT)
    dp_b[...] = dot(kv_s[pl.ds(k, KB), HD:], do_s[pl.ds(r, R), :], NT)


HALVES = ((0, 1), (2, 5), (3, 4))


def stats_kernel(which, devices, meta, lim, *refs):
    qds, kvs = refs[:devices], refs[devices : devices + 8]
    rest = refs[devices + 8 :]
    if which == FAR:
        before, rest = rest[0], rest[1:]
    out, q_s, do_s, kv_s, s0, s1, dp0, dp1, m_s, l_s, d_s = rest
    base, groups = of(which), 3 * devices
    load_sorted(meta, kvs, kv_s)
    load_rows(meta, base, qds, q_s, do_s, first=3 if which == FAR else 0)
    m_s[...] = jnp.full_like(m_s, NEG)
    l_s[...] = jnp.zeros_like(l_s)
    d_s[...] = jnp.zeros_like(d_s)
    iota = lax.broadcasted_iota(jnp.int32, (KB, R), 0)

    def online(t, s_b, dp_b, masked):
        g = meta[base + GROUP + t]
        rows = [slice(8 * i, 8 * i + 8) for i in range(KB // 8)]
        s = [s_b[r, :] * C2 for r in rows]
        if masked:
            limit = lim[which, pl.ds(g, 1), :] - meta[base + BLOCK + t] * KB
            s = [jnp.where(iota[r] < limit, x, NEG) for r, x in zip(rows, s)]
        m = m_s[g]
        top = jnp.maximum(m, tree(jnp.maximum, s))
        a = jnp.exp2(m - top)
        e = [jnp.exp2(x - top) for x in s]
        m_s[g] = top
        l_s[g] = l_s[g] * a + tree(jnp.add, e)
        d_s[g] = d_s[g] * a + tree(jnp.add, [x * dp_b[r, :] for r, x in zip(rows, e)])

    ss, dps = (s0, s1), (dp0, dp1)
    products(meta, base, 0, q_s, do_s, kv_s, s0, dp0)

    def step(t, v, masked):
        products(meta, base, t + 1, q_s, do_s, kv_s, ss[(v + 1) % 2], dps[(v + 1) % 2])
        online(t, ss[v % 2], dps[v % 2], masked)

    tiles_loop(meta[base + FULL], meta[base + COUNT], step)
    out[...] = before[...] if which == FAR else jnp.zeros_like(out)
    for g in range(groups):
        m = m_s[g]
        live = jnp.where(m > 0.5 * NEG, 1.0, 0.0)
        top = jnp.max(m, axis=0, keepdims=True)
        a = jnp.exp2(m - top) * live
        ll = jnp.sum(l_s[g] * a, axis=0, keepdims=True)
        dd = jnp.sum(d_s[g] * a, axis=0, keepdims=True)
        safe = jnp.where(ll > 0, ll, 1.0)
        lse = jnp.where(ll > 0, top + jnp.log2(safe), NEG)
        for half in range(2):
            place, pair = divmod(HALVES[g % 3][half], 3)
            row = meta[base + CANON + g // 3 * 2 + place] * 3 + pair
            at = slice(half * 128, half * 128 + 128)
            out[0, pl.ds(row, 1), :] = lse[:, at]
            out[1, pl.ds(row, 1), :] = (dd / safe)[:, at]


def grads_kernel(meta, lim, st0, st1, *refs):
    qds, kvs = refs[:4], refs[4:12]
    dqs, dkvs, dkv_other = refs[12:16], refs[16:20], refs[20]
    q_s, do_s, kv_s, s0, s1, dp0, dp1, acc, dq_s, p0, p1, ds0, ds1, lse, delta = refs[21:]
    load_sorted(meta, kvs, kv_s)
    base = of(ALL)
    load_rows(meta, base, qds, q_s, do_s)
    acc[...] = jnp.zeros_like(acc)
    dq_s[...] = jnp.zeros_like(dq_s)
    all_lse, all_delta = merged(st0[0], st0[1], st1[0], st1[1])
    lse[...] = jnp.zeros_like(lse)
    delta[...] = jnp.zeros_like(delta)
    for g in range(GROUPS):
        for half in range(2):
            row = g // 3 * 6 + HALVES[g % 3][half]
            at = slice(half * 128, half * 128 + 128)
            lse[g : g + 1, at] = all_lse[row : row + 1]
            delta[g : g + 1, at] = all_delta[row : row + 1]
    iota = lax.broadcasted_iota(jnp.int32, (KB, R), 0)

    def weights(t, s_b, dp_b, p_b, ds_b, masked):
        g = meta[base + GROUP + t]
        p = jnp.exp2(s_b[...] * C2 - lse[pl.ds(g, 1), :])
        if masked:
            limit = lim[ALL, pl.ds(g, 1), :] - meta[base + BLOCK + t] * KB
            p = jnp.where(iota < limit, p, 0.0)
        p_b[...] = p.astype(jnp.bfloat16)
        ds_b[...] = (p * (dp_b[...] - delta[pl.ds(g, 1), :])).astype(jnp.bfloat16)

    def sums(t, p_b, ds_b):
        r, k = aligned(meta[base + GROUP + t], R), aligned(meta[base + BLOCK + t], KB)
        dk = dot(ds_b[...], q_s[pl.ds(r, R), :], NN)
        dv = dot(p_b[...], do_s[pl.ds(r, R), :], NN)
        dq = dot(ds_b[...], kv_s[pl.ds(k, KB), :HD], TN)
        acc[pl.ds(k, KB), :HD] += dk
        acc[pl.ds(k, KB), HD:] += dv
        dq_s[pl.ds(r, R), :] += dq

    ss, dps, ps, dss = (s0, s1), (dp0, dp1), (p0, p1), (ds0, ds1)
    products(meta, base, 0, q_s, do_s, kv_s, s0, dp0)
    products(meta, base, 1, q_s, do_s, kv_s, s1, dp1)
    weights(0, s0, dp0, p0, ds0, True)

    def step(t, v, masked):
        a, b = v % 2, 1 - v % 2
        products(meta, base, t + 2, q_s, do_s, kv_s, ss[a], dps[a])
        weights(t + 1, ss[b], dps[b], ps[b], dss[b], masked or v == MANY - 1)
        sums(t, ps[a], dss[a])

    tiles_loop(meta[base + FULL], meta[base + COUNT], step)
    for d in range(4):
        for half in range(2):
            place = meta[base + UNIT + 2 * d + half]
            t = slice(half * SPAN, (half + 1) * SPAN)
            for h in range(HEADS):
                got = dq_s[pl.ds(row_of(place, h), SPAN), :] * SCALE
                dqs[d][t, h * HD : (h + 1) * HD] = got.astype(dqs[d].dtype)
    for s in range(64):
        r = aligned(meta[IN + s], SPAN)
        t = slice((s % 2) * SPAN, (s % 2 + 1) * SPAN)
        e = (s // 2) % 4
        ref = dkvs[s // 8] if s < 32 else dkv_other.at[s // 8 - 4]
        ref[e, t, :HD] = (acc[pl.ds(r, SPAN), :HD] * SCALE).astype(jnp.bfloat16)
        ref[e, t, HD:] = acc[pl.ds(r, SPAN), HD:].astype(jnp.bfloat16)


VM = pl.BlockSpec(memory_space=pltpu.VMEM)
SM = pl.BlockSpec(memory_space=pltpu.SMEM)
PARAMS = pltpu.CompilerParams(vmem_limit_bytes=48 * 2**20)
COPIES = [
    pltpu.VMEM(((GROUPS + 1) * R, HD), jnp.bfloat16),
    pltpu.VMEM(((GROUPS + 1) * R, HD), jnp.bfloat16),
    pltpu.VMEM((KEYS, 2 * HD), jnp.bfloat16),
] + [pltpu.VMEM((KB, R), jnp.float32)] * 4


def stats(which, meta, lim, qds, kvs, *before):
    n = len(qds)
    return pl.pallas_call(
        functools.partial(stats_kernel, which, n),
        out_shape=jax.ShapeDtypeStruct((2, 24, 128), jnp.float32),
        in_specs=[SM] + [VM] * (1 + n + 8 + len(before)),
        out_specs=VM,
        scratch_shapes=COPIES + [pltpu.VMEM((3 * n + 1, 8, R), jnp.float32)] * 3,
        compiler_params=PARAMS,
        cost_estimate=pl.CostEstimate(flops=n * 1_000_000, bytes_accessed=100_000, transcendentals=0),
        name="stats_near" if which == NEAR else "stats_far",
    )(meta, lim, *qds, *kvs, *before)


def grads(meta, lim, sts, arrays):
    dq = [jax.ShapeDtypeStruct((2 * SPAN, WIDE), t) for t in (jnp.float32,) + (jnp.bfloat16,) * 3]
    dkv = [jax.ShapeDtypeStruct((4, 2 * SPAN, 2 * HD), jnp.bfloat16)] * 4
    dkv += [jax.ShapeDtypeStruct((4, 4, 2 * SPAN, 2 * HD), jnp.bfloat16)]
    return pl.pallas_call(
        grads_kernel,
        out_shape=dq + dkv,
        in_specs=[SM] + [VM] * 15,
        out_specs=[VM] * 9,
        scratch_shapes=COPIES
        + [
            pltpu.VMEM((KEYS, 2 * HD), jnp.float32),
            pltpu.VMEM(((GROUPS + 1) * R, HD), jnp.float32),
        ]
        + [pltpu.VMEM((KB, R), jnp.bfloat16)] * 4
        + [pltpu.VMEM((16, R), jnp.float32)] * 2,
        compiler_params=PARAMS,
        name="grads",
    )(meta, lim, *sts, *arrays)


def permute(a, move):
    pairs = []
    for i in range(128):
        y, zl, core, zh, x = (int(c) for c in np.unravel_index(i, SIZES))
        y, z, core, x = (c % n for c, n in zip(move(y, 2 * zh + zl, core, x), (4, 4, 2, 4)))
        pairs.append((i, int(np.ravel_multi_index((y, z % 2, core, z // 2, x), SIZES))))
    return lax.ppermute(a, AXES, pairs)


def x_shift(a, step):
    return permute(a, lambda y, z, core, x: (y, z, core, x + step))


def first_shift(a, step):
    return permute(a, lambda y, z, core, x: (y, z + step, core, x) if core else (y + step, z, core, x))


def second_shift(a, step):
    return permute(a, lambda y, z, core, x: (y + step, z, core, x) if core else (y, z + step, core, x))


def core_swap(a):
    return permute(a, lambda y, z, core, x: (y, z, 1 - core, x))


def plan(span_slot):
    i32 = jnp.int32
    y, zl, core, zh, x = (lax.axis_index(a) for a in AXES)
    z = 2 * zh + zl
    i = jnp.arange(72, dtype=i32)
    is_key = i < 64
    low, high = (i // 2) % 4, (i // 8) % 4
    low, high = low ^ (low >> 1), high ^ (high >> 1)
    at_core = jnp.where(is_key & (i >= 32), 1 - core, core)
    at_y = jnp.where(is_key, (y - jnp.where(at_core == 0, low, high)) % 4, y)
    at_z = jnp.where(is_key, (z - jnp.where(at_core == 0, high, low)) % 4, z)
    at_x = jnp.where(is_key, x, (x - low) % 4)
    slot = ((((at_y * 2 + at_z % 2) * 2 + at_core) * 2 + at_z // 2) * 4 + at_x) * 2 + i % 2
    spans = jnp.sum(jnp.where(slot[:, None] == jnp.arange(256)[None, :], span_slot[None, :], 0), axis=1)
    arrived, queries = spans[:64], spans[64:]

    def rank(a, among):
        return jnp.sum((among[None, :] < a[:, None]).astype(i32), axis=1)

    place = rank(queries, queries)
    eight = jnp.arange(8, dtype=i32)
    hit = (place[None, :] == eight[:, None]).astype(i32)
    spans = jnp.sum(hit * queries[None, :], axis=1)
    below = rank(spans, arrived)
    own = jnp.any(arrived[None, :] == spans[:, None], axis=1).astype(i32)
    far = jnp.sum(hit[:, 6:], axis=1)
    before = jnp.sum(jnp.tril(jnp.ones((8, 8), i32), -1) * far[None, :], axis=1)
    order = jnp.stack([eight, jnp.where(far == 0, eight - before, 9), jnp.where(far == 1, before, 9)])
    taken = (order[:, None, :] == eight[None, :, None]).astype(i32)
    canon = jnp.sum(taken * eight, axis=2)
    units = jnp.sum(order[:, None, :] * hit.T[None], axis=2)
    token = jnp.tile(jnp.arange(SPAN, dtype=i32), 2)
    seen = below[:, None] * SPAN + own[:, None] * (token[None, :] + 1)
    seen = jnp.sum(taken[:, :, :, None] * seen[None, None], axis=2)
    a, b = seen[:, 0::2], seen[:, 1::2]
    lim = jnp.stack([a, a, a, b, b, b], axis=2).reshape(3, GROUPS, R)
    lim = jnp.concatenate([lim, jnp.zeros((3, 4, R), i32)], axis=1)
    most = (jnp.sum(taken * (below + own), axis=2) * SPAN + KB - 1) // KB
    least = jnp.sum(taken * below, axis=2) * SPAN // KB
    most = jnp.stack([most[:, 0::2], most[:, 1::2], most[:, 1::2]], axis=2).reshape(3, GROUPS)
    least = jnp.stack([least[:, 0::2], least[:, 0::2], least[:, 1::2]], axis=2).reshape(3, GROUPS)
    each = jnp.concatenate([least, most - least], axis=1)
    first = jnp.concatenate([jnp.zeros_like(least), least], axis=1)
    end = jnp.sum(jnp.tril(jnp.ones((2 * GROUPS, 2 * GROUPS), i32)) * each[:, None, :], axis=2)
    t = jnp.arange(LIST, dtype=i32)
    begin = end - each
    inside = ((t[None, :, None] >= begin[:, None, :]) & (t[None, :, None] < end[:, None, :])).astype(i32)
    number = jnp.tile(jnp.arange(GROUPS, dtype=i32), 2)
    group = jnp.sum(inside * number, axis=2)
    block = jnp.sum(inside * (t[None, :, None] - (begin - first)[:, None, :]), axis=2)
    group = jnp.where(t[None] < end[:, -1:], group, jnp.array([[12], [9], [3]], i32))
    lists = jnp.concatenate([units, canon, end[:, GROUPS - 1 : GROUPS], end[:, -1:], group, block], axis=1)
    return jnp.concatenate([rank(arrived, arrived), lists.reshape(-1)]).astype(i32), lim


def local(queries, keys, values, grad_out, span_slot):
    kv = jnp.concatenate([keys, values], axis=1)[None]
    kv = jnp.concatenate([kv] + [first_shift(kv, r) for r in STEPS[1:]], axis=0)
    kvs = [kv] + [second_shift(kv, r) for r in STEPS[1:]]
    qd = jnp.concatenate([queries, grad_out], axis=1)
    near = [qd, x_shift(qd, 1), x_shift(qd, 3)]
    near[1], near[2], later = lax.optimization_barrier((near[1], near[2], qd))
    far = x_shift(later, 2)
    kvs[0], kvs[1], span_slot = lax.optimization_barrier((kvs[0], kvs[1], span_slot))
    meta, lim = plan(span_slot)
    kvs = kvs + [core_swap(a) for a in kvs]
    arrays = near + [far] + kvs

    part = stats(NEAR, meta, lim, near, kvs)
    part = stats(FAR, meta, lim, [far], kvs, part)
    got = permute(part, lambda y, z, core, x: (y, z, core, x ^ 1))
    part = jnp.stack(merged(part[0], part[1], got[0], got[1]))
    got = permute(part, lambda y, z, core, x: (y, z, core, x ^ 2))
    results = grads(meta, lim, (part, got), arrays)
    dqs, dkv, dkv_other = results[:4], results[4:8], results[8]

    def total(*parts):
        out = parts[0].astype(jnp.float32)
        for part in parts[1:]:
            out = out + part.astype(jnp.float32)
        return out

    other = core_swap(dkv_other)
    pairs = [total(a, other[i]).astype(jnp.bfloat16) for i, a in enumerate(dkv)]
    some = total(pairs[0], *[second_shift(a, -r) for r, a in zip(STEPS[1:], pairs[1:])])
    back = [x_shift(dqs[1], -1), x_shift(dqs[2], -3)]
    some, back[0], back[1], last = lax.optimization_barrier((some, back[0], back[1], dqs[3]))
    sent = [first_shift(some[i].astype(jnp.bfloat16), -r) for i, r in ((1, 1), (2, 3), (3, 2))]
    dq = total(dqs[0], *back, x_shift(last, -2))
    summed = total(some[0], *sent)
    return (
        dq.astype(jnp.bfloat16),
        summed[:, :HD].astype(jnp.bfloat16),
        summed[:, HD:].astype(jnp.bfloat16),
    )


def solution(mesh):
    fine = Mesh(mesh.devices.reshape(4, 2, 2, 2, 4), AXES)
    rows = P(AXES, None)
    return jax.shard_map(
        local,
        mesh=fine,
        in_specs=(rows, rows, rows, rows, P()),
        out_specs=(rows, rows, rows),
        check_vma=False,
    )
```

```python
import functools
import math

import jax
import jax.numpy as jnp
import numpy as np
from jax import lax
from jax.experimental import pallas as pl
from jax.experimental.pallas import tpu as pltpu
from jax.sharding import Mesh, PartitionSpec as P

AXES = ("y", "zl", "core", "zh", "x")
SIZES = (4, 2, 2, 2, 4)
STEPS = (0, 1, 3, 2)
NEG = -1e30
HD = 128
SCALE = 1.0 / math.sqrt(HD)
C2 = math.log2(math.e) * SCALE
SPAN = 64
HEADS = 6
WIDE = HEADS * HD
KEYS = 4096
KB = 256
R = 256
GROUPS = 12
MANY, FEW = 16, 8
LIST = 144
IN = 0
ALL, NEAR, FAR = range(3)
UNIT, CANON, FULL, COUNT, GROUP = 0, 8, 16, 17, 18
BLOCK = GROUP + LIST
SIZE = BLOCK + LIST


OWNER = 64


def of(which):
    return 68 + which * SIZE


NT = (((1,), (1,)), ((), ()))
NN = (((1,), (0,)), ((), ()))
TN = (((0,), (0,)), ((), ()))


def dot(a, b, dims):
    return lax.dot_general(a, b, dims, preferred_element_type=jnp.float32)


def aligned(i, n):
    return pl.multiple_of(i * n, n)


def tree(op, xs):
    acc = list(xs[:4])
    for i, x in enumerate(xs[4:]):
        acc[i % 4] = op(acc[i % 4], x)
    return op(op(acc[0], acc[1]), op(acc[2], acc[3]))


def merged(lse, delta, lse_b, delta_b):
    top = jnp.maximum(lse, lse_b)
    w, w_b = jnp.exp2(lse - top), jnp.exp2(lse_b - top)
    total = w + w_b
    return top + jnp.log2(total), (w * delta + w_b * delta_b) / total


def tiles_loop(full, count, step):
    def body(size, masked):
        def run(i, carry):
            for v in range(size):
                step(i * size + v, v, masked)
            return carry

        return run

    bodies = full // MANY
    lax.fori_loop(0, bodies, body(MANY, False), 0)
    lax.fori_loop(bodies * (MANY // FEW), (count + FEW - 1) // FEW, body(FEW, True), 0)


def load_sorted(meta, kvs, kv_s):
    for s in range(64):
        r = aligned(meta[IN + s], SPAN)
        t = slice((s % 2) * SPAN, (s % 2 + 1) * SPAN)
        kv_s[pl.ds(r, SPAN), :] = kvs[s // 8][(s // 2) % 4, t, :]


def row_of(place, h):
    odd = place % 2
    inner = odd * 512 + h * SPAN if h < 4 else R + odd * 128 + (h - 4) * SPAN
    return pl.multiple_of((place // 2) * 768 + inner, SPAN)


def load_rows(meta, base, qds, q_s, do_s, first=0):
    for d, ref in enumerate(qds):
        for half in range(2):
            place = meta[base + UNIT + 2 * (first + d) + half]
            t = slice(half * SPAN, (half + 1) * SPAN)
            for h in range(HEADS):
                r = row_of(place, h)
                q_s[pl.ds(r, SPAN), :] = ref[t, h * HD : (h + 1) * HD]
                do_s[pl.ds(r, SPAN), :] = ref[t, WIDE + h * HD : WIDE + (h + 1) * HD]
    rows = 3 * R * len(qds)
    q_s[rows : rows + R, :] = jnp.zeros((R, HD), q_s.dtype)
    do_s[rows : rows + R, :] = jnp.zeros((R, HD), do_s.dtype)


def products(meta, base, t, q_s, do_s, kv_s, s_b, dp_b):
    r, k = aligned(meta[base + GROUP + t], R), aligned(meta[base + BLOCK + t], KB)
    s_b[...] = dot(kv_s[pl.ds(k, KB), :HD], q_s[pl.ds(r, R), :], NT)
    dp_b[...] = dot(kv_s[pl.ds(k, KB), HD:], do_s[pl.ds(r, R), :], NT)


HALVES = ((0, 1), (2, 5), (3, 4))


def stats_kernel(which, devices, meta, lim, *refs):
    qds, kvs = refs[:devices], refs[devices : devices + 8]
    rest = refs[devices + 8 :]
    if which == FAR:
        before, rest = rest[0], rest[1:]
    out, q_s, do_s, kv_s, s0, s1, dp0, dp1, m_s, l_s, d_s = rest
    base, groups = of(which), 3 * devices
    load_sorted(meta, kvs, kv_s)
    load_rows(meta, base, qds, q_s, do_s, first=3 if which == FAR else 0)
    m_s[...] = jnp.full_like(m_s, NEG)
    l_s[...] = jnp.zeros_like(l_s)
    d_s[...] = jnp.zeros_like(d_s)
    iota = lax.broadcasted_iota(jnp.int32, (KB, R), 0)

    def online(t, s_b, dp_b, masked):
        g = meta[base + GROUP + t]
        rows = [slice(8 * i, 8 * i + 8) for i in range(KB // 8)]
        s = [s_b[r, :] * C2 for r in rows]
        if masked:
            limit = lim[which, pl.ds(g, 1), :] - meta[base + BLOCK + t] * KB
            s = [jnp.where(iota[r] < limit, x, NEG) for r, x in zip(rows, s)]
        m = m_s[g]
        top = jnp.maximum(m, tree(jnp.maximum, s))
        a = jnp.exp2(m - top)
        e = [jnp.exp2(x - top) for x in s]
        m_s[g] = top
        l_s[g] = l_s[g] * a + tree(jnp.add, e)
        d_s[g] = d_s[g] * a + tree(jnp.add, [x * dp_b[r, :] for r, x in zip(rows, e)])

    ss, dps = (s0, s1), (dp0, dp1)
    products(meta, base, 0, q_s, do_s, kv_s, s0, dp0)

    def step(t, v, masked):
        products(meta, base, t + 1, q_s, do_s, kv_s, ss[(v + 1) % 2], dps[(v + 1) % 2])
        online(t, ss[v % 2], dps[v % 2], masked)

    tiles_loop(meta[base + FULL], meta[base + COUNT], step)
    out[...] = before[...] if which == FAR else jnp.zeros_like(out)
    for g in range(groups):
        m = m_s[g]
        live = jnp.where(m > 0.5 * NEG, 1.0, 0.0)
        top = jnp.max(m, axis=0, keepdims=True)
        a = jnp.exp2(m - top) * live
        ll = jnp.sum(l_s[g] * a, axis=0, keepdims=True)
        dd = jnp.sum(d_s[g] * a, axis=0, keepdims=True)
        safe = jnp.where(ll > 0, ll, 1.0)
        lse = jnp.where(ll > 0, top + jnp.log2(safe), NEG)
        for half in range(2):
            place, pair = divmod(HALVES[g % 3][half], 3)
            row = meta[base + CANON + g // 3 * 2 + place] * 3 + pair
            at = slice(half * 128, half * 128 + 128)
            out[0, pl.ds(row, 1), :] = lse[:, at]
            out[1, pl.ds(row, 1), :] = (dd / safe)[:, at]


def grads_kernel(meta, lim, st0, st1, *refs):
    qds, kvs = refs[:4], refs[4:12]
    dqs, dkvs, dkv_other = refs[12], refs[13:17], refs[17]
    q_s, do_s, kv_s, s0, s1, dp0, dp1, acc, dq_s, p0, p1, ds0, ds1, lse, delta = refs[18:]
    load_sorted(meta, kvs, kv_s)
    base = of(ALL)
    load_rows(meta, base, qds, q_s, do_s)
    acc[...] = jnp.zeros_like(acc)
    dq_s[...] = jnp.zeros_like(dq_s)
    all_lse, all_delta = merged(st0[0], st0[1], st1[0], st1[1])
    lse[...] = jnp.zeros_like(lse)
    delta[...] = jnp.zeros_like(delta)
    for g in range(GROUPS):
        for half in range(2):
            row = g // 3 * 6 + HALVES[g % 3][half]
            at = slice(half * 128, half * 128 + 128)
            lse[g : g + 1, at] = all_lse[row : row + 1]
            delta[g : g + 1, at] = all_delta[row : row + 1]
    iota = lax.broadcasted_iota(jnp.int32, (KB, R), 0)

    def weights(t, s_b, dp_b, p_b, ds_b, masked):
        g = meta[base + GROUP + t]
        p = jnp.exp2(s_b[...] * C2 - lse[pl.ds(g, 1), :])
        if masked:
            limit = lim[ALL, pl.ds(g, 1), :] - meta[base + BLOCK + t] * KB
            p = jnp.where(iota < limit, p, 0.0)
        p_b[...] = p.astype(jnp.bfloat16)
        ds_b[...] = (p * (dp_b[...] - delta[pl.ds(g, 1), :])).astype(jnp.bfloat16)

    def sums(t, p_b, ds_b):
        r, k = aligned(meta[base + GROUP + t], R), aligned(meta[base + BLOCK + t], KB)
        dk = dot(ds_b[...], q_s[pl.ds(r, R), :], NN)
        dv = dot(p_b[...], do_s[pl.ds(r, R), :], NN)
        dq = dot(ds_b[...], kv_s[pl.ds(k, KB), :HD], TN)
        acc[pl.ds(k, KB), :HD] += dk
        acc[pl.ds(k, KB), HD:] += dv
        dq_s[pl.ds(r, R), :] += dq

    ss, dps, ps, dss = (s0, s1), (dp0, dp1), (p0, p1), (ds0, ds1)
    products(meta, base, 0, q_s, do_s, kv_s, s0, dp0)
    products(meta, base, 1, q_s, do_s, kv_s, s1, dp1)
    weights(0, s0, dp0, p0, ds0, True)

    def step(t, v, masked):
        a, b = v % 2, 1 - v % 2
        products(meta, base, t + 2, q_s, do_s, kv_s, ss[a], dps[a])
        weights(t + 1, ss[b], dps[b], ps[b], dss[b], masked or v == MANY - 1)
        sums(t, ps[a], dss[a])

    tiles_loop(meta[base + FULL], meta[base + COUNT], step)
    for d in range(4):
        for half in range(2):
            place = meta[base + UNIT + 2 * d + half]
            t = slice(half * SPAN, (half + 1) * SPAN)
            for h in range(HEADS):
                got = dq_s[pl.ds(row_of(place, h), SPAN), :] * SCALE
                dqs[meta[OWNER + d], t, h * HD : (h + 1) * HD] = got
    for s in range(64):
        r = aligned(meta[IN + s], SPAN)
        t = slice((s % 2) * SPAN, (s % 2 + 1) * SPAN)
        e = (s // 2) % 4
        ref = dkvs[s // 8] if s < 32 else dkv_other.at[s // 8 - 4]
        ref[e, t, :HD] = (acc[pl.ds(r, SPAN), :HD] * SCALE).astype(jnp.bfloat16)
        ref[e, t, HD:] = acc[pl.ds(r, SPAN), HD:].astype(jnp.bfloat16)


VM = pl.BlockSpec(memory_space=pltpu.VMEM)
SM = pl.BlockSpec(memory_space=pltpu.SMEM)
PARAMS = pltpu.CompilerParams(vmem_limit_bytes=48 * 2**20)
COPIES = [
    pltpu.VMEM(((GROUPS + 1) * R, HD), jnp.bfloat16),
    pltpu.VMEM(((GROUPS + 1) * R, HD), jnp.bfloat16),
    pltpu.VMEM((KEYS, 2 * HD), jnp.bfloat16),
] + [pltpu.VMEM((KB, R), jnp.float32)] * 4


def stats(which, meta, lim, qds, kvs, *before):
    n = len(qds)
    return pl.pallas_call(
        functools.partial(stats_kernel, which, n),
        out_shape=jax.ShapeDtypeStruct((2, 24, 128), jnp.float32),
        in_specs=[SM] + [VM] * (1 + n + 8 + len(before)),
        out_specs=VM,
        scratch_shapes=COPIES + [pltpu.VMEM((3 * n + 1, 8, R), jnp.float32)] * 3,
        compiler_params=PARAMS,
        cost_estimate=pl.CostEstimate(flops=n * 1_000_000, bytes_accessed=100_000, transcendentals=0),
        name="stats_near" if which == NEAR else "stats_far",
    )(meta, lim, *qds, *kvs, *before)


def grads(meta, lim, sts, arrays):
    dq = [jax.ShapeDtypeStruct((4, 2 * SPAN, WIDE), jnp.float32)]
    dkv = [jax.ShapeDtypeStruct((4, 2 * SPAN, 2 * HD), jnp.bfloat16)] * 4
    dkv += [jax.ShapeDtypeStruct((4, 4, 2 * SPAN, 2 * HD), jnp.bfloat16)]
    return pl.pallas_call(
        grads_kernel,
        out_shape=dq + dkv,
        in_specs=[SM] + [VM] * 15,
        out_specs=[VM] * 6,
        scratch_shapes=COPIES
        + [
            pltpu.VMEM((KEYS, 2 * HD), jnp.float32),
            pltpu.VMEM(((GROUPS + 1) * R, HD), jnp.float32),
        ]
        + [pltpu.VMEM((KB, R), jnp.bfloat16)] * 4
        + [pltpu.VMEM((16, R), jnp.float32)] * 2,
        compiler_params=PARAMS,
        name="grads",
    )(meta, lim, *sts, *arrays)


def permute(a, move):
    pairs = []
    for i in range(128):
        y, zl, core, zh, x = (int(c) for c in np.unravel_index(i, SIZES))
        y, z, core, x = (c % n for c, n in zip(move(y, 2 * zh + zl, core, x), (4, 4, 2, 4)))
        pairs.append((i, int(np.ravel_multi_index((y, z % 2, core, z // 2, x), SIZES))))
    return lax.ppermute(a, AXES, pairs)


def x_shift(a, step):
    return permute(a, lambda y, z, core, x: (y, z, core, x + step))


def first_shift(a, step):
    return permute(a, lambda y, z, core, x: (y, z + step, core, x) if core else (y + step, z, core, x))


def second_shift(a, step):
    return permute(a, lambda y, z, core, x: (y + step, z, core, x) if core else (y, z + step, core, x))


def core_swap(a):
    return permute(a, lambda y, z, core, x: (y, z, 1 - core, x))


def plan(span_slot):
    i32 = jnp.int32
    y, zl, core, zh, x = (lax.axis_index(a) for a in AXES)
    z = 2 * zh + zl
    i = jnp.arange(72, dtype=i32)
    is_key = i < 64
    low, high = (i // 2) % 4, (i // 8) % 4
    low, high = low ^ (low >> 1), high ^ (high >> 1)
    at_core = jnp.where(is_key & (i >= 32), 1 - core, core)
    at_y = jnp.where(is_key, (y - jnp.where(at_core == 0, low, high)) % 4, y)
    at_z = jnp.where(is_key, (z - jnp.where(at_core == 0, high, low)) % 4, z)
    at_x = jnp.where(is_key, x, (x - low) % 4)
    slot = ((((at_y * 2 + at_z % 2) * 2 + at_core) * 2 + at_z // 2) * 4 + at_x) * 2 + i % 2
    spans = jnp.sum(jnp.where(slot[:, None] == jnp.arange(256)[None, :], span_slot[None, :], 0), axis=1)
    arrived, queries = spans[:64], spans[64:]

    def rank(a, among):
        return jnp.sum((among[None, :] < a[:, None]).astype(i32), axis=1)

    place = rank(queries, queries)
    eight = jnp.arange(8, dtype=i32)
    hit = (place[None, :] == eight[:, None]).astype(i32)
    spans = jnp.sum(hit * queries[None, :], axis=1)
    below = rank(spans, arrived)
    own = jnp.any(arrived[None, :] == spans[:, None], axis=1).astype(i32)
    far = jnp.sum(hit[:, 6:], axis=1)
    before = jnp.sum(jnp.tril(jnp.ones((8, 8), i32), -1) * far[None, :], axis=1)
    order = jnp.stack([eight, jnp.where(far == 0, eight - before, 9), jnp.where(far == 1, before, 9)])
    taken = (order[:, None, :] == eight[None, :, None]).astype(i32)
    canon = jnp.sum(taken * eight, axis=2)
    units = jnp.sum(order[:, None, :] * hit.T[None], axis=2)
    token = jnp.tile(jnp.arange(SPAN, dtype=i32), 2)
    seen = below[:, None] * SPAN + own[:, None] * (token[None, :] + 1)
    seen = jnp.sum(taken[:, :, :, None] * seen[None, None], axis=2)
    a, b = seen[:, 0::2], seen[:, 1::2]
    lim = jnp.stack([a, a, a, b, b, b], axis=2).reshape(3, GROUPS, R)
    lim = jnp.concatenate([lim, jnp.zeros((3, 4, R), i32)], axis=1)
    most = (jnp.sum(taken * (below + own), axis=2) * SPAN + KB - 1) // KB
    least = jnp.sum(taken * below, axis=2) * SPAN // KB
    most = jnp.stack([most[:, 0::2], most[:, 1::2], most[:, 1::2]], axis=2).reshape(3, GROUPS)
    least = jnp.stack([least[:, 0::2], least[:, 0::2], least[:, 1::2]], axis=2).reshape(3, GROUPS)
    each = jnp.concatenate([least, most - least], axis=1)
    first = jnp.concatenate([jnp.zeros_like(least), least], axis=1)
    end = jnp.sum(jnp.tril(jnp.ones((2 * GROUPS, 2 * GROUPS), i32)) * each[:, None, :], axis=2)
    t = jnp.arange(LIST, dtype=i32)
    begin = end - each
    inside = ((t[None, :, None] >= begin[:, None, :]) & (t[None, :, None] < end[:, None, :])).astype(i32)
    number = jnp.tile(jnp.arange(GROUPS, dtype=i32), 2)
    group = jnp.sum(inside * number, axis=2)
    block = jnp.sum(inside * (t[None, :, None] - (begin - first)[:, None, :]), axis=2)
    group = jnp.where(t[None] < end[:, -1:], group, jnp.array([[12], [9], [3]], i32))
    lists = jnp.concatenate([units, canon, end[:, GROUPS - 1 : GROUPS], end[:, -1:], group, block], axis=1)
    owners = (x - jnp.array(STEPS, i32)) % 4
    return jnp.concatenate([rank(arrived, arrived), owners, lists.reshape(-1)]).astype(i32), lim


def local(queries, keys, values, grad_out, span_slot):
    kv = jnp.concatenate([keys, values], axis=1)[None]
    kv = jnp.concatenate([kv] + [first_shift(kv, r) for r in STEPS[1:]], axis=0)
    kvs = [kv] + [second_shift(kv, r) for r in STEPS[1:]]
    qd = jnp.concatenate([queries, grad_out], axis=1)
    near = [qd, x_shift(qd, 1), x_shift(qd, 3)]
    near[1], near[2], later = lax.optimization_barrier((near[1], near[2], qd))
    far = x_shift(later, 2)
    kvs[0], kvs[1], span_slot = lax.optimization_barrier((kvs[0], kvs[1], span_slot))
    meta, lim = plan(span_slot)
    kvs = kvs + [core_swap(a) for a in kvs]
    arrays = near + [far] + kvs

    part = stats(NEAR, meta, lim, near, kvs)
    part = stats(FAR, meta, lim, [far], kvs, part)
    got = permute(part, lambda y, z, core, x: (y, z, core, x ^ 1))
    part = jnp.stack(merged(part[0], part[1], got[0], got[1]))
    got = permute(part, lambda y, z, core, x: (y, z, core, x ^ 2))
    results = grads(meta, lim, (part, got), arrays)
    dqs, dkv, dkv_other = results[0], results[1:5], results[5]

    def total(*parts):
        out = parts[0].astype(jnp.float32)
        for part in parts[1:]:
            out = out + part.astype(jnp.float32)
        return out

    dq = lax.psum_scatter(dqs, "x", scatter_dimension=0, tiled=False)
    other = core_swap(dkv_other)
    pairs = [total(a, other[i]).astype(jnp.bfloat16) for i, a in enumerate(dkv)]
    some = total(pairs[0], *[second_shift(a, -r) for r, a in zip(STEPS[1:], pairs[1:])])
    sent = [first_shift(some[i].astype(jnp.bfloat16), -r) for i, r in ((1, 1), (2, 3), (3, 2))]
    summed = total(some[0], *sent)
    return (
        dq.astype(jnp.bfloat16),
        summed[:, :HD].astype(jnp.bfloat16),
        summed[:, HD:].astype(jnp.bfloat16),
    )


def solution(mesh):
    fine = Mesh(mesh.devices.reshape(4, 2, 2, 2, 4), AXES)
    rows = P(AXES, None)
    return jax.shard_map(
        local,
        mesh=fine,
        in_specs=(rows, rows, rows, rows, P()),
        out_specs=(rows, rows, rows),
        check_vma=False,
    )
```

```python
import functools
import math

import jax
import jax.numpy as jnp
import numpy as np
from jax import lax
from jax.experimental import pallas as pl
from jax.experimental.pallas import tpu as pltpu
from jax.sharding import Mesh, PartitionSpec as P

AXES = ("y", "zl", "core", "zh", "x")
SIZES = (4, 2, 2, 2, 4)
STEPS = (0, 1, 3, 2)
NEG = -1e30
HD = 128
SCALE = 1.0 / math.sqrt(HD)
C2 = math.log2(math.e) * SCALE
SPAN = 64
HEADS = 6
WIDE = HEADS * HD
KEYS = 4096
KB = 256
R = 256
GROUPS = 12
MANY, SOME, FEW = 16, 8, 2
LIST = 144
IN = 0
ALL, NEAR, FAR = range(3)
UNIT, CANON, FULL, COUNT, GROUP = 0, 8, 16, 17, 18
BLOCK = GROUP + LIST
SIZE = BLOCK + LIST


def of(which):
    return 64 + which * SIZE


NT = (((1,), (1,)), ((), ()))
NN = (((1,), (0,)), ((), ()))
TN = (((0,), (0,)), ((), ()))


def dot(a, b, dims):
    return lax.dot_general(a, b, dims, preferred_element_type=jnp.float32)


def aligned(i, n):
    return pl.multiple_of(i * n, n)


def tree(op, xs):
    acc = list(xs[:4])
    for i, x in enumerate(xs[4:]):
        acc[i % 4] = op(acc[i % 4], x)
    return op(op(acc[0], acc[1]), op(acc[2], acc[3]))


def merged(lse, delta, lse_b, delta_b):
    top = jnp.maximum(lse, lse_b)
    w, w_b = jnp.exp2(lse - top), jnp.exp2(lse_b - top)
    total = w + w_b
    return top + jnp.log2(total), (w * delta + w_b * delta_b) / total


def tiles_loop(full, count, step):
    def body(size, masked):
        def run(i, carry):
            for v in range(size):
                step(i * size + v, v, masked)
            return carry

        return run

    bodies = full // MANY
    lax.fori_loop(0, bodies, body(MANY, False), 0)
    lax.fori_loop(bodies * (MANY // SOME), count // SOME, body(SOME, True), 0)
    lax.fori_loop(count // SOME * (SOME // FEW), (count + FEW - 1) // FEW, body(FEW, True), 0)


def load_sorted(meta, kvs, kv_s):
    for s in range(64):
        r = aligned(meta[IN + s], SPAN)
        t = slice((s % 2) * SPAN, (s % 2 + 1) * SPAN)
        kv_s[pl.ds(r, SPAN), :] = kvs[s // 8][(s // 2) % 4, t, :]


def row_of(place, h):
    odd = place % 2
    inner = odd * 512 + h * SPAN if h < 4 else R + odd * 128 + (h - 4) * SPAN
    return pl.multiple_of((place // 2) * 768 + inner, SPAN)


def load_rows(meta, base, qds, q_s, do_s, first=0):
    for d, ref in enumerate(qds):
        for half in range(2):
            place = meta[base + UNIT + 2 * (first + d) + half]
            t = slice(half * SPAN, (half + 1) * SPAN)
            for h in range(HEADS):
                r = row_of(place, h)
                q_s[pl.ds(r, SPAN), :] = ref[t, h * HD : (h + 1) * HD]
                do_s[pl.ds(r, SPAN), :] = ref[t, WIDE + h * HD : WIDE + (h + 1) * HD]
    rows = 3 * R * len(qds)
    q_s[rows : rows + R, :] = jnp.zeros((R, HD), q_s.dtype)
    do_s[rows : rows + R, :] = jnp.zeros((R, HD), do_s.dtype)


def products(meta, base, t, q_s, do_s, kv_s, s_b, dp_b):
    r, k = aligned(meta[base + GROUP + t], R), aligned(meta[base + BLOCK + t], KB)
    s_b[...] = dot(kv_s[pl.ds(k, KB), :HD], q_s[pl.ds(r, R), :], NT)
    dp_b[...] = dot(kv_s[pl.ds(k, KB), HD:], do_s[pl.ds(r, R), :], NT)


HALVES = ((0, 1), (2, 5), (3, 4))


def stats_kernel(which, devices, meta, lim, *refs):
    qds, kvs = refs[:devices], refs[devices : devices + 8]
    rest = refs[devices + 8 :]
    if which == FAR:
        before, rest = rest[0], rest[1:]
    out, q_s, do_s, kv_s, s0, s1, dp0, dp1, m_s, l_s, d_s = rest
    base, groups = of(which), 3 * devices
    load_sorted(meta, kvs, kv_s)
    load_rows(meta, base, qds, q_s, do_s, first=3 if which == FAR else 0)
    m_s[...] = jnp.full_like(m_s, NEG)
    l_s[...] = jnp.zeros_like(l_s)
    d_s[...] = jnp.zeros_like(d_s)
    iota = lax.broadcasted_iota(jnp.int32, (KB, R), 0)

    def online(t, s_b, dp_b, masked):
        g = meta[base + GROUP + t]
        rows = [slice(8 * i, 8 * i + 8) for i in range(KB // 8)]
        s = [s_b[r, :] * C2 for r in rows]
        if masked:
            limit = lim[which, pl.ds(g, 1), :] - meta[base + BLOCK + t] * KB
            s = [jnp.where(iota[r] < limit, x, NEG) for r, x in zip(rows, s)]
        m = m_s[g]
        top = jnp.maximum(m, tree(jnp.maximum, s))
        a = jnp.exp2(m - top)
        e = [jnp.exp2(x - top) for x in s]
        m_s[g] = top
        l_s[g] = l_s[g] * a + tree(jnp.add, e)
        d_s[g] = d_s[g] * a + tree(jnp.add, [x * dp_b[r, :] for r, x in zip(rows, e)])

    ss, dps = (s0, s1), (dp0, dp1)
    products(meta, base, 0, q_s, do_s, kv_s, s0, dp0)

    def step(t, v, masked):
        products(meta, base, t + 1, q_s, do_s, kv_s, ss[(v + 1) % 2], dps[(v + 1) % 2])
        online(t, ss[v % 2], dps[v % 2], masked)

    tiles_loop(meta[base + FULL], meta[base + COUNT], step)
    out[...] = before[...] if which == FAR else jnp.zeros_like(out)
    for g in range(groups):
        m = m_s[g]
        live = jnp.where(m > 0.5 * NEG, 1.0, 0.0)
        top = jnp.max(m, axis=0, keepdims=True)
        a = jnp.exp2(m - top) * live
        ll = jnp.sum(l_s[g] * a, axis=0, keepdims=True)
        dd = jnp.sum(d_s[g] * a, axis=0, keepdims=True)
        safe = jnp.where(ll > 0, ll, 1.0)
        lse = jnp.where(ll > 0, top + jnp.log2(safe), NEG)
        for half in range(2):
            place, pair = divmod(HALVES[g % 3][half], 3)
            row = meta[base + CANON + g // 3 * 2 + place] * 3 + pair
            at = slice(half * 128, half * 128 + 128)
            out[0, pl.ds(row, 1), :] = lse[:, at]
            out[1, pl.ds(row, 1), :] = (dd / safe)[:, at]


def grads_kernel(meta, lim, st0, st1, *refs):
    qds, kvs = refs[:4], refs[4:12]
    dqs, dkvs, dkv_other = refs[12:16], refs[16:20], refs[20]
    q_s, do_s, kv_s, s0, s1, dp0, dp1, acc, dq_s, p0, p1, ds0, ds1, lse, delta = refs[21:]
    load_sorted(meta, kvs, kv_s)
    base = of(ALL)
    load_rows(meta, base, qds, q_s, do_s)
    acc[...] = jnp.zeros_like(acc)
    dq_s[...] = jnp.zeros_like(dq_s)
    all_lse, all_delta = merged(st0[0], st0[1], st1[0], st1[1])
    lse[...] = jnp.zeros_like(lse)
    delta[...] = jnp.zeros_like(delta)
    for g in range(GROUPS):
        for half in range(2):
            row = g // 3 * 6 + HALVES[g % 3][half]
            at = slice(half * 128, half * 128 + 128)
            lse[g : g + 1, at] = all_lse[row : row + 1]
            delta[g : g + 1, at] = all_delta[row : row + 1]
    iota = lax.broadcasted_iota(jnp.int32, (KB, R), 0)

    def weights(t, s_b, dp_b, p_b, ds_b, masked):
        g = meta[base + GROUP + t]
        p = jnp.exp2(s_b[...] * C2 - lse[pl.ds(g, 1), :])
        if masked:
            limit = lim[ALL, pl.ds(g, 1), :] - meta[base + BLOCK + t] * KB
            p = jnp.where(iota < limit, p, 0.0)
        p_b[...] = p.astype(jnp.bfloat16)
        ds_b[...] = (p * (dp_b[...] - delta[pl.ds(g, 1), :])).astype(jnp.bfloat16)

    def sums(t, p_b, ds_b):
        r, k = aligned(meta[base + GROUP + t], R), aligned(meta[base + BLOCK + t], KB)
        dk = dot(ds_b[...], q_s[pl.ds(r, R), :], NN)
        dv = dot(p_b[...], do_s[pl.ds(r, R), :], NN)
        dq = dot(ds_b[...], kv_s[pl.ds(k, KB), :HD], TN)
        acc[pl.ds(k, KB), :HD] += dk
        acc[pl.ds(k, KB), HD:] += dv
        dq_s[pl.ds(r, R), :] += dq

    ss, dps, ps, dss = (s0, s1), (dp0, dp1), (p0, p1), (ds0, ds1)
    products(meta, base, 0, q_s, do_s, kv_s, s0, dp0)
    products(meta, base, 1, q_s, do_s, kv_s, s1, dp1)
    weights(0, s0, dp0, p0, ds0, True)

    def step(t, v, masked):
        a, b = v % 2, 1 - v % 2
        products(meta, base, t + 2, q_s, do_s, kv_s, ss[a], dps[a])
        weights(t + 1, ss[b], dps[b], ps[b], dss[b], masked or v == MANY - 1)
        sums(t, ps[a], dss[a])

    tiles_loop(meta[base + FULL], meta[base + COUNT], step)
    for d in range(4):
        for half in range(2):
            place = meta[base + UNIT + 2 * d + half]
            t = slice(half * SPAN, (half + 1) * SPAN)
            for h in range(HEADS):
                got = dq_s[pl.ds(row_of(place, h), SPAN), :] * SCALE
                dqs[d][t, h * HD : (h + 1) * HD] = got.astype(dqs[d].dtype)
    for s in range(64):
        r = aligned(meta[IN + s], SPAN)
        t = slice((s % 2) * SPAN, (s % 2 + 1) * SPAN)
        e = (s // 2) % 4
        ref = dkvs[s // 8] if s < 32 else dkv_other.at[s // 8 - 4]
        ref[e, t, :HD] = (acc[pl.ds(r, SPAN), :HD] * SCALE).astype(jnp.bfloat16)
        ref[e, t, HD:] = acc[pl.ds(r, SPAN), HD:].astype(jnp.bfloat16)


VM = pl.BlockSpec(memory_space=pltpu.VMEM)
SM = pl.BlockSpec(memory_space=pltpu.SMEM)
PARAMS = pltpu.CompilerParams(vmem_limit_bytes=48 * 2**20)
COPIES = [
    pltpu.VMEM(((GROUPS + 1) * R, HD), jnp.bfloat16),
    pltpu.VMEM(((GROUPS + 1) * R, HD), jnp.bfloat16),
    pltpu.VMEM((KEYS, 2 * HD), jnp.bfloat16),
] + [pltpu.VMEM((KB, R), jnp.float32)] * 4


def stats(which, meta, lim, qds, kvs, *before):
    n = len(qds)
    return pl.pallas_call(
        functools.partial(stats_kernel, which, n),
        out_shape=jax.ShapeDtypeStruct((2, 24, 128), jnp.float32),
        in_specs=[SM] + [VM] * (1 + n + 8 + len(before)),
        out_specs=VM,
        scratch_shapes=COPIES + [pltpu.VMEM((3 * n + 1, 8, R), jnp.float32)] * 3,
        compiler_params=PARAMS,
        cost_estimate=pl.CostEstimate(flops=n * 1_000_000, bytes_accessed=100_000, transcendentals=0),
        name="stats_near" if which == NEAR else "stats_far",
    )(meta, lim, *qds, *kvs, *before)


def grads(meta, lim, sts, arrays):
    dq = [jax.ShapeDtypeStruct((2 * SPAN, WIDE), t) for t in (jnp.float32,) + (jnp.bfloat16,) * 3]
    dkv = [jax.ShapeDtypeStruct((4, 2 * SPAN, 2 * HD), jnp.bfloat16)] * 4
    dkv += [jax.ShapeDtypeStruct((4, 4, 2 * SPAN, 2 * HD), jnp.bfloat16)]
    return pl.pallas_call(
        grads_kernel,
        out_shape=dq + dkv,
        in_specs=[SM] + [VM] * 15,
        out_specs=[VM] * 9,
        scratch_shapes=COPIES
        + [
            pltpu.VMEM((KEYS, 2 * HD), jnp.float32),
            pltpu.VMEM(((GROUPS + 1) * R, HD), jnp.float32),
        ]
        + [pltpu.VMEM((KB, R), jnp.bfloat16)] * 4
        + [pltpu.VMEM((16, R), jnp.float32)] * 2,
        compiler_params=PARAMS,
        name="grads",
    )(meta, lim, *sts, *arrays)


def permute(a, move):
    pairs = []
    for i in range(128):
        y, zl, core, zh, x = (int(c) for c in np.unravel_index(i, SIZES))
        y, z, core, x = (c % n for c, n in zip(move(y, 2 * zh + zl, core, x), (4, 4, 2, 4)))
        pairs.append((i, int(np.ravel_multi_index((y, z % 2, core, z // 2, x), SIZES))))
    return lax.ppermute(a, AXES, pairs)


def x_shift(a, step):
    return permute(a, lambda y, z, core, x: (y, z, core, x + step))


def first_shift(a, step):
    return permute(a, lambda y, z, core, x: (y, z + step, core, x) if core else (y + step, z, core, x))


def second_shift(a, step):
    return permute(a, lambda y, z, core, x: (y + step, z, core, x) if core else (y, z + step, core, x))


def core_swap(a):
    return permute(a, lambda y, z, core, x: (y, z, 1 - core, x))


def plan(span_slot):
    i32 = jnp.int32
    y, zl, core, zh, x = (lax.axis_index(a) for a in AXES)
    z = 2 * zh + zl
    i = jnp.arange(72, dtype=i32)
    is_key = i < 64
    low, high = (i // 2) % 4, (i // 8) % 4
    low, high = low ^ (low >> 1), high ^ (high >> 1)
    at_core = jnp.where(is_key & (i >= 32), 1 - core, core)
    at_y = jnp.where(is_key, (y - jnp.where(at_core == 0, low, high)) % 4, y)
    at_z = jnp.where(is_key, (z - jnp.where(at_core == 0, high, low)) % 4, z)
    at_x = jnp.where(is_key, x, (x - low) % 4)
    slot = ((((at_y * 2 + at_z % 2) * 2 + at_core) * 2 + at_z // 2) * 4 + at_x) * 2 + i % 2
    spans = jnp.sum(jnp.where(slot[:, None] == jnp.arange(256)[None, :], span_slot[None, :], 0), axis=1)
    arrived, queries = spans[:64], spans[64:]

    def rank(a, among):
        return jnp.sum((among[None, :] < a[:, None]).astype(i32), axis=1)

    place = rank(queries, queries)
    eight = jnp.arange(8, dtype=i32)
    hit = (place[None, :] == eight[:, None]).astype(i32)
    spans = jnp.sum(hit * queries[None, :], axis=1)
    below = rank(spans, arrived)
    own = jnp.any(arrived[None, :] == spans[:, None], axis=1).astype(i32)
    far = jnp.sum(hit[:, 6:], axis=1)
    before = jnp.sum(jnp.tril(jnp.ones((8, 8), i32), -1) * far[None, :], axis=1)
    order = jnp.stack([eight, jnp.where(far == 0, eight - before, 9), jnp.where(far == 1, before, 9)])
    taken = (order[:, None, :] == eight[None, :, None]).astype(i32)
    canon = jnp.sum(taken * eight, axis=2)
    units = jnp.sum(order[:, None, :] * hit.T[None], axis=2)
    token = jnp.tile(jnp.arange(SPAN, dtype=i32), 2)
    seen = below[:, None] * SPAN + own[:, None] * (token[None, :] + 1)
    seen = jnp.sum(taken[:, :, :, None] * seen[None, None], axis=2)
    a, b = seen[:, 0::2], seen[:, 1::2]
    lim = jnp.stack([a, a, a, b, b, b], axis=2).reshape(3, GROUPS, R)
    lim = jnp.concatenate([lim, jnp.zeros((3, 4, R), i32)], axis=1)
    most = (jnp.sum(taken * (below + own), axis=2) * SPAN + KB - 1) // KB
    least = jnp.sum(taken * below, axis=2) * SPAN // KB
    most = jnp.stack([most[:, 0::2], most[:, 1::2], most[:, 1::2]], axis=2).reshape(3, GROUPS)
    least = jnp.stack([least[:, 0::2], least[:, 0::2], least[:, 1::2]], axis=2).reshape(3, GROUPS)
    each = jnp.concatenate([least, most - least], axis=1)
    first = jnp.concatenate([jnp.zeros_like(least), least], axis=1)
    end = jnp.sum(jnp.tril(jnp.ones((2 * GROUPS, 2 * GROUPS), i32)) * each[:, None, :], axis=2)
    t = jnp.arange(LIST, dtype=i32)
    begin = end - each
    inside = ((t[None, :, None] >= begin[:, None, :]) & (t[None, :, None] < end[:, None, :])).astype(i32)
    number = jnp.tile(jnp.arange(GROUPS, dtype=i32), 2)
    group = jnp.sum(inside * number, axis=2)
    block = jnp.sum(inside * (t[None, :, None] - (begin - first)[:, None, :]), axis=2)
    group = jnp.where(t[None] < end[:, -1:], group, jnp.array([[12], [9], [3]], i32))
    lists = jnp.concatenate([units, canon, end[:, GROUPS - 1 : GROUPS], end[:, -1:], group, block], axis=1)
    return jnp.concatenate([rank(arrived, arrived), lists.reshape(-1)]).astype(i32), lim


def local(queries, keys, values, grad_out, span_slot):
    kv = jnp.concatenate([keys, values], axis=1)[None]
    kv = jnp.concatenate([kv] + [first_shift(kv, r) for r in STEPS[1:]], axis=0)
    kvs = [kv] + [second_shift(kv, r) for r in STEPS[1:]]
    qd = jnp.concatenate([queries, grad_out], axis=1)
    near = [qd, x_shift(qd, 1), x_shift(qd, 3)]
    near[1], near[2], later = lax.optimization_barrier((near[1], near[2], qd))
    far = x_shift(later, 2)
    kvs[0], kvs[1], span_slot = lax.optimization_barrier((kvs[0], kvs[1], span_slot))
    meta, lim = plan(span_slot)
    kvs = kvs + [core_swap(a) for a in kvs]
    arrays = near + [far] + kvs

    part = stats(NEAR, meta, lim, near, kvs)
    part = stats(FAR, meta, lim, [far], kvs, part)
    got = permute(part, lambda y, z, core, x: (y, z, core, x ^ 1))
    part = jnp.stack(merged(part[0], part[1], got[0], got[1]))
    got = permute(part, lambda y, z, core, x: (y, z, core, x ^ 2))
    results = grads(meta, lim, (part, got), arrays)
    dqs, dkv, dkv_other = results[:4], results[4:8], results[8]

    def total(*parts):
        out = parts[0].astype(jnp.float32)
        for part in parts[1:]:
            out = out + part.astype(jnp.float32)
        return out

    other = core_swap(dkv_other)
    pairs = [total(a, other[i]).astype(jnp.bfloat16) for i, a in enumerate(dkv)]
    some = total(pairs[0], *[second_shift(a, -r) for r, a in zip(STEPS[1:], pairs[1:])])
    dq = total(dqs[0], *[x_shift(a, -r) for r, a in zip(STEPS[1:], dqs[1:])])
    sent = [first_shift(some[i].astype(jnp.bfloat16), -r) for i, r in ((1, 1), (2, 3), (3, 2))]
    summed = total(some[0], *sent)
    return (
        dq.astype(jnp.bfloat16),
        summed[:, :HD].astype(jnp.bfloat16),
        summed[:, HD:].astype(jnp.bfloat16),
    )


def solution(mesh):
    fine = Mesh(mesh.devices.reshape(4, 2, 2, 2, 4), AXES)
    rows = P(AXES, None)
    return jax.shard_map(
        local,
        mesh=fine,
        in_specs=(rows, rows, rows, rows, P()),
        out_specs=(rows, rows, rows),
        check_vma=False,
    )
```

```python
import functools
import math

import jax
import jax.numpy as jnp
import numpy as np
from jax import lax
from jax.experimental import pallas as pl
from jax.experimental.pallas import tpu as pltpu
from jax.sharding import Mesh, PartitionSpec as P

AXES = ("y", "zl", "core", "zh", "x")
SIZES = (4, 2, 2, 2, 4)
STEPS = (0, 1, 3, 2)
NEG = -1e30
HD = 128
SCALE = 1.0 / math.sqrt(HD)
C2 = math.log2(math.e) * SCALE
SPAN = 64
HEADS = 6
WIDE = HEADS * HD
KEYS = 4096
KB = 256
R = 256
GROUPS = 12
MANY, SOME, FEW = 16, 8, 2
LIST = 144
IN = 0
ALL, NEAR, FAR = range(3)
UNIT, CANON, FULL, COUNT, GROUP = 0, 8, 16, 17, 18
BLOCK = GROUP + LIST
SIZE = BLOCK + LIST


def of(which):
    return 64 + which * SIZE


NT = (((1,), (1,)), ((), ()))
NN = (((1,), (0,)), ((), ()))
TN = (((0,), (0,)), ((), ()))


def dot(a, b, dims):
    return lax.dot_general(a, b, dims, preferred_element_type=jnp.float32)


def aligned(i, n):
    return pl.multiple_of(i * n, n)


def tree(op, xs):
    acc = list(xs[:4])
    for i, x in enumerate(xs[4:]):
        acc[i % 4] = op(acc[i % 4], x)
    return op(op(acc[0], acc[1]), op(acc[2], acc[3]))


def merged(lse, delta, lse_b, delta_b):
    top = jnp.maximum(lse, lse_b)
    w, w_b = jnp.exp2(lse - top), jnp.exp2(lse_b - top)
    total = w + w_b
    return top + jnp.log2(total), (w * delta + w_b * delta_b) / total


def tiles_loop(full, count, step):
    def body(size, masked):
        def run(i, carry):
            for v in range(size):
                step(i * size + v, v, masked)
            return carry

        return run

    bodies = full // MANY
    lax.fori_loop(0, bodies, body(MANY, False), 0)
    lax.fori_loop(bodies * (MANY // SOME), count // SOME, body(SOME, True), 0)
    lax.fori_loop(count // SOME * (SOME // FEW), (count + FEW - 1) // FEW, body(FEW, True), 0)


def load_sorted(meta, kvs, kv_s):
    for s in range(64):
        r = aligned(meta[IN + s], SPAN)
        t = slice((s % 2) * SPAN, (s % 2 + 1) * SPAN)
        kv_s[pl.ds(r, SPAN), :] = kvs[s // 8][(s // 2) % 4, t, :]


def row_of(place, h):
    odd = place % 2
    inner = odd * 512 + h * SPAN if h < 4 else R + odd * 128 + (h - 4) * SPAN
    return pl.multiple_of((place // 2) * 768 + inner, SPAN)


def load_rows(meta, base, qds, q_s, do_s, first=0):
    for d, ref in enumerate(qds):
        for half in range(2):
            place = meta[base + UNIT + 2 * (first + d) + half]
            t = slice(half * SPAN, (half + 1) * SPAN)
            for h in range(HEADS):
                r = row_of(place, h)
                q_s[pl.ds(r, SPAN), :] = ref[t, h * HD : (h + 1) * HD]
                do_s[pl.ds(r, SPAN), :] = ref[t, WIDE + h * HD : WIDE + (h + 1) * HD]
    rows = 3 * R * len(qds)
    q_s[rows : rows + R, :] = jnp.zeros((R, HD), q_s.dtype)
    do_s[rows : rows + R, :] = jnp.zeros((R, HD), do_s.dtype)


def products(meta, base, t, q_s, do_s, kv_s, s_b, dp_b):
    r, k = aligned(meta[base + GROUP + t], R), aligned(meta[base + BLOCK + t], KB)
    s_b[...] = dot(kv_s[pl.ds(k, KB), :HD], q_s[pl.ds(r, R), :], NT)
    dp_b[...] = dot(kv_s[pl.ds(k, KB), HD:], do_s[pl.ds(r, R), :], NT)


HALVES = ((0, 1), (2, 5), (3, 4))


def stats_kernel(which, devices, meta, lim, *refs):
    qds, kvs = refs[:devices], refs[devices : devices + 8]
    rest = refs[devices + 8 :]
    if which == FAR:
        before, rest = rest[0], rest[1:]
    out, q_s, do_s, kv_s, s0, s1, dp0, dp1, m_s, l_s, d_s = rest
    base, groups = of(which), 3 * devices
    load_sorted(meta, kvs, kv_s)
    load_rows(meta, base, qds, q_s, do_s, first=3 if which == FAR else 0)
    m_s[...] = jnp.full_like(m_s, NEG)
    l_s[...] = jnp.zeros_like(l_s)
    d_s[...] = jnp.zeros_like(d_s)
    iota = lax.broadcasted_iota(jnp.int32, (KB, R), 0)

    def online(t, s_b, dp_b, masked):
        g = meta[base + GROUP + t]
        rows = [slice(8 * i, 8 * i + 8) for i in range(KB // 8)]
        s = [s_b[r, :] * C2 for r in rows]
        if masked:
            limit = lim[which, pl.ds(g, 1), :] - meta[base + BLOCK + t] * KB
            s = [jnp.where(iota[r] < limit, x, NEG) for r, x in zip(rows, s)]
        m = m_s[g]
        top = jnp.maximum(m, tree(jnp.maximum, s))
        a = jnp.exp2(m - top)
        e = [jnp.exp2(x - top) for x in s]
        m_s[g] = top
        l_s[g] = l_s[g] * a + tree(jnp.add, e)
        d_s[g] = d_s[g] * a + tree(jnp.add, [x * dp_b[r, :] for r, x in zip(rows, e)])

    ss, dps = (s0, s1), (dp0, dp1)
    products(meta, base, 0, q_s, do_s, kv_s, s0, dp0)

    def step(t, v, masked):
        products(meta, base, t + 1, q_s, do_s, kv_s, ss[(v + 1) % 2], dps[(v + 1) % 2])
        online(t, ss[v % 2], dps[v % 2], masked)

    tiles_loop(meta[base + FULL], meta[base + COUNT], step)
    out[...] = before[...] if which == FAR else jnp.zeros_like(out)
    for g in range(groups):
        m = m_s[g]
        live = jnp.where(m > 0.5 * NEG, 1.0, 0.0)
        top = jnp.max(m, axis=0, keepdims=True)
        a = jnp.exp2(m - top) * live
        ll = jnp.sum(l_s[g] * a, axis=0, keepdims=True)
        dd = jnp.sum(d_s[g] * a, axis=0, keepdims=True)
        safe = jnp.where(ll > 0, ll, 1.0)
        lse = jnp.where(ll > 0, top + jnp.log2(safe), NEG)
        for half in range(2):
            place, pair = divmod(HALVES[g % 3][half], 3)
            row = meta[base + CANON + g // 3 * 2 + place] * 3 + pair
            at = slice(half * 128, half * 128 + 128)
            out[0, pl.ds(row, 1), :] = lse[:, at]
            out[1, pl.ds(row, 1), :] = (dd / safe)[:, at]


def grads_kernel(meta, lim, st0, st1, *refs):
    qds, kvs = refs[:4], refs[4:12]
    dqs, dkvs, dkv_other = refs[12:16], refs[16:20], refs[20]
    q_s, do_s, kv_s, s0, s1, dp0, dp1, acc, dq_s, p0, p1, ds0, ds1, lse, delta = refs[21:]
    load_sorted(meta, kvs, kv_s)
    base = of(ALL)
    load_rows(meta, base, qds, q_s, do_s)
    acc[...] = jnp.zeros_like(acc)
    dq_s[...] = jnp.zeros_like(dq_s)
    all_lse, all_delta = merged(st0[0], st0[1], st1[0], st1[1])
    lse[...] = jnp.zeros_like(lse)
    delta[...] = jnp.zeros_like(delta)
    for g in range(GROUPS):
        for half in range(2):
            row = g // 3 * 6 + HALVES[g % 3][half]
            at = slice(half * 128, half * 128 + 128)
            lse[g : g + 1, at] = all_lse[row : row + 1]
            delta[g : g + 1, at] = all_delta[row : row + 1]
    iota = lax.broadcasted_iota(jnp.int32, (KB, R), 0)

    def weights(t, s_b, dp_b, p_b, ds_b, masked):
        g = meta[base + GROUP + t]
        p = jnp.exp2(s_b[...] * C2 - lse[pl.ds(g, 1), :])
        if masked:
            limit = lim[ALL, pl.ds(g, 1), :] - meta[base + BLOCK + t] * KB
            p = jnp.where(iota < limit, p, 0.0)
        p_b[...] = p.astype(jnp.bfloat16)
        ds_b[...] = (p * (dp_b[...] - delta[pl.ds(g, 1), :])).astype(jnp.bfloat16)

    def sums(t, p_b, ds_b):
        r, k = aligned(meta[base + GROUP + t], R), aligned(meta[base + BLOCK + t], KB)
        dk = dot(ds_b[...], q_s[pl.ds(r, R), :], NN)
        dv = dot(p_b[...], do_s[pl.ds(r, R), :], NN)
        dq = dot(ds_b[...], kv_s[pl.ds(k, KB), :HD], TN)
        acc[pl.ds(k, KB), :HD] += dk
        acc[pl.ds(k, KB), HD:] += dv
        dq_s[pl.ds(r, R), :] += dq

    ss, dps, ps, dss = (s0, s1), (dp0, dp1), (p0, p1), (ds0, ds1)
    products(meta, base, 0, q_s, do_s, kv_s, s0, dp0)
    products(meta, base, 1, q_s, do_s, kv_s, s1, dp1)
    weights(0, s0, dp0, p0, ds0, True)

    def step(t, v, masked):
        a, b = v % 2, 1 - v % 2
        products(meta, base, t + 2, q_s, do_s, kv_s, ss[a], dps[a])
        weights(t + 1, ss[b], dps[b], ps[b], dss[b], masked or v == MANY - 1)
        sums(t, ps[a], dss[a])

    tiles_loop(meta[base + FULL], meta[base + COUNT], step)
    for d in range(4):
        for half in range(2):
            place = meta[base + UNIT + 2 * d + half]
            t = slice(half * SPAN, (half + 1) * SPAN)
            for h in range(HEADS):
                got = dq_s[pl.ds(row_of(place, h), SPAN), :] * SCALE
                dqs[d][t, h * HD : (h + 1) * HD] = got.astype(dqs[d].dtype)
    for s in range(64):
        r = aligned(meta[IN + s], SPAN)
        t = slice((s % 2) * SPAN, (s % 2 + 1) * SPAN)
        e = (s // 2) % 4
        ref = dkvs[s // 8] if s < 32 else dkv_other.at[s // 8 - 4]
        ref[e, t, :HD] = (acc[pl.ds(r, SPAN), :HD] * SCALE).astype(jnp.bfloat16)
        ref[e, t, HD:] = acc[pl.ds(r, SPAN), HD:].astype(jnp.bfloat16)


VM = pl.BlockSpec(memory_space=pltpu.VMEM)
SM = pl.BlockSpec(memory_space=pltpu.SMEM)
PARAMS = pltpu.CompilerParams(vmem_limit_bytes=48 * 2**20)
COPIES = [
    pltpu.VMEM(((GROUPS + 1) * R, HD), jnp.bfloat16),
    pltpu.VMEM(((GROUPS + 1) * R, HD), jnp.bfloat16),
    pltpu.VMEM((KEYS, 2 * HD), jnp.bfloat16),
] + [pltpu.VMEM((KB, R), jnp.float32)] * 4


def stats(which, meta, lim, qds, kvs, *before):
    n = len(qds)
    return pl.pallas_call(
        functools.partial(stats_kernel, which, n),
        out_shape=jax.ShapeDtypeStruct((2, 24, 128), jnp.float32),
        in_specs=[SM] + [VM] * (1 + n + 8 + len(before)),
        out_specs=VM,
        scratch_shapes=COPIES + [pltpu.VMEM((3 * n + 1, 8, R), jnp.float32)] * 3,
        compiler_params=PARAMS,
        cost_estimate=pl.CostEstimate(flops=n * 1_000_000, bytes_accessed=100_000, transcendentals=0),
        name="stats_near" if which == NEAR else "stats_far",
    )(meta, lim, *qds, *kvs, *before)


def grads(meta, lim, sts, arrays):
    dq = [jax.ShapeDtypeStruct((2 * SPAN, WIDE), t) for t in (jnp.float32,) + (jnp.bfloat16,) * 3]
    dkv = [jax.ShapeDtypeStruct((4, 2 * SPAN, 2 * HD), jnp.bfloat16)] * 4
    dkv += [jax.ShapeDtypeStruct((4, 4, 2 * SPAN, 2 * HD), jnp.bfloat16)]
    return pl.pallas_call(
        grads_kernel,
        out_shape=dq + dkv,
        in_specs=[SM] + [VM] * 15,
        out_specs=[VM] * 9,
        scratch_shapes=COPIES
        + [
            pltpu.VMEM((KEYS, 2 * HD), jnp.float32),
            pltpu.VMEM(((GROUPS + 1) * R, HD), jnp.float32),
        ]
        + [pltpu.VMEM((KB, R), jnp.bfloat16)] * 4
        + [pltpu.VMEM((16, R), jnp.float32)] * 2,
        compiler_params=PARAMS,
        name="grads",
    )(meta, lim, *sts, *arrays)


def permute(a, move):
    pairs = []
    for i in range(128):
        y, zl, core, zh, x = (int(c) for c in np.unravel_index(i, SIZES))
        y, z, core, x = (c % n for c, n in zip(move(y, 2 * zh + zl, core, x), (4, 4, 2, 4)))
        pairs.append((i, int(np.ravel_multi_index((y, z % 2, core, z // 2, x), SIZES))))
    return lax.ppermute(a, AXES, pairs)


def x_shift(a, step):
    return permute(a, lambda y, z, core, x: (y, z, core, x + step))


def first_shift(a, step):
    return permute(a, lambda y, z, core, x: (y, z + step, core, x) if core else (y + step, z, core, x))


def second_shift(a, step):
    return permute(a, lambda y, z, core, x: (y + step, z, core, x) if core else (y, z + step, core, x))


def core_swap(a):
    return permute(a, lambda y, z, core, x: (y, z, 1 - core, x))


def plan(span_slot):
    i32 = jnp.int32
    y, zl, core, zh, x = (lax.axis_index(a) for a in AXES)
    z = 2 * zh + zl
    i = jnp.arange(72, dtype=i32)
    is_key = i < 64
    low, high = (i // 2) % 4, (i // 8) % 4
    low, high = low ^ (low >> 1), high ^ (high >> 1)
    at_core = jnp.where(is_key & (i >= 32), 1 - core, core)
    at_y = jnp.where(is_key, (y - jnp.where(at_core == 0, low, high)) % 4, y)
    at_z = jnp.where(is_key, (z - jnp.where(at_core == 0, high, low)) % 4, z)
    at_x = jnp.where(is_key, x, (x - low) % 4)
    slot = ((((at_y * 2 + at_z % 2) * 2 + at_core) * 2 + at_z // 2) * 4 + at_x) * 2 + i % 2
    spans = jnp.sum(jnp.where(slot[:, None] == jnp.arange(256)[None, :], span_slot[None, :], 0), axis=1)
    arrived, queries = spans[:64], spans[64:]

    def rank(a, among):
        return jnp.sum((among[None, :] < a[:, None]).astype(i32), axis=1)

    place = rank(queries, queries)
    eight = jnp.arange(8, dtype=i32)
    hit = (place[None, :] == eight[:, None]).astype(i32)
    spans = jnp.sum(hit * queries[None, :], axis=1)
    below = rank(spans, arrived)
    own = jnp.any(arrived[None, :] == spans[:, None], axis=1).astype(i32)
    far = jnp.sum(hit[:, 6:], axis=1)
    before = jnp.sum(jnp.tril(jnp.ones((8, 8), i32), -1) * far[None, :], axis=1)
    order = jnp.stack([eight, jnp.where(far == 0, eight - before, 9), jnp.where(far == 1, before, 9)])
    taken = (order[:, None, :] == eight[None, :, None]).astype(i32)
    canon = jnp.sum(taken * eight, axis=2)
    units = jnp.sum(order[:, None, :] * hit.T[None], axis=2)
    token = jnp.tile(jnp.arange(SPAN, dtype=i32), 2)
    seen = below[:, None] * SPAN + own[:, None] * (token[None, :] + 1)
    seen = jnp.sum(taken[:, :, :, None] * seen[None, None], axis=2)
    a, b = seen[:, 0::2], seen[:, 1::2]
    lim = jnp.stack([a, a, a, b, b, b], axis=2).reshape(3, GROUPS, R)
    lim = jnp.concatenate([lim, jnp.zeros((3, 4, R), i32)], axis=1)
    most = (jnp.sum(taken * (below + own), axis=2) * SPAN + KB - 1) // KB
    least = jnp.sum(taken * below, axis=2) * SPAN // KB
    most = jnp.stack([most[:, 0::2], most[:, 1::2], most[:, 1::2]], axis=2).reshape(3, GROUPS)
    least = jnp.stack([least[:, 0::2], least[:, 0::2], least[:, 1::2]], axis=2).reshape(3, GROUPS)
    each = jnp.concatenate([least, most - least], axis=1)
    first = jnp.concatenate([jnp.zeros_like(least), least], axis=1)
    end = jnp.sum(jnp.tril(jnp.ones((2 * GROUPS, 2 * GROUPS), i32)) * each[:, None, :], axis=2)
    t = jnp.arange(LIST, dtype=i32)
    begin = end - each
    inside = ((t[None, :, None] >= begin[:, None, :]) & (t[None, :, None] < end[:, None, :])).astype(i32)
    number = jnp.tile(jnp.arange(GROUPS, dtype=i32), 2)
    group = jnp.sum(inside * number, axis=2)
    block = jnp.sum(inside * (t[None, :, None] - (begin - first)[:, None, :]), axis=2)
    which = jnp.arange(3, dtype=i32)[:, None]
    group = jnp.where(t[None] < end[:, -1:], group, jnp.where(which == ALL, 12, jnp.where(which == NEAR, 9, 3)))
    lists = jnp.concatenate([units, canon, end[:, GROUPS - 1 : GROUPS], end[:, -1:], group, block], axis=1)
    return jnp.concatenate([rank(arrived, arrived), lists.reshape(-1)]).astype(i32), lim


def local(queries, keys, values, grad_out, span_slot):
    kv = jnp.concatenate([keys, values], axis=1)[None]
    kv = jnp.concatenate([kv] + [first_shift(kv, r) for r in STEPS[1:]], axis=0)
    kvs = [kv] + [second_shift(kv, r) for r in STEPS[1:]]
    qd = jnp.concatenate([queries, grad_out], axis=1)
    near = [qd, x_shift(qd, 1), x_shift(qd, 3)]
    near[1], near[2], later = lax.optimization_barrier((near[1], near[2], qd))
    far = x_shift(later, 2)
    kvs[0], kvs[1], span_slot = lax.optimization_barrier((kvs[0], kvs[1], span_slot))
    meta, lim = plan(span_slot)
    kvs = kvs + [core_swap(a) for a in kvs]
    arrays = near + [far] + kvs

    part = stats(NEAR, meta, lim, near, kvs)
    part = stats(FAR, meta, lim, [far], kvs, part)
    got = permute(part, lambda y, z, core, x: (y, z, core, x ^ 1))
    part = jnp.stack(merged(part[0], part[1], got[0], got[1]))
    got = permute(part, lambda y, z, core, x: (y, z, core, x ^ 2))
    results = grads(meta, lim, (part, got), arrays)
    dqs, dkv, dkv_other = results[:4], results[4:8], results[8]

    def total(*parts):
        out = parts[0].astype(jnp.float32)
        for part in parts[1:]:
            out = out + part.astype(jnp.float32)
        return out

    other = core_swap(dkv_other)
    pairs = [total(a, other[i]).astype(jnp.bfloat16) for i, a in enumerate(dkv)]
    some = total(pairs[0], *[second_shift(a, -r) for r, a in zip(STEPS[1:], pairs[1:])])
    dq = total(dqs[0], *[x_shift(a, -r) for r, a in zip(STEPS[1:], dqs[1:])])
    sent = [first_shift(some[i].astype(jnp.bfloat16), -r) for i, r in ((1, 1), (2, 3), (3, 2))]
    summed = total(some[0], *sent)
    return (
        dq.astype(jnp.bfloat16),
        summed[:, :HD].astype(jnp.bfloat16),
        summed[:, HD:].astype(jnp.bfloat16),
    )


def solution(mesh):
    fine = Mesh(mesh.devices.reshape(4, 2, 2, 2, 4), AXES)
    rows = P(AXES, None)
    return jax.shard_map(
        local,
        mesh=fine,
        in_specs=(rows, rows, rows, rows, P()),
        out_specs=(rows, rows, rows),
        check_vma=False,
    )
```

```python
import functools
import math

import jax
import jax.numpy as jnp
import numpy as np
from jax import lax
from jax.experimental import pallas as pl
from jax.experimental.pallas import tpu as pltpu
from jax.sharding import Mesh, PartitionSpec as P

AXES = ("y", "zl", "core", "zh", "x")
SIZES = (4, 2, 2, 2, 4)
STEPS = (0, 1, 3, 2)
NEG = -1e30
HD = 128
SCALE = 1.0 / math.sqrt(HD)
C2 = math.log2(math.e) * SCALE
SPAN = 64
HEADS = 6
WIDE = HEADS * HD
KEYS = 4096
KB = 256
R = 256
GROUPS = 12
MANY, SOME, FEW = 16, 8, 2
LIST = 144
IN = 0
ALL, NEAR, FAR = range(3)
UNIT, CANON, FULL, COUNT, GROUP = 0, 8, 16, 17, 18
BLOCK = GROUP + LIST
SIZE = BLOCK + LIST


def of(which):
    return 64 + which * SIZE


NT = (((1,), (1,)), ((), ()))
NN = (((1,), (0,)), ((), ()))
TN = (((0,), (0,)), ((), ()))


def dot(a, b, dims):
    return lax.dot_general(a, b, dims, preferred_element_type=jnp.float32)


def aligned(i, n):
    return pl.multiple_of(i * n, n)


def tree(op, xs):
    acc = list(xs[:4])
    for i, x in enumerate(xs[4:]):
        acc[i % 4] = op(acc[i % 4], x)
    return op(op(acc[0], acc[1]), op(acc[2], acc[3]))


def merged(lse, delta, lse_b, delta_b):
    top = jnp.maximum(lse, lse_b)
    w, w_b = jnp.exp2(lse - top), jnp.exp2(lse_b - top)
    total = w + w_b
    return top + jnp.log2(total), (w * delta + w_b * delta_b) / total


def tiles_loop(full, count, step):
    def body(size, masked):
        def run(i, carry):
            for v in range(size):
                step(i * size + v, v, masked)
            return carry

        return run

    bodies = full // MANY
    lax.fori_loop(0, bodies, body(MANY, False), 0)
    lax.fori_loop(bodies * (MANY // SOME), count // SOME, body(SOME, True), 0)
    lax.fori_loop(count // SOME * (SOME // FEW), (count + FEW - 1) // FEW, body(FEW, True), 0)


def load_sorted(meta, kvs, kv_s):
    for s in range(64):
        r = aligned(meta[IN + s], SPAN)
        t = slice((s % 2) * SPAN, (s % 2 + 1) * SPAN)
        kv_s[pl.ds(r, SPAN), :] = kvs[s // 8][(s // 2) % 4, t, :]


def row_of(place, h):
    odd = place % 2
    inner = odd * 512 + h * SPAN if h < 4 else R + odd * 128 + (h - 4) * SPAN
    return pl.multiple_of((place // 2) * 768 + inner, SPAN)


def load_rows(meta, base, qds, q_s, do_s, first=0):
    for d, ref in enumerate(qds):
        for half in range(2):
            place = meta[base + UNIT + 2 * (first + d) + half]
            t = slice(half * SPAN, (half + 1) * SPAN)
            for h in range(HEADS):
                r = row_of(place, h)
                q_s[pl.ds(r, SPAN), :] = ref[t, h * HD : (h + 1) * HD]
                do_s[pl.ds(r, SPAN), :] = ref[t, WIDE + h * HD : WIDE + (h + 1) * HD]
    rows = 3 * R * len(qds)
    q_s[rows : rows + R, :] = jnp.zeros((R, HD), q_s.dtype)
    do_s[rows : rows + R, :] = jnp.zeros((R, HD), do_s.dtype)


def products(meta, base, t, q_s, do_s, kv_s, s_b, dp_b):
    r, k = aligned(meta[base + GROUP + t], R), aligned(meta[base + BLOCK + t], KB)
    s_b[...] = dot(kv_s[pl.ds(k, KB), :HD], q_s[pl.ds(r, R), :], NT)
    dp_b[...] = dot(kv_s[pl.ds(k, KB), HD:], do_s[pl.ds(r, R), :], NT)


HALVES = ((0, 1), (2, 5), (3, 4))


def stats_kernel(which, devices, meta, lim, *refs):
    qds, kvs = refs[:devices], refs[devices : devices + 8]
    rest = refs[devices + 8 :]
    if which == FAR:
        before, rest = rest[0], rest[1:]
    out, q_s, do_s, kv_s, s0, s1, dp0, dp1, m_s, l_s, d_s = rest
    base, groups = of(which), 3 * devices
    load_sorted(meta, kvs, kv_s)
    load_rows(meta, base, qds, q_s, do_s, first=3 if which == FAR else 0)
    m_s[...] = jnp.full_like(m_s, NEG)
    l_s[...] = jnp.zeros_like(l_s)
    d_s[...] = jnp.zeros_like(d_s)
    iota = lax.broadcasted_iota(jnp.int32, (KB, R), 0)

    def online(t, s_b, dp_b, masked):
        g = meta[base + GROUP + t]
        rows = [slice(8 * i, 8 * i + 8) for i in range(KB // 8)]
        s = [s_b[r, :] * C2 for r in rows]
        if masked:
            limit = lim[which, pl.ds(g, 1), :] - meta[base + BLOCK + t] * KB
            s = [jnp.where(iota[r] < limit, x, NEG) for r, x in zip(rows, s)]
        m = m_s[g]
        top = jnp.maximum(m, tree(jnp.maximum, s))
        a = jnp.exp2(m - top)
        e = [jnp.exp2(x - top) for x in s]
        m_s[g] = top
        l_s[g] = l_s[g] * a + tree(jnp.add, e)
        d_s[g] = d_s[g] * a + tree(jnp.add, [x * dp_b[r, :] for r, x in zip(rows, e)])

    ss, dps = (s0, s1), (dp0, dp1)
    products(meta, base, 0, q_s, do_s, kv_s, s0, dp0)

    def step(t, v, masked):
        products(meta, base, t + 1, q_s, do_s, kv_s, ss[(v + 1) % 2], dps[(v + 1) % 2])
        online(t, ss[v % 2], dps[v % 2], masked)

    tiles_loop(meta[base + FULL], meta[base + COUNT], step)
    out[...] = before[...] if which == FAR else jnp.zeros_like(out)
    for g in range(groups):
        m = m_s[g]
        live = jnp.where(m > 0.5 * NEG, 1.0, 0.0)
        top = jnp.max(m, axis=0, keepdims=True)
        a = jnp.exp2(m - top) * live
        ll = jnp.sum(l_s[g] * a, axis=0, keepdims=True)
        dd = jnp.sum(d_s[g] * a, axis=0, keepdims=True)
        safe = jnp.where(ll > 0, ll, 1.0)
        lse = jnp.where(ll > 0, top + jnp.log2(safe), NEG)
        for half in range(2):
            place, pair = divmod(HALVES[g % 3][half], 3)
            row = meta[base + CANON + g // 3 * 2 + place] * 3 + pair
            at = slice(half * 128, half * 128 + 128)
            out[0, pl.ds(row, 1), :] = lse[:, at]
            out[1, pl.ds(row, 1), :] = (dd / safe)[:, at]


def grads_kernel(meta, lim, st0, st1, st2, st3, *refs):
    qds, kvs = refs[:4], refs[4:12]
    dqs, dkvs, dkv_other = refs[12:16], refs[16:20], refs[20]
    q_s, do_s, kv_s, s0, s1, dp0, dp1, acc, dq_s, p0, p1, ds0, ds1, lse, delta = refs[21:]
    load_sorted(meta, kvs, kv_s)
    base = of(ALL)
    load_rows(meta, base, qds, q_s, do_s)
    acc[...] = jnp.zeros_like(acc)
    dq_s[...] = jnp.zeros_like(dq_s)
    left, right = merged(st0[0], st0[1], st1[0], st1[1]), merged(st2[0], st2[1], st3[0], st3[1])
    all_lse, all_delta = merged(*left, *right)
    lse[...] = jnp.zeros_like(lse)
    delta[...] = jnp.zeros_like(delta)
    for g in range(GROUPS):
        for half in range(2):
            row = g // 3 * 6 + HALVES[g % 3][half]
            at = slice(half * 128, half * 128 + 128)
            lse[g : g + 1, at] = all_lse[row : row + 1]
            delta[g : g + 1, at] = all_delta[row : row + 1]
    iota = lax.broadcasted_iota(jnp.int32, (KB, R), 0)

    def weights(t, s_b, dp_b, p_b, ds_b, masked):
        g = meta[base + GROUP + t]
        p = jnp.exp2(s_b[...] * C2 - lse[pl.ds(g, 1), :])
        if masked:
            limit = lim[ALL, pl.ds(g, 1), :] - meta[base + BLOCK + t] * KB
            p = jnp.where(iota < limit, p, 0.0)
        p_b[...] = p.astype(jnp.bfloat16)
        ds_b[...] = (p * (dp_b[...] - delta[pl.ds(g, 1), :])).astype(jnp.bfloat16)

    def sums(t, p_b, ds_b):
        r, k = aligned(meta[base + GROUP + t], R), aligned(meta[base + BLOCK + t], KB)
        dk = dot(ds_b[...], q_s[pl.ds(r, R), :], NN)
        dv = dot(p_b[...], do_s[pl.ds(r, R), :], NN)
        dq = dot(ds_b[...], kv_s[pl.ds(k, KB), :HD], TN)
        acc[pl.ds(k, KB), :HD] += dk
        acc[pl.ds(k, KB), HD:] += dv
        dq_s[pl.ds(r, R), :] += dq

    ss, dps, ps, dss = (s0, s1), (dp0, dp1), (p0, p1), (ds0, ds1)
    products(meta, base, 0, q_s, do_s, kv_s, s0, dp0)
    products(meta, base, 1, q_s, do_s, kv_s, s1, dp1)
    weights(0, s0, dp0, p0, ds0, True)

    def step(t, v, masked):
        a, b = v % 2, 1 - v % 2
        products(meta, base, t + 2, q_s, do_s, kv_s, ss[a], dps[a])
        weights(t + 1, ss[b], dps[b], ps[b], dss[b], masked or v == MANY - 1)
        sums(t, ps[a], dss[a])

    tiles_loop(meta[base + FULL], meta[base + COUNT], step)
    for d in range(4):
        for half in range(2):
            place = meta[base + UNIT + 2 * d + half]
            t = slice(half * SPAN, (half + 1) * SPAN)
            for h in range(HEADS):
                got = dq_s[pl.ds(row_of(place, h), SPAN), :] * SCALE
                dqs[d][t, h * HD : (h + 1) * HD] = got.astype(dqs[d].dtype)
    for s in range(64):
        r = aligned(meta[IN + s], SPAN)
        t = slice((s % 2) * SPAN, (s % 2 + 1) * SPAN)
        e = (s // 2) % 4
        ref = dkvs[s // 8] if s < 32 else dkv_other.at[s // 8 - 4]
        ref[e, t, :HD] = (acc[pl.ds(r, SPAN), :HD] * SCALE).astype(jnp.bfloat16)
        ref[e, t, HD:] = acc[pl.ds(r, SPAN), HD:].astype(jnp.bfloat16)


VM = pl.BlockSpec(memory_space=pltpu.VMEM)
SM = pl.BlockSpec(memory_space=pltpu.SMEM)
PARAMS = pltpu.CompilerParams(vmem_limit_bytes=48 * 2**20)
COPIES = [
    pltpu.VMEM(((GROUPS + 1) * R, HD), jnp.bfloat16),
    pltpu.VMEM(((GROUPS + 1) * R, HD), jnp.bfloat16),
    pltpu.VMEM((KEYS, 2 * HD), jnp.bfloat16),
] + [pltpu.VMEM((KB, R), jnp.float32)] * 4


def stats(which, meta, lim, qds, kvs, *before):
    n = len(qds)
    return pl.pallas_call(
        functools.partial(stats_kernel, which, n),
        out_shape=jax.ShapeDtypeStruct((2, 24, 128), jnp.float32),
        in_specs=[SM] + [VM] * (1 + n + 8 + len(before)),
        out_specs=VM,
        scratch_shapes=COPIES + [pltpu.VMEM((3 * n + 1, 8, R), jnp.float32)] * 3,
        compiler_params=PARAMS,
        cost_estimate=pl.CostEstimate(flops=n * 1_000_000, bytes_accessed=100_000, transcendentals=0),
        name="stats_near" if which == NEAR else "stats_far",
    )(meta, lim, *qds, *kvs, *before)


def grads(meta, lim, sts, arrays):
    dq = [jax.ShapeDtypeStruct((2 * SPAN, WIDE), t) for t in (jnp.float32,) + (jnp.bfloat16,) * 3]
    dkv = [jax.ShapeDtypeStruct((4, 2 * SPAN, 2 * HD), jnp.bfloat16)] * 4
    dkv += [jax.ShapeDtypeStruct((4, 4, 2 * SPAN, 2 * HD), jnp.bfloat16)]
    return pl.pallas_call(
        grads_kernel,
        out_shape=dq + dkv,
        in_specs=[SM] + [VM] * 17,
        out_specs=[VM] * 9,
        scratch_shapes=COPIES
        + [
            pltpu.VMEM((KEYS, 2 * HD), jnp.float32),
            pltpu.VMEM(((GROUPS + 1) * R, HD), jnp.float32),
        ]
        + [pltpu.VMEM((KB, R), jnp.bfloat16)] * 4
        + [pltpu.VMEM((16, R), jnp.float32)] * 2,
        compiler_params=PARAMS,
        name="grads",
    )(meta, lim, *sts, *arrays)


def permute(a, move):
    pairs = []
    for i in range(128):
        y, zl, core, zh, x = (int(c) for c in np.unravel_index(i, SIZES))
        y, z, core, x = (c % n for c, n in zip(move(y, 2 * zh + zl, core, x), (4, 4, 2, 4)))
        pairs.append((i, int(np.ravel_multi_index((y, z % 2, core, z // 2, x), SIZES))))
    return lax.ppermute(a, AXES, pairs)


def x_shift(a, step):
    return permute(a, lambda y, z, core, x: (y, z, core, x + step))


def first_shift(a, step):
    return permute(a, lambda y, z, core, x: (y, z + step, core, x) if core else (y + step, z, core, x))


def second_shift(a, step):
    return permute(a, lambda y, z, core, x: (y + step, z, core, x) if core else (y, z + step, core, x))


def core_swap(a):
    return permute(a, lambda y, z, core, x: (y, z, 1 - core, x))


def plan(span_slot):
    i32 = jnp.int32
    y, zl, core, zh, x = (lax.axis_index(a) for a in AXES)
    z = 2 * zh + zl
    i = jnp.arange(72, dtype=i32)
    is_key = i < 64
    low, high = (i // 2) % 4, (i // 8) % 4
    low, high = low ^ (low >> 1), high ^ (high >> 1)
    at_core = jnp.where(is_key & (i >= 32), 1 - core, core)
    at_y = jnp.where(is_key, (y - jnp.where(at_core == 0, low, high)) % 4, y)
    at_z = jnp.where(is_key, (z - jnp.where(at_core == 0, high, low)) % 4, z)
    at_x = jnp.where(is_key, x, (x - low) % 4)
    slot = ((((at_y * 2 + at_z % 2) * 2 + at_core) * 2 + at_z // 2) * 4 + at_x) * 2 + i % 2
    spans = jnp.sum(jnp.where(slot[:, None] == jnp.arange(256)[None, :], span_slot[None, :], 0), axis=1)
    arrived, queries = spans[:64], spans[64:]

    def rank(a, among):
        return jnp.sum((among[None, :] < a[:, None]).astype(i32), axis=1)

    place = rank(queries, queries)
    eight = jnp.arange(8, dtype=i32)
    hit = (place[None, :] == eight[:, None]).astype(i32)
    spans = jnp.sum(hit * queries[None, :], axis=1)
    below = rank(spans, arrived)
    own = jnp.any(arrived[None, :] == spans[:, None], axis=1).astype(i32)
    far = jnp.sum(hit[:, 6:], axis=1)
    before = jnp.sum(jnp.tril(jnp.ones((8, 8), i32), -1) * far[None, :], axis=1)
    order = jnp.stack([eight, jnp.where(far == 0, eight - before, 9), jnp.where(far == 1, before, 9)])
    taken = (order[:, None, :] == eight[None, :, None]).astype(i32)
    canon = jnp.sum(taken * eight, axis=2)
    units = jnp.sum(order[:, None, :] * hit.T[None], axis=2)
    token = jnp.tile(jnp.arange(SPAN, dtype=i32), 2)
    seen = below[:, None] * SPAN + own[:, None] * (token[None, :] + 1)
    seen = jnp.sum(taken[:, :, :, None] * seen[None, None], axis=2)
    a, b = seen[:, 0::2], seen[:, 1::2]
    lim = jnp.stack([a, a, a, b, b, b], axis=2).reshape(3, GROUPS, R)
    lim = jnp.concatenate([lim, jnp.zeros((3, 4, R), i32)], axis=1)
    most = (jnp.sum(taken * (below + own), axis=2) * SPAN + KB - 1) // KB
    least = jnp.sum(taken * below, axis=2) * SPAN // KB
    most = jnp.stack([most[:, 0::2], most[:, 1::2], most[:, 1::2]], axis=2).reshape(3, GROUPS)
    least = jnp.stack([least[:, 0::2], least[:, 0::2], least[:, 1::2]], axis=2).reshape(3, GROUPS)
    each = jnp.concatenate([least, most - least], axis=1)
    first = jnp.concatenate([jnp.zeros_like(least), least], axis=1)
    end = jnp.sum(jnp.tril(jnp.ones((2 * GROUPS, 2 * GROUPS), i32)) * each[:, None, :], axis=2)
    t = jnp.arange(LIST, dtype=i32)
    begin = end - each
    inside = ((t[None, :, None] >= begin[:, None, :]) & (t[None, :, None] < end[:, None, :])).astype(i32)
    number = jnp.tile(jnp.arange(GROUPS, dtype=i32), 2)
    group = jnp.sum(inside * number, axis=2)
    block = jnp.sum(inside * (t[None, :, None] - (begin - first)[:, None, :]), axis=2)
    which = jnp.arange(3, dtype=i32)[:, None]
    group = jnp.where(t[None] < end[:, -1:], group, jnp.where(which == ALL, 12, jnp.where(which == NEAR, 9, 3)))
    lists = jnp.concatenate([units, canon, end[:, GROUPS - 1 : GROUPS], end[:, -1:], group, block], axis=1)
    return jnp.concatenate([rank(arrived, arrived), lists.reshape(-1)]).astype(i32), lim


def local(queries, keys, values, grad_out, span_slot):
    kv = jnp.concatenate([keys, values], axis=1)[None]
    kv = jnp.concatenate([kv] + [first_shift(kv, r) for r in STEPS[1:]], axis=0)
    kvs = [kv] + [second_shift(kv, r) for r in STEPS[1:]]
    qd = jnp.concatenate([queries, grad_out], axis=1)
    near = [qd, x_shift(qd, 1), x_shift(qd, 3)]
    near[1], near[2], later = lax.optimization_barrier((near[1], near[2], qd))
    far = x_shift(later, 2)
    kvs[0], kvs[1], span_slot = lax.optimization_barrier((kvs[0], kvs[1], span_slot))
    meta, lim = plan(span_slot)
    kvs = kvs + [core_swap(a) for a in kvs]
    arrays = near + [far] + kvs

    part = stats(NEAR, meta, lim, near, kvs)
    part = stats(FAR, meta, lim, [far], kvs, part)
    sts = [part] + [x_shift(part, r) for r in STEPS[1:]]
    results = grads(meta, lim, sts, arrays)
    dqs, dkv, dkv_other = results[:4], results[4:8], results[8]

    def total(*parts):
        out = parts[0].astype(jnp.float32)
        for part in parts[1:]:
            out = out + part.astype(jnp.float32)
        return out

    other = core_swap(dkv_other)
    pairs = [total(a, other[i]).astype(jnp.bfloat16) for i, a in enumerate(dkv)]
    some = total(pairs[0], *[second_shift(a, -r) for r, a in zip(STEPS[1:], pairs[1:])])
    dq = total(dqs[0], *[x_shift(a, -r) for r, a in zip(STEPS[1:], dqs[1:])])
    sent = [first_shift(some[i].astype(jnp.bfloat16), -r) for i, r in ((1, 1), (2, 3), (3, 2))]
    summed = total(some[0], *sent)
    return (
        dq.astype(jnp.bfloat16),
        summed[:, :HD].astype(jnp.bfloat16),
        summed[:, HD:].astype(jnp.bfloat16),
    )


def solution(mesh):
    fine = Mesh(mesh.devices.reshape(4, 2, 2, 2, 4), AXES)
    rows = P(AXES, None)
    return jax.shard_map(
        local,
        mesh=fine,
        in_specs=(rows, rows, rows, rows, P()),
        out_specs=(rows, rows, rows),
        check_vma=False,
    )
```
